32 devices in a mesh: clips: 2 (over y), tiles: 16 (over z, x, core).
Axes of the slice: x: 2, y: 2, z: 4, core: 2. Of those that a mesh axis runs over, the one named last changes fastest.
Arguments:
- frames: bfloat16 [4, 64, 256, 128], P(None, None, ('clips', 'tiles')), parts along dimension 2, may hold values from -6 to 6
- motion_forward: int32 [3, 512], P(None, ('clips', 'tiles')), parts along dimension 1, may hold values from 0 to 255, as said below
- motion_backward: int32 [3, 512], P(None, ('clips', 'tiles')), parts along dimension 1, may hold values from 0 to 255, as said below
- join_weight: bfloat16 [2, 64, 128], replicated, may hold values from -0.5 to 0.5
- conv_weight: bfloat16 [2, 4, 9, 64, 64], replicated, may hold values from -0.125 to 0.125
Outputs:
- forward_features: bfloat16 [4, 64, 256, 128], P(None, None, ('clips', 'tiles')), parts along dimension 2
- backward_features: bfloat16 [4, 64, 256, 128], P(None, None, ('clips', 'tiles')), parts along dimension 2
The draws below stay inside these ranges and needn't reach their ends.
There are 2 independent parts, one for each index of `clips`. The reference program is written for one: setup_inputs(seed, part) draws one part's arguments, and reference() takes and returns one part's arrays. A program takes and returns all parts, laid end to end along the dimension named above; an argument that names none is the same for every part. Nothing has to cross between parts.
Inputs may be any that keep to these rules, and one draw needn't show every extreme that they name: `motion_forward`: entries are block numbers of the frame; block number k lies in rows held by device k // 16. A block of device d takes a block of a device at most 2 away from d, at most two block columns to either side of its own column. Of the 16 blocks of one device, either none or exactly 4 take blocks of any one other device; in every frame some device takes 4 blocks from each device up to 2 away on both sides. `motion_backward`: entries are block numbers of the frame; block number k lies in rows held by device k // 16. A block of device d takes a block of a device at most 2 away from d, at most two block columns to either side of its own column. Of the 16 blocks of one device, either none or exactly 4 take blocks of any one other device; in every frame some device takes 4 blocks from each device up to 2 away on both sides.
All inputs are finite; a program needn't handle non-finite values.
Results may differ from the reference program's by a relative error of at most 0.018.
Values may be sent and summed in bfloat16 or wider, within the bound.
No kernel may reach another device: no remote copies, remote signals or barrier semaphores. Data moves between devices by JAX's collectives and lax.ppermute only.
A program may use at most 64 MiB of HBM per device.

```python
import jax
import jax.numpy as jnp
from jax import lax

C = 64
ROWS_DEV = 8
COLS = 128
FRAMES = 4
CONVS = 4
BS = 8
REACH = 2
HEIGHT = 128
N_TILES = 16


def motion_lists(key, salt):
    block_count = ROWS_DEV // BS * (COLS // BS)
    capacity = block_count // (2 * REACH)
    block_rows = ROWS_DEV // BS
    block_cols = COLS // BS
    band_width = N_TILES // 8
    offset_table = jnp.array([offset for offset in range(-REACH, REACH + 1) if offset != 0], jnp.int32)
    frame_keys = jax.random.split(jax.random.fold_in(key, salt), FRAMES - 1)

    def one_frame(frame_key):
        center = jax.random.randint(jax.random.fold_in(frame_key, 1), (), 0, N_TILES)

        def one_device(device):
            device_key = jax.random.fold_in(frame_key, device + 7)
            fast_strip = jnp.abs(device - center) <= band_width
            slot_offset = jnp.repeat(offset_table, capacity)
            allowed = fast_strip | (jnp.abs(slot_offset) == 1)
            source_strip = device + slot_offset
            usable = allowed & (source_strip >= 0) & (source_strip < N_TILES)
            slot_offset = jnp.where(usable, slot_offset, 0)
            mixing = jax.random.permutation(jax.random.fold_in(device_key, 2), block_count)
            dest_offset = slot_offset[mixing]
            positions = jnp.arange(block_count).astype(jnp.int32)
            dest_col = positions % block_cols
            source_row = jax.random.randint(jax.random.fold_in(device_key, 3), (block_count,), 0, block_rows)
            drift = jax.random.randint(jax.random.fold_in(device_key, 4), (block_count,), -2, 3)
            source_col = jnp.clip(dest_col + drift, 0, block_cols - 1)
            return ((device + dest_offset) * block_count + source_row * block_cols + source_col).astype(jnp.int32)
        return jax.vmap(one_device)(jnp.arange(N_TILES).astype(jnp.int32)).reshape(-1)
    return jax.vmap(one_frame)(frame_keys)


def draw_motion_forward(key, part):
    return motion_lists(key, 11)


def draw_motion_backward(key, part):
    return motion_lists(key, 23)


def levels(rng, extent, cuts, smallest, high):
    def one(dim, shards_of):
        draws = jax.random.uniform(jax.random.fold_in(jax.random.fold_in(rng, 6), dim), (shards_of,), jnp.float32, smallest / len(cuts), high / len(cuts))
        return jnp.repeat(jnp.exp(draws), extent[dim] // shards_of).reshape((-1,) + (1,) * (len(extent) - dim - 1))

    factor_of = one(*cuts[0])
    for cut in cuts[1:]:
        factor_of = factor_of * one(*cut)
    return factor_of


def normal_values(stream_key, extent, width, limit, pieces=(), dtype=jnp.bfloat16):
    drawn = jax.random.normal(stream_key, extent, jnp.float32) * width
    if len(pieces) > 0:
        drawn = levels(stream_key, extent, pieces, -0.22, 0.18) * drawn
    return jnp.clip(drawn, min=-limit, max=limit).astype(dtype)


def setup_inputs(seed: int = 0, part: int = 0) -> dict:
    key_list = jax.random.split(jax.random.key(seed), 6)
    part_splits = jax.random.split(jax.random.fold_in(key_list[5], part), 6)
    frames = normal_values(part_splits[0], (FRAMES, C, HEIGHT, COLS), 1.0, 6.0, ((2, 16),))
    motion_forward = draw_motion_forward(jax.random.fold_in(jax.random.fold_in(key_list[5], part), 71), part)
    motion_backward = draw_motion_backward(jax.random.fold_in(jax.random.fold_in(key_list[5], part), 71), part)
    join_weight = normal_values(key_list[3], (2, C, 2 * C), (2 * C) ** -0.5, 0.5)
    conv_weight = normal_values(key_list[4], (2, CONVS, 9, C, C), (36 * C) ** -0.5, 0.125)
    return {"frames": frames, "motion_forward": motion_forward, "motion_backward": motion_backward, "join_weight": join_weight, "conv_weight": conv_weight}


def frame_blocks(field):
    channels, height, breadth = field.shape
    block_grid = field.reshape(channels, height // BS, BS, breadth // BS, BS)
    return block_grid.transpose(1, 3, 0, 2, 4).reshape(-1, channels * BS * BS)


def blocks_frame(blocks, channels, height, breadth):
    block_grid = blocks.reshape(height // BS, breadth // BS, channels, BS, BS)
    return block_grid.transpose(2, 0, 3, 1, 4).reshape(channels, height, breadth)


def refine(aligned, inputs, join_matrix, conv_layers):
    channels, height, breadth = inputs.shape
    mixed = jnp.einsum("oc,chw->ohw", join_matrix[:, :channels].astype(jnp.float32), aligned.astype(jnp.float32))
    mixed = mixed + jnp.einsum("oc,chw->ohw", join_matrix[:, channels:].astype(jnp.float32), inputs.astype(jnp.float32))
    carried = lax.optimization_barrier(mixed.astype(jnp.bfloat16))
    for layer_index in range(conv_layers.shape[0]):
        widened = carried.astype(jnp.float32)
        active = jnp.where(widened >= 0, widened, 0.1 * widened).astype(jnp.bfloat16)
        active = lax.optimization_barrier(active)
        padded = jnp.pad(active, ((0, 0), (1, 1), (1, 1))).astype(jnp.float32)
        summed = jnp.zeros(widened.shape, jnp.float32)
        for tap_index in range(9):
            row_shift = tap_index // 3
            column_shift = tap_index % 3
            window = padded[:, row_shift:row_shift + height, column_shift:column_shift + breadth]
            kernel = conv_layers[layer_index, tap_index].astype(jnp.float32)
            summed = summed + jnp.einsum("oi,ihw->ohw", kernel, window)
        carried = lax.optimization_barrier((widened + summed).astype(jnp.bfloat16))
    return carried


def reference(frames, motion_forward, motion_backward, join_weight, conv_weight):
    frame_total, channels, height, breadth = frames.shape
    forward = []
    carried = None
    for frame_time in range(frame_total):
        if frame_time == 0:
            aligned = jnp.zeros(frames.shape[1:], jnp.bfloat16)
        else:
            moved = jnp.take(frame_blocks(carried), motion_forward[frame_time - 1].astype(jnp.int32), axis=0)
            aligned = blocks_frame(moved, channels, height, breadth)
        carried = refine(aligned, frames[frame_time], join_weight[0], conv_weight[0])
        forward.append(carried)
    backward = []
    carried = None
    for frame_time in range(frame_total - 1, -1, -1):
        if frame_time == frame_total - 1:
            aligned = jnp.zeros(frames.shape[1:], jnp.bfloat16)
        else:
            moved = jnp.take(frame_blocks(carried), motion_backward[frame_time].astype(jnp.int32), axis=0)
            aligned = blocks_frame(moved, channels, height, breadth)
        carried = refine(aligned, frames[frame_time], join_weight[1], conv_weight[1])
        backward.append(carried)
    return jnp.stack(forward), jnp.stack(backward[::-1])
```

```python
import functools

import jax
import jax.numpy as jnp
from jax import lax
from jax.experimental import pallas as pl
from jax.experimental.pallas import tpu as pltpu
from jax.sharding import PartitionSpec as P

BS = 8
REACH = 2
QUAD = 4
HALO = 4
BF = jnp.bfloat16
F32 = jnp.float32


def leaky(value):
    widened = value.astype(F32)
    return jnp.maximum(widened, 0.1 * widened).astype(BF)


def rows_first(src, src_start, dst, dst_start, tmp, ch):
    tmp[...] = src[pl.ds(src_start, BS * ch), :].astype(F32)
    for r in range(BS):
        row = tmp[pl.ds(r, ch, stride=BS), :]
        dst[pl.ds(dst_start + r * ch, ch), :] = row.astype(BF)


def channels_first(src, src_start, dst, tmp, ch):
    for r in range(BS):
        tmp[pl.ds(r, ch, stride=BS), :] = src[pl.ds(src_start + r * ch, ch), :].astype(F32)
    dst[...] = tmp[...].astype(BF)


def gather_first_kernel(ch, scal, r0, r1, r2, r3, xq, msg_e, msg_o, tmp):
    strip = BS * ch
    place = scal[0]
    for k, piece in enumerate((r0, r1, r2, r3)):
        start = pl.multiple_of((place ^ k) * strip, strip)
        rows_first(piece, 0, xq, start, tmp, ch)
    edge_messages(ch, scal, xq, msg_e, msg_o)


def edge_messages(ch, scal, xq, msg_e, msg_o):
    half = HALO * ch
    low = (QUAD * BS - HALO) * ch
    start_e = pl.multiple_of(low - scal[1] * low, half)
    start_o = pl.multiple_of(scal[1] * low, half)
    msg_e[...] = xq[pl.ds(start_e, half), :]
    msg_o[...] = xq[pl.ds(start_o, half), :]


def gather_rest_kernel(ch, steps, scal, r0, r1, r2, r3, xr, codes, msg_e, msg_o, tmp):
    strip = BS * ch
    half = HALO * ch
    place = scal[0]
    crow = codes.shape[0] // QUAD
    for k, piece in enumerate((r0, r1, r2, r3)):
        pos = place ^ k
        for s in range(steps):
            src = pl.multiple_of((s + scal[4] * (steps - 1 - 2 * s)) * strip, strip)
            rows_first(piece, src, xr.at[s], pl.multiple_of(pos * strip, strip), tmp, ch)
        codes[pl.ds(pl.multiple_of(pos * crow, crow), crow), :] = piece[pl.ds(steps * strip, crow), :]
    low = (QUAD * BS - HALO) * ch
    start_e = pl.multiple_of(low - scal[1] * low, half)
    start_o = pl.multiple_of(scal[1] * low, half)
    code_e = pl.multiple_of((1 - scal[1]) * ((QUAD - 1) * crow), crow)
    code_o = pl.multiple_of(scal[1] * ((QUAD - 1) * crow), crow)
    for s in range(steps):
        msg_e[pl.ds(s * half, half), :] = xr[s, pl.ds(start_e, half), :]
        msg_o[pl.ds(s * half, half), :] = xr[s, pl.ds(start_o, half), :]
    msg_e[pl.ds(steps * half, crow), :] = codes[pl.ds(code_e, crow), :]
    msg_o[pl.ds(steps * half, crow), :] = codes[pl.ds(code_o, crow), :]


def choose(code, offset, base, stride):
    return jnp.where(code - base == offset * stride, 1.0, 0.0).astype(BF)


def step_kernel(ch, step, steps, last, *refs):
    strip = BS * ch
    half = HALO * ch
    rows = QUAD * BS
    if step == 0:
        scal, xq, halo_e, halo_o, join, conv = refs[:6]
        refs = refs[6:]
    else:
        scal, feat, feat_e, feat_o, xq, halo_e, halo_o, codes, join, conv = refs[:10]
        refs = refs[10:]
    if last:
        (own, part), refs = refs[:2], refs[2:]
        fout = refs[-1]
        refs = refs[:-1]
    else:
        (fout, msg_e, msg_o, own, part), refs = refs[:5], refs[5:]
    tmp, act_a, act_b, held, halo = refs[:5]
    width = xq.shape[-1]
    par = scal[1]
    frame = step - 1
    halo[pl.ds(pl.multiple_of((1 - par) * half, half), half), :] = halo_e[pl.ds(max(frame, 0) * half, half), :]
    halo[pl.ds(pl.multiple_of(par * half, half), half), :] = halo_o[pl.ds(max(frame, 0) * half, half), :]
    groups = (rows + 2 * HALO) // 4
    if step > 0:
        fext, aligned, sel = refs[5:8]
        reach_rows = feat_e.shape[0]
        far = reach_rows + rows * ch
        fext[pl.ds(pl.multiple_of((1 - par) * far, half), reach_rows), :] = feat_e[...]
        fext[pl.ds(pl.multiple_of(par * far, half), reach_rows), :] = feat_o[...]
        fext[pl.ds(reach_rows, rows * ch), :] = feat[...]
        stride = 2 * (width // BS)
        k_id = lax.broadcasted_iota(jnp.int32, (width, width), 0)
        l_id = lax.broadcasted_iota(jnp.int32, (width, width), 1)
        base = (k_id // BS - l_id // BS + REACH * stride + width // BS - 1).astype(F32)
        base = jnp.where(k_id % BS == l_id % BS, base, -1.0e4)
        crow = codes.shape[0] // QUAD
        dsteps = steps - 1
        pick = scal[4] * dsteps + frame

        def code_of(ref, start):
            return ref[pl.ds(start, crow), :].astype(F32)

        row_id = lax.broadcasted_iota(jnp.int32, (crow, width), 0)

        def code_row(ref, start):
            block = code_of(ref, start)
            return jnp.sum(jnp.where(row_id == pick, block, 0.0), axis=0, keepdims=True)

        top_e = code_row(halo_e, dsteps * half)
        top_o = code_row(halo_o, dsteps * half)
        is_odd = par == 1
        code_above = jnp.where(is_odd, top_e, top_o)
        code_below = jnp.where(is_odd, top_o, top_e)
        code = [code_row(codes, d * crow) for d in range(QUAD)]

        def fext_rows(first_row, count):
            return fext[pl.ds((first_row + reach_rows // ch) * ch, count * ch), :]

        for edge, dest, sub, at in ((code_above, -1, BS - HALO, 0), (code_below, QUAD, 0, rows + HALO)):
            for n, ds in enumerate(range(-REACH, REACH + 1)):
                sel[pl.ds(n * width, width), pl.ds(0, width)] = choose(edge, ds, base, stride)
            left = jnp.concatenate(
                [fext_rows((dest + ds) * BS + sub, HALO) for ds in range(-REACH, REACH + 1)], axis=1
            )
            got = jnp.dot(
                left, sel[pl.ds(0, (2 * REACH + 1) * width), pl.ds(0, width)], preferred_element_type=F32
            )
            aligned[pl.ds(at * ch, half), :] = got.astype(BF)
        for dest in range(0, QUAD, 2):
            for n, ds in enumerate(range(-REACH, REACH + 2)):
                for m in range(2):
                    here = (
                        choose(code[dest + m], ds - m, base, stride)
                        if abs(ds - m) <= REACH
                        else jnp.zeros((width, width), BF)
                    )
                    sel[pl.ds(n * width, width), pl.ds(m * width, width)] = here
            left = jnp.concatenate(
                [fext_rows((dest + ds) * BS, BS) for ds in range(-REACH, REACH + 2)], axis=1
            )
            got = jnp.dot(left, sel[...], preferred_element_type=F32).astype(BF)
            for m in range(2):
                aligned[pl.ds(((dest + m) * BS + HALO) * ch, strip), :] = got[:, m * width : (m + 1) * width]

    off = 8
    top_ok = scal[2] == 1
    bottom_ok = scal[3] == 1

    def keep(value, row):
        if row < 0:
            return jnp.where(top_ok, value, jnp.zeros_like(value))
        if row >= rows:
            return jnp.where(bottom_ok, value, jnp.zeros_like(value))
        return value

    zero = jnp.zeros((ch, width), BF)
    for buf in (act_a, act_b):
        for row in (-HALO - 1, rows + HALO):
            buf[pl.ds((row + off) * ch, ch), :] = zero

    join_mat = join[...]
    for g in range(groups):
        first = g * 4 - HALO
        if first < 0:
            inp = halo[pl.ds(0, half), :]
        elif first >= rows:
            inp = halo[pl.ds(half, half), :]
        else:
            inp = xq[pl.ds(first * ch, 4 * ch), :]
        if step == 0:
            right = jnp.concatenate([inp[: 2 * ch], inp[2 * ch :]], axis=1)
        else:
            al = aligned[pl.ds(g * 4 * ch, 4 * ch), :]
            sides = []
            for h in range(2):
                a, b = 2 * h * ch, (2 * h + 1) * ch
                sides.append(
                    jnp.concatenate([al[a : a + ch], inp[a : a + ch], al[b : b + ch], inp[b : b + ch]], axis=0)
                )
            right = jnp.concatenate(sides, axis=1)
        mixed = jnp.dot(join_mat, right, preferred_element_type=F32).astype(BF)
        for h in range(2):
            for s in range(2):
                row = first + 2 * h + s
                value = mixed[s * ch : (s + 1) * ch, h * width : (h + 1) * width]
                held[pl.ds((row + off) * ch, ch), :] = value
                act_a[pl.ds((row + off) * ch, ch), :] = keep(leaky(value), row)

    lane = lax.broadcasted_iota(jnp.int32, (ch, width), 1)
    not_first = lane > 0
    not_last = lane < width - 1
    layers = conv.shape[0]
    source, target = act_a, act_b
    for layer in range(layers):
        need = layers - 1 - layer
        reach = -(-need // 2) * 2
        start, stop = -reach, rows + reach
        count = stop - start
        if count % 4:
            start, stop = start - 1, stop + 1
        if (stop - start) % 4:
            start, stop = -HALO, rows + HALO
        weight = conv[layer]

        def group(first, edge, layer=layer, source=source, target=target, weight=weight):
            def at(row):
                value = (row + off) * ch
                return value if isinstance(value, int) else pl.multiple_of(value, ch)

            lo = source[pl.ds(at(first - 1), 4 * ch), :]
            hi = source[pl.ds(at(first + 1), 4 * ch), :]
            out = jnp.dot(weight, jnp.concatenate([lo, hi], axis=1), preferred_element_type=F32)
            for h in range(2):
                for s in range(2):
                    row = first + 2 * h + s
                    m = s * 3 * ch
                    cols = slice(h * width, (h + 1) * width)
                    left = out[m : m + ch, cols]
                    mid = out[m + ch : m + 2 * ch, cols]
                    right = out[m + 2 * ch : m + 3 * ch, cols]
                    total = held[pl.ds(at(row), ch), :].astype(F32) + mid
                    total += jnp.where(not_first, pltpu.roll(left, 1, 1), 0.0)
                    total += jnp.where(not_last, pltpu.roll(right, width - 1, 1), 0.0)
                    value = total.astype(BF)
                    if layer < layers - 1:
                        held[pl.ds(at(row), ch), :] = value
                        act = leaky(value)
                        target[pl.ds(at(row), ch), :] = keep(act, row) if edge else act
                    else:
                        fout[pl.ds(pl.multiple_of(row * ch, ch), ch), :] = value

        for g in range((stop - start) // 4):
            first = start + 4 * g
            group(first, first < 0 or first + 4 > rows)
        source, target = target, source

    if not last:
        send = msg_e.shape[0]
        low = rows * ch - send
        msg_e[...] = fout[pl.ds(pl.multiple_of(low - par * low, half), send), :]
        msg_o[...] = fout[pl.ds(pl.multiple_of(par * low, half), send), :]
    channels_first(fout, pl.multiple_of(scal[0] * strip, strip), own, tmp, ch)
    channels_first(fout, pl.multiple_of((scal[0] ^ 1) * strip, strip), part, tmp, ch)


def call(kernel, outs, scratch, name, flops=0):
    vmem = pl.BlockSpec(memory_space=pltpu.VMEM)

    def run(scal, *args):
        moved = sum(a.size * a.dtype.itemsize for a in args)
        return pl.pallas_call(
            kernel,
            out_shape=[jax.ShapeDtypeStruct(o, BF) for o in outs],
            in_specs=[pl.BlockSpec(memory_space=pltpu.SMEM)] + [vmem] * len(args),
            out_specs=[vmem] * len(outs),
            scratch_shapes=scratch,
            compiler_params=pltpu.CompilerParams(vmem_limit_bytes=40 << 20),
            cost_estimate=pl.CostEstimate(flops=flops, bytes_accessed=moved, transcendentals=0),
            name=name,
        )(scal, *args)

    return run


def pairings(count):
    groups = count // QUAD
    out = []
    for parity in range(2):
        pairs = []
        for i in range(count):
            g = i // QUAD
            other = g + 1 if g % 2 == parity else g - 1
            pairs.append((i, i % QUAD + other * QUAD if 0 <= other < groups else i ^ 2))
        out.append(pairs)
    return out


def on_device(frames, motion_forward, motion_backward, join_weight, conv_weight):
    steps, ch, strip_rows, width = frames.shape
    strip = strip_rows * ch
    count = lax.axis_size("tiles")
    me = lax.axis_index("tiles")
    place = me % QUAD
    group = me // QUAD
    core = me % 2
    scal = jnp.stack(
        [place, group % 2, (group > 0).astype(jnp.int32), (group < count // QUAD - 1).astype(jnp.int32), core]
    ).astype(jnp.int32)
    even, odd = pairings(count)

    def near(k):
        return [(i, i ^ k) for i in range(count)]

    def send(value, pairs):
        return lax.ppermute(value, "tiles", pairs)

    blocks = motion_forward.shape[1]
    motion = jnp.stack([motion_forward, motion_backward[::-1]])
    across = motion // blocks - me + REACH
    along = motion % blocks - jnp.arange(blocks) + blocks - 1
    code = jnp.repeat(across * (2 * blocks) + along, BS, axis=2).astype(BF)
    crow = 16
    code = jnp.pad(code.reshape(-1, width), ((0, crow - 2 * (steps - 1)), (0, 0)))

    flat = frames.reshape(steps, strip, width)
    first_mine = lax.dynamic_index_in_dim(flat, core * (steps - 1), 0, keepdims=False)
    first_other = lax.dynamic_index_in_dim(flat, (1 - core) * (steps - 1), 0, keepdims=False)
    firsts = [first_mine] + [send(first_mine if k == 2 else first_other, near(k)) for k in (1, 2, 3)]

    half = HALO * ch
    tmp = pltpu.VMEM((strip, width), F32)
    xq, edge_e, edge_o = call(
        functools.partial(gather_first_kernel, ch),
        [(QUAD * strip, width), (half, width), (half, width)],
        [tmp],
        "gather_first",
    )(scal, *firsts)
    halo_e, halo_o = send(edge_e, even), send(edge_o, odd)

    def rest_of(start):
        body = lax.dynamic_slice_in_dim(flat, start, steps - 1, 0).reshape(-1, width)
        return jnp.concatenate([body, code], axis=0)

    rest_mine = rest_of(1 - core)
    rest_other = rest_of(core)
    rests = [rest_mine] + [send(rest_mine if k == 2 else rest_other, near(k)) for k in (1, 2, 3)]

    join = lax.dynamic_index_in_dim(join_weight, core, 0, keepdims=False)
    pad = jnp.zeros_like(join)
    join_both = jnp.block([[join, pad], [pad, join]])
    enter = join[:, ch:]
    join_first = jnp.block([[enter, jnp.zeros_like(enter)], [jnp.zeros_like(enter), enter]])
    conv = lax.dynamic_index_in_dim(conv_weight, core, 0, keepdims=False)
    layers = conv.shape[0]
    conv = conv.reshape(layers, 3, 3, ch, ch).transpose(0, 2, 3, 1, 4).reshape(layers, 3 * ch, 3 * ch)
    conv = jnp.concatenate(
        [jnp.pad(conv, ((0, 0), (0, 0), (0, ch))), jnp.pad(conv, ((0, 0), (0, 0), (ch, 0)))], axis=1
    )

    rows = QUAD * BS
    reach_rows = (HALO + REACH * BS) * ch
    buf = pltpu.VMEM(((rows + 16) * ch, width), BF)
    scratch = [tmp, buf, buf, buf, pltpu.VMEM((2 * half, width), BF)]
    align_scratch = [
        pltpu.VMEM((rows * ch + 2 * reach_rows, width), BF),
        pltpu.VMEM(((rows + 2 * HALO) * ch, width), BF),
        pltpu.VMEM(((2 * REACH + 2) * width, 2 * width), BF),
    ]
    piece = (strip, width)
    outs = [(rows * ch, width), (reach_rows, width), (reach_rows, width), piece, piece]
    flops = 2 * (rows + 2 * HALO) * width * ch * ch * 9 * layers

    feat, msg_e, msg_o, own, part = call(
        functools.partial(step_kernel, ch, 0, steps, False), outs, scratch, "refine_first", flops
    )(scal, xq, halo_e, halo_o, join_first, conv)
    owns = [own]
    parts = [send(part, near(1))]

    xr, codes, edge_e, edge_o = call(
        functools.partial(gather_rest_kernel, ch, steps - 1),
        [
            (steps - 1, QUAD * strip, width),
            (QUAD * crow, width),
            ((steps - 1) * half + crow, width),
            ((steps - 1) * half + crow, width),
        ],
        [tmp],
        "gather_rest",
    )(scal, *rests)
    halo_e, halo_o = send(edge_e, even), send(edge_o, odd)

    for step in range(1, steps):
        last = step == steps - 1
        feat_e, feat_o = send(msg_e, even), send(msg_o, odd)
        results = call(
            functools.partial(step_kernel, ch, step, steps, last),
            outs[3:] if last else outs,
            scratch + align_scratch + ([pltpu.VMEM(outs[0], BF)] if last else []),
            "refine",
            flops,
        )(scal, feat, feat_e, feat_o, xr[step - 1], halo_e, halo_o, codes, join_both, conv)
        if not last:
            feat, msg_e, msg_o = results[:3]
        own, part = results[-2:]
        owns.append(own)
        parts.append(send(part, near(1)))

    owns = jnp.stack(owns)
    parts = jnp.stack(parts)
    forward = jnp.where(core == 0, owns, parts)
    backward = jnp.where(core == 0, parts, owns)[::-1]
    return forward.reshape(frames.shape), backward.reshape(frames.shape)


def solution(mesh):
    return jax.shard_map(
        on_device,
        mesh=mesh,
        in_specs=(
            P(None, None, ("clips", "tiles"), None),
            P(None, ("clips", "tiles")),
            P(None, ("clips", "tiles")),
            P(),
            P(),
        ),
        out_specs=(
            P(None, None, ("clips", "tiles"), None),
            P(None, None, ("clips", "tiles"), None),
        ),
        check_vma=False,
    )
```

```python
import functools

import jax
import jax.numpy as jnp
from jax import lax
from jax.experimental import pallas as pl
from jax.experimental.pallas import tpu as pltpu
from jax.sharding import PartitionSpec as P

BS = 8
REACH = 2
QUAD = 4
HALO = 4
CAPACITY = 4
BF = jnp.bfloat16
F32 = jnp.float32


class Place:
    def __init__(self):
        me = lax.axis_index("tiles")
        self.me = me
        self.strip = me % QUAD
        self.core = me % 2
        self.side = self.strip // 2
        self.group = me // QUAD
        self.odd = self.group % 2
        self.top = self.group == 0
        self.bottom = self.group == lax.axis_size("tiles") // QUAD - 1


def leaky(value):
    widened = value.astype(F32)
    return jnp.maximum(widened, 0.1 * widened).astype(BF)


def rows_first(src, src_start, dst, dst_start, tmp, ch):
    tmp[...] = src[pl.ds(src_start, BS * ch), :].astype(F32)
    for r in range(BS):
        row = tmp[pl.ds(r, ch, stride=BS), :]
        dst[pl.ds(dst_start + r * ch, ch), :] = row.astype(BF)


def channels_first(src, src_start, dst, tmp, ch):
    for r in range(BS):
        tmp[pl.ds(r, ch, stride=BS), :] = src[pl.ds(src_start + r * ch, ch), :].astype(F32)
    dst[...] = tmp[...].astype(BF)


def pack_first_kernel(ch, crow, frames, motion_f, motion_b, mine, other, following, motion_buf, tmp, sems):
    place = Place()
    steps, strip = frames.shape[:2]
    half = HALO * ch
    core = place.core
    outs = (mine, other)
    lists = [
        pltpu.make_async_copy(motion, motion_buf.at[n], sems.at[4 + n]) for n, motion in enumerate((motion_f, motion_b))
    ]
    copies = []
    for n in range(2):
        back = 1 - core if n else core
        copies.append(frame_copy(frames, 0, back, outs[n].at[pl.ds(0, strip)], sems.at[n]))
        copies.append(frame_copy(frames, 1, back, following.at[n], sems.at[2 + n]))
    for copy in lists + copies:
        copy.start()
    for copy in lists:
        copy.wait()
    blocks = motion_f.shape[1]
    width = mine.shape[1]
    column = lax.broadcasted_iota(jnp.int32, motion_f.shape, 1)
    spread = jnp.where(
        lax.broadcasted_iota(jnp.int32, (blocks, width), 1) // BS
        == lax.broadcasted_iota(jnp.int32, (blocks, width), 0),
        1.0,
        0.0,
    ).astype(BF)
    wides = []
    for n in range(2):
        taken = motion_buf[n]
        across = taken // blocks
        code = (across - place.me + REACH) * (2 * blocks) + (taken - across * blocks - column + blocks - 1)
        wide = jnp.dot(code.astype(BF), spread, preferred_element_type=F32).astype(BF)
        frames_order = range(steps - 1) if n == 0 else range(steps - 2, -1, -1)
        wides += [wide[frame : frame + 1] for frame in frames_order]
    wides.append(jnp.zeros((crow - len(wides), width), BF))
    code = jnp.concatenate(wides, axis=0)
    for out in outs:
        out[pl.ds(strip, crow), :] = code
    for copy in copies:
        copy.wait()
    for n, out in enumerate(outs):
        tmp[...] = following[n].astype(F32)
        for r in range(HALO):
            row = tmp[pl.ds(place.side * (BS - HALO) + r, ch, stride=BS), :]
            out[pl.ds(strip + crow + r * ch, ch), :] = row.astype(BF)


def pair_first_kernel(ch, crow, mine, swapped, out):
    place = Place()
    strip = BS * ch
    half = HALO * ch
    for n, piece in enumerate((mine, swapped)):
        at = place.core ^ n
        out[pl.ds(pl.multiple_of(at * strip, strip), strip), :] = piece[pl.ds(0, strip), :]
        out[pl.ds(pl.multiple_of(2 * strip + at * crow, crow), crow), :] = piece[pl.ds(strip, crow), :]

        @pl.when(at == place.side)
        def _(piece=piece):
            out[pl.ds(2 * (strip + crow), half), :] = piece[pl.ds(strip + crow, half), :]


def frame_copy(frames, step, back, out, sem):
    steps = frames.shape[0]
    return pltpu.make_async_copy(frames.at[step + back * (steps - 1 - 2 * step)], out, sem)


def pack_rest_kernel(frames, after, other, sems):
    steps = frames.shape[0]
    strip = frames.shape[1]
    core = Place().core
    copies = [
        frame_copy(frames, step, 1 - core, other.at[pl.ds((step - 1) * strip, strip)], sems.at[step - 1])
        for step in range(1, steps)
    ]
    for copy in copies:
        copy.start()
    for copy in copies:
        copy.wait()


def pair_copies(frames, swapped, core, first, count, out, sems):
    strip = frames.shape[1]
    copies = []
    for n in range(count):
        step = first + n
        own = out.at[pl.ds(pl.multiple_of((2 * n + core) * strip, strip), strip)]
        his = out.at[pl.ds(pl.multiple_of((2 * n + 1 - core) * strip, strip), strip)]
        copies.append(frame_copy(frames, step, core, own, sems.at[2 * n]))
        copies.append(
            pltpu.make_async_copy(swapped.at[pl.ds((step - 1) * strip, strip)], his, sems.at[2 * n + 1])
        )
    return copies


def pair_kernel(first, count, frames, swapped, out, sems):
    copies = pair_copies(frames, swapped, Place().core, first, count, out, sems)
    for copy in copies:
        copy.start()
    for copy in copies:
        copy.wait()


def gather_first_kernel(ch, crow, pair, received, rest, xq, codes, msg_e, msg_o, rest_out, tmp, edges):
    place = Place()
    strip = BS * ch
    half = HALO * ch
    for n, piece in enumerate((pair, received)):
        side = place.side ^ n
        for m in range(2):
            at = side * 2 + m
            rows_first(piece, m * strip, xq, pl.multiple_of(at * strip, strip), tmp, ch)
            code_at = pl.multiple_of(at * crow, crow)
            codes[pl.ds(code_at, crow), :] = piece[pl.ds(2 * strip + m * crow, crow), :]
        edges[side] = piece[pl.ds(2 * (strip + crow), half), :]
    low = (QUAD * BS - HALO) * ch
    msg_e[pl.ds(0, half), :] = xq[pl.ds(pl.multiple_of(low - place.odd * low, half), half), :]
    msg_o[pl.ds(0, half), :] = xq[pl.ds(pl.multiple_of(place.odd * low, half), half), :]
    msg_e[pl.ds(half, half), :] = edges[1 - place.odd]
    msg_o[pl.ds(half, half), :] = edges[place.odd]
    msg_e[pl.ds(2 * half, codes.shape[0]), :] = codes[...]
    msg_o[pl.ds(2 * half, codes.shape[0]), :] = codes[...]


def gather_kernel(ch, at, pair, received, after, xq, tmp):
    strip = BS * ch
    side = Place().side
    for n, piece in enumerate((pair, received)):
        for m in range(2):
            start = ((side + n) % 2 * 2 + m) * strip
            rows_first(piece, (2 * at + m) * strip, xq, pl.multiple_of(start, strip), tmp, ch)


class Codes:
    def __init__(self, rows):
        width = rows[0].shape[1]
        self.rows = rows
        self.blocks = width // BS
        k_id = lax.broadcasted_iota(jnp.int32, (width, width), 0)
        l_id = lax.broadcasted_iota(jnp.int32, (width, width), 1)
        base = (k_id // BS - l_id // BS + self.blocks - 1).astype(F32)
        self.base = jnp.where(k_id % BS == l_id % BS, base, -1.0e4)
        self.slot = k_id.astype(F32)
        self.before = jnp.where((k_id % BS == 0) & (k_id // BS < l_id // BS), 1.0, 0.0).astype(BF)
        self.lane = (lax.broadcasted_iota(jnp.int32, (1, width), 1) % BS).astype(F32)
        self.zero = jnp.zeros((width, width), BF)
        self.ranks = {}

    def plain(self, dest, source):
        ds = source - dest
        if abs(ds) > REACH:
            return self.zero
        shift = float((ds + REACH) * 2 * self.blocks)
        return jnp.where(self.rows[dest + 2] - shift == self.base, 1.0, 0.0).astype(BF)

    def rank_all(self, wanted):
        rows = []
        for dest, source in wanted:
            low = float((source - dest + REACH) * 2 * self.blocks)
            code = self.rows[dest + 2]
            rows.append(jnp.where((code >= low) & (code < low + 2 * self.blocks), 1.0, 0.0))
        count = len(rows)
        rows += [rows[0]] * (-count % 16)
        stacked = jnp.concatenate(rows, axis=0)
        before = jnp.dot(stacked.astype(BF), self.before, preferred_element_type=F32)
        for n, key in enumerate(wanted):
            self.ranks[key] = jnp.where(
                stacked[n : n + 1] > 0, before[n : n + 1] * BS + self.lane, -1.0e4
            )

    def packed(self, dest, source, region):
        at = self.ranks[dest, source] + float(region * CAPACITY * BS)
        return jnp.where(self.slot == at, 1.0, 0.0).astype(BF)

    def pack(self, dest, source, region):
        return lax.dot_general(
            self.plain(dest, source),
            self.packed(dest, source, region),
            (((1,), (1,)), ((), ())),
            preferred_element_type=F32,
        )


FROM_ABOVE = (((0, -2), (-1, -2), (-1, -3)), ((1, -1), (0, -1), (0, -2)))
FROM_BELOW = (
    ((QUAD - 1, QUAD + 1), (QUAD, QUAD + 1), (QUAD, QUAD + 2)),
    ((QUAD - 2, QUAD), (QUAD - 1, QUAD), (QUAD - 1, QUAD + 1)),
)
TO_BELOW = tuple(tuple((d + QUAD, s + QUAD) for d, s in tile) for tile in FROM_ABOVE)
TO_ABOVE = tuple(tuple((d - QUAD, s - QUAD) for d, s in tile) for tile in FROM_BELOW)


def step_codes(ch, place, step, steps, codes, halo_e, halo_o):
    crow = codes.shape[0] // QUAD
    width = codes.shape[1]
    pick = place.core * (steps - 1) + step - 1
    row_id = lax.broadcasted_iota(jnp.int32, (crow, width), 0)

    def row(ref, start):
        block = ref[pl.ds(start, crow), :].astype(F32)
        return jnp.sum(jnp.where(row_id == pick, block, 0.0), axis=0, keepdims=True)

    odd = place.odd == 1
    half = HALO * ch

    def beside(strip, above):
        e = row(halo_e, 2 * half + strip * crow)
        o = row(halo_o, 2 * half + strip * crow)
        return jnp.where(odd, e, o) if above else jnp.where(odd, o, e)

    rows = [beside(QUAD - 2, True), beside(QUAD - 1, True)]
    rows += [row(codes, strip * crow) for strip in range(QUAD)]
    rows += [beside(0, False), beside(1, False)]
    return Codes(rows)


PARTS = (((-1,), True), ((0, 1), False), ((0, 1), True), ((2, 3), False), ((2, 3), True), ((QUAD,), False))


def tiles_of(dests, bottom):
    tiles = [source for source in range(QUAD) if any(abs(source - d) <= REACH for d in dests)]
    for side, near, tables in ((0, -1, FROM_ABOVE), (1, QUAD, FROM_BELOW)):
        if any(abs(near - d) <= REACH for d in dests):
            whole = bottom if side == 0 else not bottom
            tiles += [(side, 0), (side, 1)] if whole else [(side, 2)]
    return tiles


def receive_choice(code, dests, bottom, out):
    width = out.shape[0] // len(tiles_of(dests, bottom))
    for n, tile in enumerate(tiles_of(dests, bottom)):
        for m, dest in enumerate(dests):
            if isinstance(tile, int):
                value = code.plain(dest, tile)
            elif tile[1] == 0:
                value = code.plain(dest, -1 if tile[0] == 0 else QUAD)
            else:
                table = (FROM_ABOVE, FROM_BELOW)[tile[0]][tile[1] - 1]
                value = sum(
                    (code.packed(d, source, at) for at, (d, source) in enumerate(table) if d == dest), code.zero
                )
            out[pl.ds(n * width, width), pl.ds(m * width, width)] = value


SENT = tuple((side, tile) for side in range(2) for tile in range(2))


def sent_regions(side, tile):
    regions = (TO_ABOVE, TO_BELOW)[side][tile]
    return regions, sorted({source for _, source in regions})


def send_choice(code, side, tile, out):
    regions, sources = sent_regions(side, tile)
    width = out.shape[1]
    for n, source in enumerate(sources):
        total = sum(code.pack(d, source, at) for at, (d, origin) in enumerate(regions) if origin == source)
        out[pl.ds(n * width, width), :] = total.astype(BF)


def all_pairs(*tables):
    return [pair for table in tables for tile in table for pair in tile]


def choices_kernel(ch, step, steps, codes, code_e, code_o, after, *outs):
    place = Place()
    code = step_codes(ch, place, step, steps, codes, code_e, code_o)
    code.rank_all(all_pairs(FROM_ABOVE, FROM_BELOW))
    for part, out in zip(PARTS, outs):
        receive_choice(code, *part, out)
    if step + 1 < steps:
        code = step_codes(ch, place, step + 1, steps, codes, code_e, code_o)
        code.rank_all(all_pairs(TO_ABOVE, TO_BELOW))
        for item, out in zip(SENT, outs[len(PARTS) :]):
            send_choice(code, *item, out)


def choice_shapes(width):
    parts = [(len(tiles_of(*part)) * width, len(part[0]) * width) for part in PARTS]
    return parts, [(len(sent_regions(*item)[1]) * width, width) for item in SENT]


def align(ch, feat, recv, aligned, offset, part, choice, only=None):
    dests, bottom = part
    half = HALO * ch
    shift = half if bottom else 0
    width = feat.shape[1]
    left = [
        feat[pl.ds(tile * BS * ch + shift, half), :]
        if isinstance(tile, int)
        else recv[tile[0], pl.ds(tile[1] * half, half), :]
        for tile in tiles_of(dests, bottom)
    ]
    if only is None:
        right = choice[...]
    else:
        right = choice[:, only * width : (only + 1) * width]
        dests = (dests[only],)
    got = jnp.dot(jnp.concatenate(left, axis=1), right, preferred_element_type=F32).astype(BF)
    for n, d in enumerate(dests):
        aligned[pl.ds((d * BS + offset) * ch + shift, half), :] = got[:, n * width : (n + 1) * width]


def pack_messages(ch, fout, par, sent, choices, msg_e, msg_o):
    half = HALO * ch
    strip = BS * ch
    for side, near in ((0, 0), (1, QUAD - 1)):
        shift = half if side == 1 else 0
        sent[side, pl.ds(0, half), :] = fout[pl.ds(near * strip + shift, half), :]
    for (side, tile), choice in zip(SENT, choices):
        shift = half if (side == 1) == (tile == 0) else 0
        left = [fout[pl.ds(source * strip + shift, half), :] for source in sent_regions(side, tile)[1]]
        got = jnp.dot(jnp.concatenate(left, axis=1), choice[...], preferred_element_type=F32)
        sent[side, pl.ds((tile + 1) * half, half), :] = got.astype(BF)
    msg_e[...] = sent[1 - par]
    msg_o[...] = sent[par]


def step_kernel(ch, step, steps, *refs):
    strip = BS * ch
    half = HALO * ch
    last = step == steps - 1
    refs = list(refs)

    def take(count):
        taken = refs[:count]
        del refs[:count]
        return taken

    xq, halo_e, halo_o, join, conv = take(5)
    if step > 0:
        feat, feat_e, feat_o = take(3)
        choices = take(len(PARTS) + (0 if last else len(SENT)))
        before, back, out_a, out_b = take(4)
        if not last:
            (x_next,) = take(1)
    else:
        (codes,) = take(1)
    if not last:
        fout, msg_e, msg_o = take(3)
    own_out, part_out = take(2)
    if step > 0:
        out_f, out_g = take(2)
    tmp, act_a, act_b, held, xext = take(5)
    if step > 0:
        sems, aligned, recv = take(3)
    else:
        choices = take(len(SENT))
    if last:
        (fout,) = take(1)
    else:
        (sent,) = take(1)
    width = xq.shape[-1]
    place = Place()
    par = place.odd
    core = place.core
    quad_rows = QUAD * BS
    rows = 2 * BS if last else quad_rows
    right_side = place.side
    own = place.core if last else place.strip

    copies = []
    if step > 0:
        copies = result_copies(strip, step - 1, steps, before, back, out_f, out_g, sems)
        for n, copy in copies:
            pl.when(core == n)(copy.start)
    halo_at = (0, half)[step] if step < 2 else 3 * half

    above = pl.ds(pl.multiple_of((1 - par) * (quad_rows + HALO) * ch, half), half)
    below = pl.ds(pl.multiple_of(par * (quad_rows + HALO) * ch, half), half)
    xext[above, :] = halo_e[pl.ds(halo_at, half), :]
    xext[below, :] = halo_o[pl.ds(halo_at, half), :]
    xext[pl.ds(half, quad_rows * ch), :] = xq[...]
    if step > 0:
        recv[1 - par] = feat_e[pl.ds(0, 3 * half), :]
        recv[par] = feat_o[pl.ds(0, 3 * half), :]
        if last:

            @pl.when(right_side == 0)
            def _():
                for n in range(3):
                    align(ch, feat, recv, aligned, HALO, PARTS[n], choices[n])
                align(ch, feat, recv, aligned, HALO, PARTS[3], choices[3], 0)

            @pl.when(right_side == 1)
            def _():
                offset = HALO - 2 * BS
                align(ch, feat, recv, aligned, offset, PARTS[2], choices[2], 1)
                for n in range(3, 6):
                    align(ch, feat, recv, aligned, offset, PARTS[n], choices[n])

        else:
            for n, rows_part in enumerate(PARTS):
                align(ch, feat, recv, aligned, HALO, rows_part, choices[n])
            sent[0, pl.ds(3 * half, half), :] = x_next[pl.ds(0, half), :]
            sent[1, pl.ds(3 * half, half), :] = x_next[pl.ds((quad_rows - HALO) * ch, half), :]
    else:
        code = step_codes(ch, place, 1, steps, codes, halo_e, halo_o)
        code.rank_all(all_pairs(TO_ABOVE, TO_BELOW))
        for item, out in zip(SENT, choices):
            send_choice(code, *item, out)

    off = 8
    top_ok = jnp.logical_not(place.top)
    bottom_ok = jnp.logical_not(place.bottom)
    if last:
        top_ok = top_ok | (right_side == 1)
        bottom_ok = bottom_ok | (right_side == 0)
    start_row = right_side * (2 * BS) if last else 0
    lane = lax.broadcasted_iota(jnp.int32, (ch, width), 1)
    not_first = lane > 0
    not_last = lane < width - 1
    zero = jnp.zeros((ch, width), BF)

    def put(buf, row, act):
        if row < 0:
            act = jnp.where(top_ok, act, zero)
        if row >= rows:
            act = jnp.where(bottom_ok, act, zero)
        here = pl.ds((row + off) * ch, ch)
        buf[0, here, :] = jnp.where(not_first, pltpu.roll(act, 1, 1), zero)
        buf[1, here, :] = act
        buf[2, here, :] = jnp.where(not_last, pltpu.roll(act, width - 1, 1), zero)

    for buf in (act_a, act_b):
        for row in (-HALO - 1, rows + HALO):
            for n in range(3):
                buf[n, pl.ds((row + off) * ch, ch), :] = zero

    join_mat = join[...]
    for g in range((rows + 2 * HALO) // 4):
        first = g * 4 - HALO
        at = (start_row + g * 4) * ch
        inp = xext[pl.ds(pl.multiple_of(at, 4 * ch) if last else at, 4 * ch), :]
        if step == 0:
            right = jnp.concatenate([inp[: 2 * ch], inp[2 * ch :]], axis=1)
        else:
            al = aligned[pl.ds(g * 4 * ch, 4 * ch), :]
            sides = []
            for h in range(2):
                a, b = 2 * h * ch, (2 * h + 1) * ch
                sides.append(
                    jnp.concatenate([al[a : a + ch], inp[a : a + ch], al[b : b + ch], inp[b : b + ch]], axis=0)
                )
            right = jnp.concatenate(sides, axis=1)
        mixed = jnp.dot(join_mat, right, preferred_element_type=F32).astype(BF)
        for h in range(2):
            for q in range(2):
                row = first + 2 * h + q
                value = mixed[q * ch : (q + 1) * ch, h * width : (h + 1) * width]
                held[pl.ds((row + off) * ch, ch), :] = value
                put(act_a, row, leaky(value))

    layers = conv.shape[0]
    source, target = act_a, act_b
    for layer in range(layers):
        need = layers - 1 - layer
        reach = -(-need // 2) * 2
        start, stop = -reach, rows + reach
        if (stop - start) % 4:
            start, stop = -HALO, rows + HALO
        weight = conv[layer]
        for first in range(start, stop, 4):
            sides = [
                jnp.concatenate([source[n, pl.ds((first + 2 * h - 1 + off) * ch, 4 * ch), :] for n in range(3)], axis=0)
                for h in range(2)
            ]
            out = jnp.dot(weight, jnp.concatenate(sides, axis=1), preferred_element_type=F32)
            for h in range(2):
                for q in range(2):
                    row = first + 2 * h + q
                    here = pl.ds((row + off) * ch, ch)
                    total = held[here, :].astype(F32) + out[q * ch : (q + 1) * ch, h * width : (h + 1) * width]
                    value = total.astype(BF)
                    if layer < layers - 1:
                        held[here, :] = value
                        put(target, row, leaky(value))
                    else:
                        fout[pl.ds(row * ch, ch), :] = value
        source, target = target, source

    if not last:
        pack_messages(ch, fout, par, sent, choices[-len(SENT) :], msg_e, msg_o)
    channels_first(fout, pl.multiple_of(own * strip, strip), own_out, tmp, ch)
    channels_first(fout, pl.multiple_of((own ^ 1) * strip, strip), part_out, tmp, ch)
    for n, copy in copies:
        pl.when(core == n)(copy.wait)


def result_copies(strip, step, steps, own, back, out_f, out_g, sems):
    copies = []
    for n in range(2):
        forth, other = (out_f, out_g) if n == 0 else (out_g, out_f)
        at = step if n == 0 else steps - 1 - step
        other_at = steps - 1 - at
        copies.append((n, pltpu.make_async_copy(own, forth.at[pl.ds(at * strip, strip)], sems.at[0])))
        copies.append((n, pltpu.make_async_copy(back, other.at[pl.ds(other_at * strip, strip)], sems.at[1])))
    return copies


def finish_kernel(strip, steps, own, back, out_a, out_b, out_f, out_g, sems):
    core = Place().core
    copies = result_copies(strip, steps - 1, steps, own, back, out_f, out_g, sems)
    for n, copy in copies:
        pl.when(core == n)(copy.start)
    for n, copy in copies:
        pl.when(core == n)(copy.wait)


def weights_kernel(conv, join, wide, join_both, join_first):
    core = Place().core
    layers, ch = conv.shape[1], conv.shape[3]
    zero = jnp.zeros((ch, ch), BF)
    for layer in range(layers):
        for dx in range(3):
            taps = [conv[core, layer, 3 * dy + dx] for dy in range(3)]
            for q in range(2):
                line = [zero] * q + taps + [zero] * (1 - q)
                wide[layer, pl.ds(q * ch, ch), pl.ds(dx * 4 * ch, 4 * ch)] = jnp.concatenate(line, axis=1)
    both = join[core]
    none = jnp.zeros_like(both)
    join_both[pl.ds(0, ch), :] = jnp.concatenate([both, none], axis=1)
    join_both[pl.ds(ch, ch), :] = jnp.concatenate([none, both], axis=1)
    enter = both[:, ch:]
    join_first[pl.ds(0, ch), :] = jnp.concatenate([enter, zero], axis=1)
    join_first[pl.ds(ch, ch), :] = jnp.concatenate([zero, enter], axis=1)


VMEM = pl.BlockSpec(memory_space=pltpu.VMEM)
ANY = pl.BlockSpec(memory_space=pl.ANY)
HBM = pl.BlockSpec(memory_space=pltpu.HBM)


def call(kernel, name, args, outs, scratch=(), flops=0, in_any=(), out_any=(), aliases=None, in_hbm=()):
    args = [pltpu.with_memory_space_constraint(a, pltpu.HBM) if n in in_hbm else a for n, a in enumerate(args)]
    return pl.pallas_call(
        kernel,
        out_shape=[jax.ShapeDtypeStruct(o, BF) for o in outs],
        in_specs=[HBM if n in in_hbm else ANY if n in in_any else VMEM for n in range(len(args))],
        out_specs=[ANY if n in out_any else VMEM for n in range(len(outs))],
        scratch_shapes=list(scratch),
        input_output_aliases=aliases or {},
        compiler_params=pltpu.CompilerParams(vmem_limit_bytes=32 << 20),
        cost_estimate=pl.CostEstimate(
            flops=flops, bytes_accessed=sum(a.size * a.dtype.itemsize for a in args), transcendentals=0
        ),
        name=name,
    )(*args)


def pairings(count):
    groups = count // QUAD
    out = []
    for parity in range(2):
        pairs = []
        for i in range(count):
            g = i // QUAD
            other = g + 1 if g % 2 == parity else g - 1
            pairs.append((i, i % QUAD + other * QUAD if 0 <= other < groups else i ^ 1))
        out.append(pairs)
    return out


def on_device(frames, motion_forward, motion_backward, join_weight, conv_weight):
    steps, ch, strip_rows, width = frames.shape
    strip = strip_rows * ch
    half = HALO * ch
    crow = 16
    count = lax.axis_size("tiles")
    even, odd = pairings(count)

    def near(k):
        return [(i, i ^ k) for i in range(count)]

    def send(value, pairs):
        return lax.ppermute(value, "tiles", pairs)

    tmp = pltpu.VMEM((strip, width), F32)
    piece = (strip, width)
    rows = QUAD * BS
    messages = [(3 * half, width)] + [(4 * half, width)] * (steps - 2)
    feature = (rows * ch, width)
    whole = (steps * strip, width)
    flat = frames.reshape(steps, strip, width)
    mine, other = call(
        functools.partial(pack_first_kernel, ch, crow),
        "pack_first",
        (flat, motion_forward, motion_backward),
        [(strip + crow + half, width)] * 2,
        [
            pltpu.VMEM((2, *piece), BF),
            pltpu.VMEM((2, *motion_forward.shape), jnp.int32),
            tmp,
            pltpu.SemaphoreType.DMA((6,)),
        ],
        in_hbm=(0, 1, 2),
    )
    (pair,) = call(
        functools.partial(pair_first_kernel, ch, crow),
        "pair_first",
        (mine, send(other, near(1))),
        [(2 * (strip + crow) + half, width)],
    )
    received = send(pair, near(2))
    (rest,) = call(
        pack_rest_kernel,
        "pack_rest",
        (flat, pair),
        [((steps - 1) * strip, width)],
        [pltpu.SemaphoreType.DMA((steps - 1,))],
        in_hbm=(0,),
        in_any=(1,),
        out_any=(0,),
    )
    swapped = send(rest, near(1))
    many = 2 * (steps - 1)
    (pair_rest,) = call(
        functools.partial(pair_kernel, 1, steps - 1),
        "pair_rest",
        (flat, swapped),
        [(many * strip, width)],
        [pltpu.SemaphoreType.DMA((many,))],
        in_hbm=(0,),
        in_any=(1,),
        out_any=(0,),
    )
    layers = conv_weight.shape[1]
    conv, join_both, join_first = call(
        weights_kernel,
        "weights",
        (conv_weight, join_weight),
        [(layers, 2 * ch, 12 * ch), (2 * ch, 4 * ch), (2 * ch, 2 * ch)],
    )
    xq, codes, edge_e, edge_o, pair_rest = call(
        functools.partial(gather_first_kernel, ch, crow),
        "gather_first",
        (pair, received, pair_rest),
        [feature, (QUAD * crow, width)] + [(2 * half + QUAD * crow, width)] * 2 + [pair_rest.shape],
        [tmp, pltpu.VMEM((2, half, width), BF)],
        in_any=(2,),
        out_any=(4,),
        aliases={2: 4},
    )
    halo_e, halo_o = code_e, code_o = send(edge_e, even), send(edge_o, odd)
    received_rest = send(pair_rest, near(2))

    wide_act = pltpu.VMEM((3, (rows + 16) * ch, width), BF)
    flops = 2 * (rows + 2 * HALO) * width * ch * ch * 9 * layers
    part_shapes, sent_shapes = choice_shapes(width)
    for step in range(steps):
        last = step == steps - 1
        args = [xq, halo_e, halo_o, join_both if step else join_first, conv]
        outs = [] if last else [feature, messages[step], messages[step]]
        outs += [piece, piece]
        scratch = [tmp, wide_act, wide_act, pltpu.VMEM(((rows + 16) * ch, width), BF)]
        scratch += [pltpu.VMEM(((rows + 2 * HALO) * ch, width), BF)]
        if step:
            args += [feat, feat_e, feat_o, *choices, own, back, *outputs]
            many = len(args)
            in_any = (many - 4, many - 3, many - 2, many - 1)
            aliases = {many - 2: len(outs), many - 1: len(outs) + 1}
            out_any = (len(outs), len(outs) + 1)
            outs += [whole, whole]
            if not last:
                args += [x_next]
            scratch += [pltpu.SemaphoreType.DMA((2,))]
            scratch += [pltpu.VMEM(((rows + 2 * HALO) * ch, width), BF), pltpu.VMEM((2, 3 * half, width), BF)]
        else:
            args += [codes]
            in_any = out_any = ()
            aliases = {}
            scratch += [pltpu.VMEM(shape, BF) for shape in sent_shapes]
        scratch += [pltpu.VMEM((2 * strip, width) if last else (2, *messages[step]), BF)]
        results = call(
            functools.partial(step_kernel, ch, step, steps),
            "refine",
            args,
            outs,
            scratch,
            flops,
            in_any,
            out_any,
            aliases,
        )
        if not last:
            feat, msg_e, msg_o, *results = results
            feat_e, feat_o = send(msg_e, even), send(msg_o, odd)
            if step:
                halo_e, halo_o = feat_e, feat_o
            choices = call(
                functools.partial(choices_kernel, ch, step + 1, steps),
                "choices",
                (codes, code_e, code_o, msg_e),
                part_shapes + (sent_shapes if step + 2 < steps else []),
                in_any=(3,),
            )
        own, part, *results = results
        back = send(part, near(1))
        if step == 0:
            outputs = call(lambda after, a, b: None, "results", (part,), [whole, whole], in_any=(0,), out_any=(0, 1))

            def later(frame):
                return call(
                    functools.partial(gather_kernel, ch, frame - 1),
                    "gather",
                    (pair_rest, received_rest, msg_e),
                    [feature],
                    [tmp],
                    in_any=(2,),
                )[0]

            xq, x_next = later(1), later(2)
        else:
            outputs = results
            if not last:
                xq = x_next
                x_next = later(step + 2) if step + 2 < steps else None

    outputs = call(
        functools.partial(finish_kernel, strip, steps),
        "finish",
        [own, back, *outputs],
        [whole] * 2,
        [pltpu.SemaphoreType.DMA((2,))],
        in_any=(0, 1, 2, 3),
        out_any=(0, 1),
        aliases={2: 0, 3: 1},
    )
    return tuple(o.reshape(frames.shape) for o in outputs)


def solution(mesh):
    return jax.shard_map(
        on_device,
        mesh=mesh,
        in_specs=(
            P(None, None, ("clips", "tiles"), None),
            P(None, ("clips", "tiles")),
            P(None, ("clips", "tiles")),
            P(),
            P(),
        ),
        out_specs=(
            P(None, None, ("clips", "tiles"), None),
            P(None, None, ("clips", "tiles"), None),
        ),
        check_vma=False,
    )
```

```python
import functools

import jax
import jax.numpy as jnp
from jax import lax
from jax.experimental import pallas as pl
from jax.experimental.pallas import tpu as pltpu
from jax.sharding import PartitionSpec as P

BS = 8
REACH = 2
QUAD = 4
HALO = 4
CAPACITY = 4
BF = jnp.bfloat16
F32 = jnp.float32


class Place:
    def __init__(self):
        me = lax.axis_index("tiles")
        self.me = me
        self.strip = me % QUAD
        self.core = me % 2
        self.side = self.strip // 2
        self.group = me // QUAD
        self.odd = self.group % 2
        self.top = self.group == 0
        self.bottom = self.group == lax.axis_size("tiles") // QUAD - 1


def leaky(value):
    widened = value.astype(F32)
    return jnp.maximum(widened, 0.1 * widened).astype(BF)


def rows_first(src, src_start, dst, dst_start, tmp, ch):
    tmp[...] = src[pl.ds(src_start, BS * ch), :].astype(F32)
    for r in range(BS):
        row = tmp[pl.ds(r, ch, stride=BS), :]
        dst[pl.ds(dst_start + r * ch, ch), :] = row.astype(BF)


def channels_first(src, src_start, dst, tmp, ch):
    for r in range(BS):
        tmp[pl.ds(r, ch, stride=BS), :] = src[pl.ds(src_start + r * ch, ch), :].astype(F32)
    dst[...] = tmp[...].astype(BF)


def pack_first_kernel(ch, crow, frames, motion_f, motion_b, mine, other, rest, following, motion_buf, tmp, sems):
    place = Place()
    steps, strip = frames.shape[:2]
    half = HALO * ch
    core = place.core
    outs = (mine, other)
    lists = [
        pltpu.make_async_copy(motion, motion_buf.at[n], sems.at[4 + n]) for n, motion in enumerate((motion_f, motion_b))
    ]
    copies = []
    for n in range(2):
        back = 1 - core if n else core
        copies.append(frame_copy(frames, 0, back, outs[n].at[pl.ds(0, strip)], sems.at[n]))
        copies.append(frame_copy(frames, 1, back, following.at[n], sems.at[2 + n]))
    later = [
        frame_copy(frames, step, 1 - core, rest.at[pl.ds((step - 1) * strip, strip)], sems.at[5 + step])
        for step in range(1, steps)
    ]
    for copy in lists + copies + later:
        copy.start()
    for copy in lists:
        copy.wait()
    blocks = motion_f.shape[1]
    width = mine.shape[1]
    column = lax.broadcasted_iota(jnp.int32, motion_f.shape, 1)
    spread = jnp.where(
        lax.broadcasted_iota(jnp.int32, (blocks, width), 1) // BS
        == lax.broadcasted_iota(jnp.int32, (blocks, width), 0),
        1.0,
        0.0,
    ).astype(BF)
    wides = []
    for n in range(2):
        taken = motion_buf[n]
        across = taken // blocks
        code = (across - place.me + REACH) * (2 * blocks) + (taken - across * blocks - column + blocks - 1)
        wide = jnp.dot(code.astype(BF), spread, preferred_element_type=F32).astype(BF)
        frames_order = range(steps - 1) if n == 0 else range(steps - 2, -1, -1)
        wides += [wide[frame : frame + 1] for frame in frames_order]
    wides.append(jnp.zeros((crow - len(wides), width), BF))
    code = jnp.concatenate(wides, axis=0)
    for out in outs:
        out[pl.ds(strip, crow), :] = code
    for copy in copies:
        copy.wait()
    for n, out in enumerate(outs):
        tmp[...] = following[n].astype(F32)
        for r in range(HALO):
            row = tmp[pl.ds(place.side * (BS - HALO) + r, ch, stride=BS), :]
            out[pl.ds(strip + crow + r * ch, ch), :] = row.astype(BF)
    for copy in later:
        copy.wait()


def pair_first_kernel(ch, crow, mine, swapped, rest_in, out, rest_out):
    place = Place()
    strip = BS * ch
    half = HALO * ch
    for n, piece in enumerate((mine, swapped)):
        at = place.core ^ n
        out[pl.ds(pl.multiple_of(at * strip, strip), strip), :] = piece[pl.ds(0, strip), :]
        out[pl.ds(pl.multiple_of(2 * strip + at * crow, crow), crow), :] = piece[pl.ds(strip, crow), :]

        @pl.when(at == place.side)
        def _(piece=piece):
            out[pl.ds(2 * (strip + crow), half), :] = piece[pl.ds(strip + crow, half), :]


def frame_copy(frames, step, back, out, sem):
    steps = frames.shape[0]
    return pltpu.make_async_copy(frames.at[step + back * (steps - 1 - 2 * step)], out, sem)


def pair_copies(frames, swapped, core, first, count, out, sems):
    strip = frames.shape[1]
    copies = []
    for n in range(count):
        step = first + n
        own = out.at[pl.ds(pl.multiple_of((2 * n + core) * strip, strip), strip)]
        his = out.at[pl.ds(pl.multiple_of((2 * n + 1 - core) * strip, strip), strip)]
        copies.append(frame_copy(frames, step, core, own, sems.at[2 * n]))
        copies.append(
            pltpu.make_async_copy(swapped.at[pl.ds((step - 1) * strip, strip)], his, sems.at[2 * n + 1])
        )
    return copies


def pair_kernel(many, frames, swapped, near_out, far_out, sems):
    steps = frames.shape[0]
    core = Place().core
    copies = pair_copies(frames, swapped, core, 1, many, near_out, sems)
    copies += pair_copies(frames, swapped, core, 1 + many, steps - 1 - many, far_out, sems.at[pl.ds(2 * many, 2 * (steps - 1 - many))])
    for copy in copies:
        copy.start()
    for copy in copies:
        copy.wait()


def gather_first_kernel(ch, crow, pair, received, near_in, xq, codes, msg_e, msg_o, near_out, tmp, edges):
    place = Place()
    strip = BS * ch
    half = HALO * ch
    for n, piece in enumerate((pair, received)):
        side = place.side ^ n
        for m in range(2):
            at = side * 2 + m
            rows_first(piece, m * strip, xq, pl.multiple_of(at * strip, strip), tmp, ch)
            code_at = pl.multiple_of(at * crow, crow)
            codes[pl.ds(code_at, crow), :] = piece[pl.ds(2 * strip + m * crow, crow), :]
        edges[side] = piece[pl.ds(2 * (strip + crow), half), :]
    low = (QUAD * BS - HALO) * ch
    msg_e[pl.ds(0, half), :] = xq[pl.ds(pl.multiple_of(low - place.odd * low, half), half), :]
    msg_o[pl.ds(0, half), :] = xq[pl.ds(pl.multiple_of(place.odd * low, half), half), :]
    msg_e[pl.ds(half, half), :] = edges[1 - place.odd]
    msg_o[pl.ds(half, half), :] = edges[place.odd]
    msg_e[pl.ds(2 * half, codes.shape[0]), :] = codes[...]
    msg_o[pl.ds(2 * half, codes.shape[0]), :] = codes[...]


def gather_kernel(ch, at, pair, received, after, xq, tmp):
    strip = BS * ch
    side = Place().side
    for n, piece in enumerate((pair, received)):
        for m in range(2):
            start = ((side + n) % 2 * 2 + m) * strip
            rows_first(piece, (2 * at + m) * strip, xq, pl.multiple_of(start, strip), tmp, ch)


class Codes:
    def __init__(self, rows):
        width = rows[0].shape[1]
        self.rows = rows
        self.blocks = width // BS
        k_id = lax.broadcasted_iota(jnp.int32, (width, width), 0)
        l_id = lax.broadcasted_iota(jnp.int32, (width, width), 1)
        base = (k_id // BS - l_id // BS + self.blocks - 1).astype(F32)
        self.base = jnp.where(k_id % BS == l_id % BS, base, -1.0e4)
        self.slot = k_id.astype(F32)
        self.before = jnp.where((k_id % BS == 0) & (k_id // BS < l_id // BS), 1.0, 0.0).astype(BF)
        self.lane = (lax.broadcasted_iota(jnp.int32, (1, width), 1) % BS).astype(F32)
        self.zero = jnp.zeros((width, width), BF)
        self.ranks = {}

    def plain(self, dest, source):
        ds = source - dest
        if abs(ds) > REACH:
            return self.zero
        shift = float((ds + REACH) * 2 * self.blocks)
        return jnp.where(self.rows[dest + 2] - shift == self.base, 1.0, 0.0).astype(BF)

    def rank_all(self, wanted):
        rows = []
        for dest, source in wanted:
            low = float((source - dest + REACH) * 2 * self.blocks)
            code = self.rows[dest + 2]
            rows.append(jnp.where((code >= low) & (code < low + 2 * self.blocks), 1.0, 0.0))
        count = len(rows)
        rows += [rows[0]] * (-count % 16)
        stacked = jnp.concatenate(rows, axis=0)
        before = jnp.dot(stacked.astype(BF), self.before, preferred_element_type=F32)
        for n, key in enumerate(wanted):
            self.ranks[key] = jnp.where(
                stacked[n : n + 1] > 0, before[n : n + 1] * BS + self.lane, -1.0e4
            )

    def packed(self, dest, source, region):
        at = self.ranks[dest, source] + float(region * CAPACITY * BS)
        return jnp.where(self.slot == at, 1.0, 0.0).astype(BF)

    def pack(self, dest, source, region):
        return lax.dot_general(
            self.plain(dest, source),
            self.packed(dest, source, region),
            (((1,), (1,)), ((), ())),
            preferred_element_type=F32,
        )


FROM_ABOVE = (((0, -2), (-1, -2), (-1, -3)), ((1, -1), (0, -1), (0, -2)))
FROM_BELOW = (
    ((QUAD - 1, QUAD + 1), (QUAD, QUAD + 1), (QUAD, QUAD + 2)),
    ((QUAD - 2, QUAD), (QUAD - 1, QUAD), (QUAD - 1, QUAD + 1)),
)
TO_BELOW = tuple(tuple((d + QUAD, s + QUAD) for d, s in tile) for tile in FROM_ABOVE)
TO_ABOVE = tuple(tuple((d - QUAD, s - QUAD) for d, s in tile) for tile in FROM_BELOW)


def step_codes(ch, place, step, steps, codes, halo_e, halo_o):
    crow = codes.shape[0] // QUAD
    width = codes.shape[1]
    pick = place.core * (steps - 1) + step - 1
    row_id = lax.broadcasted_iota(jnp.int32, (crow, width), 0)

    def row(ref, start):
        block = ref[pl.ds(start, crow), :].astype(F32)
        return jnp.sum(jnp.where(row_id == pick, block, 0.0), axis=0, keepdims=True)

    odd = place.odd == 1
    half = HALO * ch

    def beside(strip, above):
        e = row(halo_e, 2 * half + strip * crow)
        o = row(halo_o, 2 * half + strip * crow)
        return jnp.where(odd, e, o) if above else jnp.where(odd, o, e)

    rows = [beside(QUAD - 2, True), beside(QUAD - 1, True)]
    rows += [row(codes, strip * crow) for strip in range(QUAD)]
    rows += [beside(0, False), beside(1, False)]
    return Codes(rows)


PARTS = (((-1,), True), ((0, 1), False), ((0, 1), True), ((2, 3), False), ((2, 3), True), ((QUAD,), False))


def tiles_of(dests, bottom):
    tiles = [source for source in range(QUAD) if any(abs(source - d) <= REACH for d in dests)]
    for side, near, tables in ((0, -1, FROM_ABOVE), (1, QUAD, FROM_BELOW)):
        if any(abs(near - d) <= REACH for d in dests):
            whole = bottom if side == 0 else not bottom
            tiles += [(side, 0), (side, 1)] if whole else [(side, 2)]
    return tiles


def receive_choice(code, dests, bottom, out):
    width = out.shape[0] // len(tiles_of(dests, bottom))
    for n, tile in enumerate(tiles_of(dests, bottom)):
        for m, dest in enumerate(dests):
            if isinstance(tile, int):
                value = code.plain(dest, tile)
            elif tile[1] == 0:
                value = code.plain(dest, -1 if tile[0] == 0 else QUAD)
            else:
                table = (FROM_ABOVE, FROM_BELOW)[tile[0]][tile[1] - 1]
                value = sum(
                    (code.packed(d, source, at) for at, (d, source) in enumerate(table) if d == dest), code.zero
                )
            out[pl.ds(n * width, width), pl.ds(m * width, width)] = value


SENT = tuple((side, tile) for side in range(2) for tile in range(2))


def sent_regions(side, tile):
    regions = (TO_ABOVE, TO_BELOW)[side][tile]
    return regions, sorted({source for _, source in regions})


def send_choice(code, side, tile, out):
    regions, sources = sent_regions(side, tile)
    width = out.shape[1]
    for n, source in enumerate(sources):
        total = sum(code.pack(d, source, at) for at, (d, origin) in enumerate(regions) if origin == source)
        out[pl.ds(n * width, width), :] = total.astype(BF)


def all_pairs(*tables):
    return [pair for table in tables for tile in table for pair in tile]


def choices_kernel(ch, step, steps, codes, code_e, code_o, after, *outs):
    place = Place()
    code = step_codes(ch, place, step, steps, codes, code_e, code_o)
    code.rank_all(all_pairs(FROM_ABOVE, FROM_BELOW))
    for part, out in zip(PARTS, outs):
        receive_choice(code, *part, out)
    if step + 1 < steps:
        code = step_codes(ch, place, step + 1, steps, codes, code_e, code_o)
        code.rank_all(all_pairs(TO_ABOVE, TO_BELOW))
        for item, out in zip(SENT, outs[len(PARTS) :]):
            send_choice(code, *item, out)


def choice_shapes(width):
    parts = [(len(tiles_of(*part)) * width, len(part[0]) * width) for part in PARTS]
    return parts, [(len(sent_regions(*item)[1]) * width, width) for item in SENT]


def align(ch, feat, recv, aligned, offset, part, choice, only=None):
    dests, bottom = part
    half = HALO * ch
    shift = half if bottom else 0
    width = feat.shape[1]
    left = [
        feat[pl.ds(tile * BS * ch + shift, half), :]
        if isinstance(tile, int)
        else recv[tile[0], pl.ds(tile[1] * half, half), :]
        for tile in tiles_of(dests, bottom)
    ]
    if only is None:
        right = choice[...]
    else:
        right = choice[:, only * width : (only + 1) * width]
        dests = (dests[only],)
    got = jnp.dot(jnp.concatenate(left, axis=1), right, preferred_element_type=F32).astype(BF)
    for n, d in enumerate(dests):
        aligned[pl.ds((d * BS + offset) * ch + shift, half), :] = got[:, n * width : (n + 1) * width]


def pack_messages(ch, fout, par, sent, choices, msg_e, msg_o):
    half = HALO * ch
    strip = BS * ch
    for side, near in ((0, 0), (1, QUAD - 1)):
        shift = half if side == 1 else 0
        sent[side, pl.ds(0, half), :] = fout[pl.ds(near * strip + shift, half), :]
    for (side, tile), choice in zip(SENT, choices):
        shift = half if (side == 1) == (tile == 0) else 0
        left = [fout[pl.ds(source * strip + shift, half), :] for source in sent_regions(side, tile)[1]]
        got = jnp.dot(jnp.concatenate(left, axis=1), choice[...], preferred_element_type=F32)
        sent[side, pl.ds((tile + 1) * half, half), :] = got.astype(BF)
    msg_e[...] = sent[1 - par]
    msg_o[...] = sent[par]


class Rows:
    def __init__(self, ch, width, top_ok, bottom_ok, count):
        lane = lax.broadcasted_iota(jnp.int32, (ch, width), 1)
        self.not_first = lane > 0
        self.not_last = lane < width - 1
        self.zero = jnp.zeros((ch, width), BF)
        self.top_ok = top_ok
        self.bottom_ok = bottom_ok
        self.count = count

    def active(self, value, row):
        act = leaky(value)
        if row < 0:
            act = jnp.where(self.top_ok, act, self.zero)
        if row >= self.count:
            act = jnp.where(self.bottom_ok, act, self.zero)
        return (
            jnp.where(self.not_first, pltpu.roll(act, 1, 1), self.zero),
            act,
            jnp.where(self.not_last, pltpu.roll(act, act.shape[1] - 1, 1), self.zero),
        )

    def put(self, buf, here, value, row):
        for n, act in enumerate(self.active(value, row)):
            buf[n, here, :] = act


OFF = 8


def here_of(row, ch, count=1):
    return pl.ds((row + OFF) * ch, count * ch)


def conv_layer(ch, weight, source, held, start, stop, emit):
    width = held.shape[1]
    for first in range(start, stop, 4):
        sides = [
            jnp.concatenate([source[n, here_of(first + 2 * h - 1, ch, 4), :] for n in range(3)], axis=0)
            for h in range(2)
        ]
        out = jnp.dot(weight, jnp.concatenate(sides, axis=1), preferred_element_type=F32)
        for h in range(2):
            for q in range(2):
                row = first + 2 * h + q
                total = held[here_of(row, ch), :].astype(F32)
                total += out[q * ch : (q + 1) * ch, h * width : (h + 1) * width]
                emit(row, total.astype(BF))


def join_first_rows(ch, join_mat, inp):
    width = inp.shape[1]
    mixed = jnp.dot(
        join_mat, jnp.concatenate([inp[: 2 * ch], inp[2 * ch :]], axis=1), preferred_element_type=F32
    ).astype(BF)
    return [mixed[q * ch : (q + 1) * ch, h * width : (h + 1) * width] for h in range(2) for q in range(2)]


def inner_kernel(ch, xq, join, conv, feat, saved, saved_held, act_a, act_b, held):
    rows = QUAD * BS
    layers = conv.shape[0]
    space = Rows(ch, xq.shape[1], True, True, rows)
    for buf in (act_a, act_b):
        for row in (-1, rows):
            for n in range(3):
                buf[n, here_of(row, ch), :] = space.zero
    join_mat = join[...]
    for first in range(0, rows, 4):
        for n, value in enumerate(join_first_rows(ch, join_mat, xq[pl.ds(first * ch, 4 * ch), :])):
            held[here_of(first + n, ch), :] = value
            space.put(act_a, here_of(first + n, ch), value, first + n)
    source, target = act_a, act_b
    for layer in range(layers):
        for side, row, both in ((0, layer, layer), (1, rows - 1 - layer, rows - 2 - layer)):
            for n in range(3):
                saved[layer, side, n] = source[n, here_of(both, ch, 2), :]
            saved_held[layer, side] = held[here_of(row, ch), :]
        edge = (layer + 1) // 2 * 2

        def emit(row, value, layer=layer, target=target):
            if layer < layers - 1:
                held[here_of(row, ch), :] = value
                space.put(target, here_of(row, ch), value, row)
            else:
                feat[pl.ds(row * ch, ch), :] = value

        conv_layer(ch, conv[layer], source, held, edge, rows - edge, emit)
        source, target = target, source


def outer_kernel(ch, steps, *refs):
    feat_in, saved, saved_held, halo_e, halo_o, join, conv, codes, far_in, *refs = refs
    fout, msg_e, msg_o, own_out, part_out, far_out, tmp, sent, *choices = refs
    half = HALO * ch
    strip = BS * ch
    rows = QUAD * BS
    place = Place()
    layers = conv.shape[0]
    width = feat_in.shape[1]
    space = Rows(ch, width, jnp.logical_not(place.top), jnp.logical_not(place.bottom), rows)
    code = step_codes(ch, place, 1, steps, codes, halo_e, halo_o)
    code.rank_all(all_pairs(TO_ABOVE, TO_BELOW))
    for item, out in zip(SENT, choices):
        send_choice(code, *item, out)
    fout[pl.ds(half, (rows - 2 * HALO) * ch), :] = feat_in[pl.ds(half, (rows - 2 * HALO) * ch), :]
    odd = place.odd == 1
    one, two = halo_e[pl.ds(0, half), :].astype(F32), halo_o[pl.ds(0, half), :].astype(F32)
    halos = [jnp.where(odd, one, two).astype(BF), jnp.where(odd, two, one).astype(BF)]
    join_mat = join[...]
    values = [join_first_rows(ch, join_mat, halo) for halo in halos]
    starts = [-HALO, rows]
    for layer in range(layers):
        weight = conv[layer]
        for side in range(2):
            acts = [space.active(value, starts[side] + n) for n, value in enumerate(values[side])]
            kept = [
                tuple(saved[layer, side, n, pl.ds(m * ch, ch), :] for n in range(3)) for m in range(2)
            ]
            beside = saved_held[layer, side]
            if side == 0:
                window, base = acts + kept, values[side][1:] + [beside]
                starts[side] += 1
            else:
                window, base = kept + acts, [beside] + values[side][:3]
                starts[side] -= 1
            halves = [
                jnp.concatenate([window[2 * h + m][n] for n in range(3) for m in range(4)], axis=0) for h in range(2)
            ]
            out = jnp.dot(weight, jnp.concatenate(halves, axis=1), preferred_element_type=F32)
            values[side] = [
                (
                    base[2 * h + q].astype(F32) + out[q * ch : (q + 1) * ch, h * width : (h + 1) * width]
                ).astype(BF)
                for h in range(2)
                for q in range(2)
            ]
    for side in range(2):
        for n, value in enumerate(values[side]):
            fout[pl.ds((starts[side] + n) * ch, ch), :] = value
    pack_messages(ch, fout, place.odd, sent, choices, msg_e, msg_o)
    channels_first(fout, pl.multiple_of(place.strip * strip, strip), own_out, tmp, ch)
    channels_first(fout, pl.multiple_of((place.strip ^ 1) * strip, strip), part_out, tmp, ch)


def step_kernel(ch, step, steps, *refs):
    strip = BS * ch
    half = HALO * ch
    last = step == steps - 1
    refs = list(refs)

    def take(count):
        taken = refs[:count]
        del refs[:count]
        return taken

    xq, halo_e, halo_o, join, conv = take(5)
    feat, feat_e, feat_o = take(3)
    choices = take(len(PARTS) + (0 if last else len(SENT)))
    before, back, out_a, out_b = take(4)
    if not last:
        x_next, fout, msg_e, msg_o = take(4)
    own_out, part_out, out_f, out_g = take(4)
    tmp, act_a, act_b, held, xext, sems, aligned, recv = take(8)
    if last:
        (fout,) = take(1)
    else:
        (sent,) = take(1)
    width = xq.shape[-1]
    place = Place()
    par = place.odd
    core = place.core
    quad_rows = QUAD * BS
    rows = 2 * BS if last else quad_rows
    right_side = place.side
    own = place.core if last else place.strip

    copies = result_copies(strip, step - 1, steps, before, back, out_f, out_g, sems)
    for n, copy in copies:
        pl.when(core == n)(copy.start)
    halo_at = half if step == 1 else 3 * half
    above = pl.ds(pl.multiple_of((1 - par) * (quad_rows + HALO) * ch, half), half)
    below = pl.ds(pl.multiple_of(par * (quad_rows + HALO) * ch, half), half)
    xext[above, :] = halo_e[pl.ds(halo_at, half), :]
    xext[below, :] = halo_o[pl.ds(halo_at, half), :]
    xext[pl.ds(half, quad_rows * ch), :] = xq[...]
    recv[1 - par] = feat_e[pl.ds(0, 3 * half), :]
    recv[par] = feat_o[pl.ds(0, 3 * half), :]
    if last:

        @pl.when(right_side == 0)
        def _():
            for n in range(3):
                align(ch, feat, recv, aligned, HALO, PARTS[n], choices[n])
            align(ch, feat, recv, aligned, HALO, PARTS[3], choices[3], 0)

        @pl.when(right_side == 1)
        def _():
            offset = HALO - 2 * BS
            align(ch, feat, recv, aligned, offset, PARTS[2], choices[2], 1)
            for n in range(3, 6):
                align(ch, feat, recv, aligned, offset, PARTS[n], choices[n])

    else:
        for n, rows_part in enumerate(PARTS):
            align(ch, feat, recv, aligned, HALO, rows_part, choices[n])
        sent[0, pl.ds(3 * half, half), :] = x_next[pl.ds(0, half), :]
        sent[1, pl.ds(3 * half, half), :] = x_next[pl.ds((quad_rows - HALO) * ch, half), :]

    top_ok = jnp.logical_not(place.top)
    bottom_ok = jnp.logical_not(place.bottom)
    if last:
        top_ok = top_ok | (right_side == 1)
        bottom_ok = bottom_ok | (right_side == 0)
    start_row = right_side * (2 * BS) if last else 0
    space = Rows(ch, width, top_ok, bottom_ok, rows)
    for buf in (act_a, act_b):
        for row in (-HALO - 1, rows + HALO):
            for n in range(3):
                buf[n, here_of(row, ch), :] = space.zero

    join_mat = join[...]
    for g in range((rows + 2 * HALO) // 4):
        first = g * 4 - HALO
        at = (start_row + g * 4) * ch
        inp = xext[pl.ds(pl.multiple_of(at, 4 * ch) if last else at, 4 * ch), :]
        al = aligned[pl.ds(g * 4 * ch, 4 * ch), :]
        sides = []
        for h in range(2):
            a, b = 2 * h * ch, (2 * h + 1) * ch
            sides.append(jnp.concatenate([al[a : a + ch], inp[a : a + ch], al[b : b + ch], inp[b : b + ch]], axis=0))
        mixed = jnp.dot(join_mat, jnp.concatenate(sides, axis=1), preferred_element_type=F32).astype(BF)
        for h in range(2):
            for q in range(2):
                row = first + 2 * h + q
                value = mixed[q * ch : (q + 1) * ch, h * width : (h + 1) * width]
                held[here_of(row, ch), :] = value
                space.put(act_a, here_of(row, ch), value, row)

    layers = conv.shape[0]
    source, target = act_a, act_b
    for layer in range(layers):
        need = layers - 1 - layer
        reach = -(-need // 2) * 2
        start, stop = -reach, rows + reach
        if (stop - start) % 4:
            start, stop = -HALO, rows + HALO

        def emit(row, value, layer=layer, target=target):
            if layer < layers - 1:
                held[here_of(row, ch), :] = value
                space.put(target, here_of(row, ch), value, row)
            else:
                fout[pl.ds(row * ch, ch), :] = value

        conv_layer(ch, conv[layer], source, held, start, stop, emit)
        source, target = target, source

    if not last:
        pack_messages(ch, fout, par, sent, choices[-len(SENT) :], msg_e, msg_o)
    channels_first(fout, pl.multiple_of(own * strip, strip), own_out, tmp, ch)
    channels_first(fout, pl.multiple_of((own ^ 1) * strip, strip), part_out, tmp, ch)
    for n, copy in copies:
        pl.when(core == n)(copy.wait)


def result_copies(strip, step, steps, own, back, out_f, out_g, sems):
    copies = []
    for n in range(2):
        forth, other = (out_f, out_g) if n == 0 else (out_g, out_f)
        at = step if n == 0 else steps - 1 - step
        other_at = steps - 1 - at
        copies.append((n, pltpu.make_async_copy(own, forth.at[pl.ds(at * strip, strip)], sems.at[0])))
        copies.append((n, pltpu.make_async_copy(back, other.at[pl.ds(other_at * strip, strip)], sems.at[1])))
    return copies


def finish_kernel(strip, steps, own, back, out_a, out_b, out_f, out_g, sems):
    core = Place().core
    copies = result_copies(strip, steps - 1, steps, own, back, out_f, out_g, sems)
    for n, copy in copies:
        pl.when(core == n)(copy.start)
    for n, copy in copies:
        pl.when(core == n)(copy.wait)


def weights_kernel(conv, join, wide, join_both, join_first):
    core = Place().core
    layers, ch = conv.shape[1], conv.shape[3]
    zero = jnp.zeros((ch, ch), BF)
    for layer in range(layers):
        for dx in range(3):
            taps = [conv[core, layer, 3 * dy + dx] for dy in range(3)]
            for q in range(2):
                line = [zero] * q + taps + [zero] * (1 - q)
                wide[layer, pl.ds(q * ch, ch), pl.ds(dx * 4 * ch, 4 * ch)] = jnp.concatenate(line, axis=1)
    both = join[core]
    none = jnp.zeros_like(both)
    join_both[pl.ds(0, ch), :] = jnp.concatenate([both, none], axis=1)
    join_both[pl.ds(ch, ch), :] = jnp.concatenate([none, both], axis=1)
    enter = both[:, ch:]
    join_first[pl.ds(0, ch), :] = jnp.concatenate([enter, zero], axis=1)
    join_first[pl.ds(ch, ch), :] = jnp.concatenate([zero, enter], axis=1)


VMEM = pl.BlockSpec(memory_space=pltpu.VMEM)
ANY = pl.BlockSpec(memory_space=pl.ANY)
HBM = pl.BlockSpec(memory_space=pltpu.HBM)


def call(kernel, name, args, outs, scratch=(), flops=0, in_any=(), out_any=(), aliases=None, in_hbm=(), free=False):
    args = [pltpu.with_memory_space_constraint(a, pltpu.HBM) if n in in_hbm else a for n, a in enumerate(args)]
    return pl.pallas_call(
        kernel,
        out_shape=[jax.ShapeDtypeStruct(o, BF) for o in outs],
        in_specs=[HBM if n in in_hbm else ANY if n in in_any else VMEM for n in range(len(args))],
        out_specs=[ANY if n in out_any else VMEM for n in range(len(outs))],
        scratch_shapes=list(scratch),
        input_output_aliases=aliases or {},
        compiler_params=pltpu.CompilerParams(vmem_limit_bytes=32 << 20),
        cost_estimate=pl.CostEstimate(
            flops=flops,
            bytes_accessed=0 if free else sum(a.size * a.dtype.itemsize for a in args),
            transcendentals=0,
        ),
        name=name,
    )(*args)


def pairings(count):
    groups = count // QUAD
    out = []
    for parity in range(2):
        pairs = []
        for i in range(count):
            g = i // QUAD
            other = g + 1 if g % 2 == parity else g - 1
            pairs.append((i, i % QUAD + other * QUAD if 0 <= other < groups else i ^ 1))
        out.append(pairs)
    return out


def on_device(frames, motion_forward, motion_backward, join_weight, conv_weight):
    steps, ch, strip_rows, width = frames.shape
    strip = strip_rows * ch
    half = HALO * ch
    crow = 16
    count = lax.axis_size("tiles")
    even, odd = pairings(count)

    def near(k):
        return [(i, i ^ k) for i in range(count)]

    def send(value, pairs):
        return lax.ppermute(value, "tiles", pairs)

    tmp = pltpu.VMEM((strip, width), F32)
    piece = (strip, width)
    rows = QUAD * BS
    messages = [(3 * half, width)] + [(4 * half, width)] * (steps - 2)
    feature = (rows * ch, width)
    whole = (steps * strip, width)
    flat = frames.reshape(steps, strip, width)
    later = ((steps - 1) * strip, width)
    mine, other, rest = call(
        functools.partial(pack_first_kernel, ch, crow),
        "pack_first",
        (flat, motion_forward, motion_backward),
        [(strip + crow + half, width)] * 2 + [later],
        [
            pltpu.VMEM((2, *piece), BF),
            pltpu.VMEM((2, *motion_forward.shape), jnp.int32),
            tmp,
            pltpu.SemaphoreType.DMA((5 + steps,)),
        ],
        in_hbm=(0, 1, 2),
        out_any=(2,),
    )
    pair, rest = call(
        functools.partial(pair_first_kernel, ch, crow),
        "pair_first",
        (mine, send(other, near(1)), rest),
        [(2 * (strip + crow) + half, width), later],
        in_any=(2,),
        out_any=(1,),
        aliases={2: 1},
    )
    received = send(pair, near(2))
    swapped = send(rest, near(1))
    soon = min(2, steps - 1)
    pair_near, pair_far = call(
        functools.partial(pair_kernel, soon),
        "pair_rest",
        (flat, swapped),
        [(2 * soon * strip, width), (2 * (steps - 1 - soon) * strip, width)],
        [pltpu.SemaphoreType.DMA((2 * (steps - 1),))],
        in_hbm=(0,),
        in_any=(1,),
        out_any=(0, 1),
    )
    layers = conv_weight.shape[1]
    conv, join_both, join_first = call(
        weights_kernel,
        "weights",
        (conv_weight, join_weight),
        [(layers, 2 * ch, 12 * ch), (2 * ch, 4 * ch), (2 * ch, 2 * ch)],
        free=True,
    )
    xq, codes, edge_e, edge_o, pair_near = call(
        functools.partial(gather_first_kernel, ch, crow),
        "gather_first",
        (pair, received, pair_near),
        [feature, (QUAD * crow, width)] + [(2 * half + QUAD * crow, width)] * 2 + [pair_near.shape],
        [tmp, pltpu.VMEM((2, half, width), BF)],
        in_any=(2,),
        out_any=(4,),
        aliases={2: 4},
    )
    halo_e, halo_o = code_e, code_o = send(edge_e, even), send(edge_o, odd)

    wide_act = pltpu.VMEM((3, (rows + 16) * ch, width), BF)
    flops = 2 * (rows + 2 * HALO) * width * ch * ch * 9 * layers
    part_shapes, sent_shapes = choice_shapes(width)
    acts = [wide_act, wide_act, pltpu.VMEM(((rows + 16) * ch, width), BF)]
    inner, saved, saved_held = call(
        functools.partial(inner_kernel, ch),
        "refine_inner",
        (xq, join_first, conv),
        [feature, (layers, 2, 3, 2 * ch, width), (layers, 2, ch, width)],
        acts,
        flops,
    )
    received_near = send(pair_near, near(2))
    feat, msg_e, msg_o, own, part, pair_far = call(
        functools.partial(outer_kernel, ch, steps),
        "refine_outer",
        (inner, saved, saved_held, halo_e, halo_o, join_first, conv, codes, pair_far),
        [feature, messages[0], messages[0], piece, piece, pair_far.shape],
        [tmp, pltpu.VMEM((2, *messages[0]), BF)] + [pltpu.VMEM(shape, BF) for shape in sent_shapes],
        flops // 4,
        in_any=(8,),
        out_any=(5,),
        aliases={8: 5},
    )
    feat_e, feat_o = send(msg_e, even), send(msg_o, odd)
    back = send(part, near(1))
    received_far = send(pair_far, near(2))
    outputs = call(lambda after, a, b: None, "results", (part,), [whole, whole], in_any=(0,), out_any=(0, 1), free=True)

    def choices_of(step):
        return call(
            functools.partial(choices_kernel, ch, step, steps),
            "choices",
            (codes, code_e, code_o, msg_e),
            part_shapes + (sent_shapes if step + 1 < steps else []),
            in_any=(3,),
        )

    def frame_of(step):
        near_one = step <= soon
        source = (pair_near, received_near) if near_one else (pair_far, received_far)
        return call(
            functools.partial(gather_kernel, ch, step - 1 if near_one else step - 1 - soon),
            "gather",
            (*source, msg_e),
            [feature],
            [tmp],
            in_any=(2,),
        )[0]

    x_now = frame_of(1)
    for step in range(1, steps):
        last = step == steps - 1
        choices = choices_of(step)
        args = [x_now, halo_e, halo_o, join_both, conv, feat, feat_e, feat_o, *choices, own, back, *outputs]
        many = len(args)
        outs = [] if last else [feature, messages[step], messages[step]]
        outs += [piece, piece, whole, whole]
        scratch = [tmp, *acts, pltpu.VMEM(((rows + 2 * HALO) * ch, width), BF), pltpu.SemaphoreType.DMA((2,))]
        scratch += [pltpu.VMEM(((rows + 2 * HALO) * ch, width), BF), pltpu.VMEM((2, 3 * half, width), BF)]
        scratch += [pltpu.VMEM((2 * strip, width) if last else (2, *messages[step]), BF)]
        if not last:
            x_now = frame_of(step + 1)
            args += [x_now]
        *results, own, part, out_f, out_g = call(
            functools.partial(step_kernel, ch, step, steps),
            "refine",
            args,
            outs,
            scratch,
            flops,
            in_any=(many - 4, many - 3, many - 2, many - 1),
            out_any=(len(outs) - 2, len(outs) - 1),
            aliases={many - 2: len(outs) - 2, many - 1: len(outs) - 1},
        )
        outputs = out_f, out_g
        if not last:
            feat, msg_e, msg_o = results
            halo_e, halo_o = feat_e, feat_o = send(msg_e, even), send(msg_o, odd)
        back = send(part, near(1))

    outputs = call(
        functools.partial(finish_kernel, strip, steps),
        "finish",
        [own, back, *outputs],
        [whole] * 2,
        [pltpu.SemaphoreType.DMA((2,))],
        in_any=(0, 1, 2, 3),
        out_any=(0, 1),
        aliases={2: 0, 3: 1},
    )
    return tuple(o.reshape(frames.shape) for o in outputs)


def solution(mesh):
    return jax.shard_map(
        on_device,
        mesh=mesh,
        in_specs=(
            P(None, None, ("clips", "tiles"), None),
            P(None, ("clips", "tiles")),
            P(None, ("clips", "tiles")),
            P(),
            P(),
        ),
        out_specs=(
            P(None, None, ("clips", "tiles"), None),
            P(None, None, ("clips", "tiles"), None),
        ),
        check_vma=False,
    )
```

```python
import functools

import jax
import jax.numpy as jnp
from jax import lax
from jax.experimental import pallas as pl
from jax.experimental.pallas import tpu as pltpu
from jax.sharding import PartitionSpec as P

BS = 8
REACH = 2
QUAD = 4
HALO = 4
CAPACITY = 4
BF = jnp.bfloat16
F32 = jnp.float32


class Place:
    def __init__(self):
        me = lax.axis_index("tiles")
        self.me = me
        self.strip = me % QUAD
        self.core = me % 2
        self.side = self.strip // 2
        self.group = me // QUAD
        self.odd = self.group % 2
        self.top = self.group == 0
        self.bottom = self.group == lax.axis_size("tiles") // QUAD - 1


def leaky(value):
    widened = value.astype(F32)
    return jnp.maximum(widened, 0.1 * widened).astype(BF)


def rows_first(src, src_start, dst, dst_start, tmp, ch):
    tmp[...] = src[pl.ds(src_start, BS * ch), :].astype(F32)
    for r in range(BS):
        row = tmp[pl.ds(r, ch, stride=BS), :]
        dst[pl.ds(dst_start + r * ch, ch), :] = row.astype(BF)


def channels_first(src, src_start, dst, tmp, ch):
    for r in range(BS):
        tmp[pl.ds(r, ch, stride=BS), :] = src[pl.ds(src_start + r * ch, ch), :].astype(F32)
    dst[...] = tmp[...].astype(BF)


def pack_first_kernel(ch, crow, frames, motion_f, motion_b, mine, other, rest, following, motion_buf, tmp, sems):
    place = Place()
    steps, strip = frames.shape[:2]
    half = HALO * ch
    core = place.core
    outs = (mine, other)
    lists = [
        pltpu.make_async_copy(motion, motion_buf.at[n], sems.at[4 + n]) for n, motion in enumerate((motion_f, motion_b))
    ]
    copies = []
    for n in range(2):
        back = 1 - core if n else core
        copies.append(frame_copy(frames, 0, back, outs[n].at[pl.ds(0, strip)], sems.at[n]))
        copies.append(frame_copy(frames, 1, back, following.at[n], sems.at[2 + n]))
    later = [
        frame_copy(frames, step, 1 - core, rest.at[pl.ds((step - 1) * strip, strip)], sems.at[5 + step])
        for step in range(1, steps)
    ]
    for copy in lists + copies + later:
        copy.start()
    for copy in lists:
        copy.wait()
    blocks = motion_f.shape[1]
    width = mine.shape[1]
    column = lax.broadcasted_iota(jnp.int32, motion_f.shape, 1)
    spread = jnp.where(
        lax.broadcasted_iota(jnp.int32, (blocks, width), 1) // BS
        == lax.broadcasted_iota(jnp.int32, (blocks, width), 0),
        1.0,
        0.0,
    ).astype(BF)
    wides = []
    for n in range(2):
        taken = motion_buf[n]
        across = taken // blocks
        code = (across - place.me + REACH) * (2 * blocks) + (taken - across * blocks - column + blocks - 1)
        wide = jnp.dot(code.astype(BF), spread, preferred_element_type=F32).astype(BF)
        frames_order = range(steps - 1) if n == 0 else range(steps - 2, -1, -1)
        wides += [wide[frame : frame + 1] for frame in frames_order]
    wides.append(jnp.zeros((crow - len(wides), width), BF))
    code = jnp.concatenate(wides, axis=0)
    for out in outs:
        out[pl.ds(strip, crow), :] = code
    for copy in copies:
        copy.wait()
    for n, out in enumerate(outs):
        tmp[...] = following[n].astype(F32)
        for r in range(HALO):
            row = tmp[pl.ds(place.side * (BS - HALO) + r, ch, stride=BS), :]
            out[pl.ds(strip + crow + r * ch, ch), :] = row.astype(BF)
    for copy in later:
        copy.wait()


def pair_first_kernel(ch, crow, mine, swapped, rest_in, out, edge, rest_out, tmp):
    place = Place()
    strip = BS * ch
    half = HALO * ch
    for n, piece in enumerate((mine, swapped)):
        at = place.core ^ n
        out[pl.ds(pl.multiple_of(at * strip, strip), strip), :] = piece[pl.ds(0, strip), :]
        for ref, start in ((out, 2 * strip), (edge, 2 * half)):
            ref[pl.ds(pl.multiple_of(start + at * crow, crow), crow), :] = piece[pl.ds(strip, crow), :]

        @pl.when(at == place.side)
        def _(piece=piece):
            tmp[...] = piece[pl.ds(0, strip), :].astype(F32)
            for r in range(HALO):
                row = tmp[pl.ds(place.side * (BS - HALO) + r, ch, stride=BS), :]
                edge[pl.ds(r * ch, ch), :] = row.astype(BF)
            edge[pl.ds(half, half), :] = piece[pl.ds(strip + crow, half), :]


def above_below(place, along, cross):
    left = place.side == 0
    along, cross = along.astype(F32), cross.astype(F32)
    return jnp.where(left, cross, along).astype(BF), jnp.where(left, along, cross).astype(BF)


def frame_copy(frames, step, back, out, sem):
    steps = frames.shape[0]
    return pltpu.make_async_copy(frames.at[step + back * (steps - 1 - 2 * step)], out, sem)


def pair_copies(frames, swapped, core, first, count, out, sems):
    strip = frames.shape[1]
    copies = []
    for n in range(count):
        step = first + n
        own = out.at[pl.ds(pl.multiple_of((2 * n + core) * strip, strip), strip)]
        his = out.at[pl.ds(pl.multiple_of((2 * n + 1 - core) * strip, strip), strip)]
        copies.append(frame_copy(frames, step, core, own, sems.at[2 * n]))
        copies.append(
            pltpu.make_async_copy(swapped.at[pl.ds((step - 1) * strip, strip)], his, sems.at[2 * n + 1])
        )
    return copies


def edge_rows(place, ch, pair, outer, out, start, tmp):
    strip = BS * ch
    one, two = pair[pl.ds(0, strip), :].astype(F32), pair[pl.ds(strip, strip), :].astype(F32)
    left = place.side == 0
    if outer:
        tmp[...] = jnp.where(left, one, two)
        first = place.side * (BS - HALO)
    else:
        tmp[...] = jnp.where(left, two, one)
        first = (1 - place.side) * (BS - HALO)
    for r in range(HALO):
        out[pl.ds(start + r * ch, ch), :] = tmp[pl.ds(first + r, ch, stride=BS), :].astype(BF)


def pair_kernel(ch, frames, swapped, near_out, far_out, last_out, tmp, sems):
    place = Place()
    steps, strip = frames.shape[:2]
    half = HALO * ch
    between = range(2, steps - 1)
    pairs = {1: near_out.at[pl.ds(0, 2 * strip)], steps - 1: last_out}
    for n, step in enumerate(between):
        pairs[step] = far_out.at[pl.ds(2 * n * strip, 2 * strip)]
    copies = []
    for step, out in pairs.items():
        copies += pair_copies(frames, swapped, place.core, step, 1, out, sems.at[pl.ds(2 * step, 2)])
    for copy in copies:
        copy.start()
    for copy in copies:
        copy.wait()
    edge_rows(place, ch, pairs[2], True, near_out, 2 * strip, tmp)
    at = 2 * len(between) * strip
    for step in range(3, steps):
        edge_rows(place, ch, pairs[step], True, far_out, at, tmp)
        at += half
    edge_rows(place, ch, last_out, False, far_out, at, tmp)


def gather_first_kernel(ch, crow, pair, received, near_in, conv, xq, codes, near_out, tmp):
    place = Place()
    strip = BS * ch
    for n, piece in enumerate((pair, received)):
        side = place.side ^ n
        for m in range(2):
            at = side * 2 + m
            rows_first(piece, m * strip, xq, pl.multiple_of(at * strip, strip), tmp, ch)
            code_at = pl.multiple_of(at * crow, crow)
            codes[pl.ds(code_at, crow), :] = piece[pl.ds(2 * strip + m * crow, crow), :]


def gather_kernel(ch, pair_at, edge_at, pair, received, after, xq, edges, tmp):
    strip = BS * ch
    half = HALO * ch
    side = Place().side
    for n, piece in enumerate((pair, received)):
        for m in range(2):
            start = ((side + n) % 2 * 2 + m) * strip
            rows_first(piece, pair_at + m * strip, xq, pl.multiple_of(start, strip), tmp, ch)
        edges[side ^ n] = piece[pl.ds(edge_at, half), :]


def gather_last_kernel(ch, inner_at, pair, received, after, xq, inner, tmp):
    strip = BS * ch
    for m in range(2):
        rows_first(pair, m * strip, xq, m * strip, tmp, ch)
    inner[...] = received[pl.ds(inner_at, HALO * ch), :]


class Codes:
    def __init__(self, rows):
        width = rows[0].shape[1]
        self.rows = rows
        self.blocks = width // BS
        k_id = lax.broadcasted_iota(jnp.int32, (width, width), 0)
        l_id = lax.broadcasted_iota(jnp.int32, (width, width), 1)
        base = (k_id // BS - l_id // BS + self.blocks - 1).astype(F32)
        self.base = jnp.where(k_id % BS == l_id % BS, base, -1.0e4)
        self.slot = k_id.astype(F32)
        self.before = jnp.where((k_id % BS == 0) & (k_id // BS < l_id // BS), 1.0, 0.0).astype(BF)
        self.lane = (lax.broadcasted_iota(jnp.int32, (1, width), 1) % BS).astype(F32)
        self.zero = jnp.zeros((width, width), BF)
        self.ranks = {}

    def plain(self, dest, source):
        ds = source - dest
        if abs(ds) > REACH:
            return self.zero
        shift = float((ds + REACH) * 2 * self.blocks)
        return jnp.where(self.rows[dest + 2] - shift == self.base, 1.0, 0.0).astype(BF)

    def rank_all(self, wanted):
        rows = []
        for dest, source in wanted:
            low = float((source - dest + REACH) * 2 * self.blocks)
            code = self.rows[dest + 2]
            rows.append(jnp.where((code >= low) & (code < low + 2 * self.blocks), 1.0, 0.0))
        count = len(rows)
        rows += [rows[0]] * (-count % 16)
        stacked = jnp.concatenate(rows, axis=0)
        before = jnp.dot(stacked.astype(BF), self.before, preferred_element_type=F32)
        for n, key in enumerate(wanted):
            self.ranks[key] = jnp.where(
                stacked[n : n + 1] > 0, before[n : n + 1] * BS + self.lane, -1.0e4
            )

    def packed(self, dest, source, region):
        at = self.ranks[dest, source] + float(region * CAPACITY * BS)
        return jnp.where(self.slot == at, 1.0, 0.0).astype(BF)

    def pack(self, dest, source, region):
        return lax.dot_general(
            self.plain(dest, source),
            self.packed(dest, source, region),
            (((1,), (1,)), ((), ())),
            preferred_element_type=F32,
        )


FROM_ABOVE = (((0, -2), (-1, -2), (-1, -3), (1, -1)), ((0, -1), (0, -2)))
FROM_BELOW = (
    ((QUAD - 1, QUAD + 1), (QUAD, QUAD + 1), (QUAD, QUAD + 2), (QUAD - 2, QUAD)),
    ((QUAD - 1, QUAD), (QUAD - 1, QUAD + 1)),
)
TO_BELOW = tuple(tuple((d + QUAD, s + QUAD) for d, s in tile) for tile in FROM_ABOVE)
TO_ABOVE = tuple(tuple((d - QUAD, s - QUAD) for d, s in tile) for tile in FROM_BELOW)


def step_codes(ch, place, step, steps, codes, along, cross):
    crow = codes.shape[0] // QUAD
    width = codes.shape[1]
    pick = place.core * (steps - 1) + step - 1
    row_id = lax.broadcasted_iota(jnp.int32, (crow, width), 0)
    start = 2 * HALO * ch
    above, below = above_below(
        place, along[pl.ds(start, 2 * crow), :], cross[pl.ds(start, 2 * crow), :]
    )

    def row(block):
        return jnp.sum(jnp.where(row_id == pick, block.astype(F32), 0.0), axis=0, keepdims=True)

    rows = [row(above[n * crow : (n + 1) * crow]) for n in range(2)]
    rows += [row(codes[pl.ds(strip * crow, crow), :]) for strip in range(QUAD)]
    rows += [row(below[n * crow : (n + 1) * crow]) for n in range(2)]
    return Codes(rows)


PARTS = (((-1,), True), ((0, 1), False), ((0, 1), True), ((2, 3), False), ((2, 3), True), ((QUAD,), False))


def tiles_of(dests, bottom):
    tiles = [source for source in range(QUAD) if any(abs(source - d) <= REACH for d in dests)]
    for side, near, tables in ((0, -1, FROM_ABOVE), (1, QUAD, FROM_BELOW)):
        if any(abs(near - d) <= REACH for d in dests):
            whole = bottom if side == 0 else not bottom
            tiles += [(side, 0), (side, 1)] if whole else [(side, 1), (side, 2)]
    return tiles


def receive_choice(code, dests, bottom, out):
    width = out.shape[0] // len(tiles_of(dests, bottom))
    for n, tile in enumerate(tiles_of(dests, bottom)):
        for m, dest in enumerate(dests):
            if isinstance(tile, int):
                value = code.plain(dest, tile)
            elif tile[1] == 0:
                value = code.plain(dest, -1 if tile[0] == 0 else QUAD)
            else:
                side, kind = tile
                regions = list(enumerate((FROM_ABOVE, FROM_BELOW)[side][kind - 1]))
                if kind == 1:
                    regions = regions[:3] if bottom == (side == 0) else regions[3:]
                value = sum((code.packed(d, source, at) for at, (d, source) in regions if d == dest), code.zero)
            out[pl.ds(n * width, width), pl.ds(m * width, width)] = value


SENT = tuple((side, tile) for side in range(2) for tile in range(2))


def sent_regions(side, tile):
    picks = {}
    for at, (dest, source) in enumerate((TO_ABOVE, TO_BELOW)[side][tile]):
        lower = (side == 1) == (tile == 0 and at < 3)
        picks.setdefault((source, lower), []).append((at, dest))
    return picks


def send_choice(code, side, tile, out):
    width = out.shape[1]
    for n, ((source, _), regions) in enumerate(sent_regions(side, tile).items()):
        total = sum(code.pack(dest, source, at) for at, dest in regions)
        out[pl.ds(n * width, width), :] = total.astype(BF)


def all_pairs(*tables):
    return sorted({pair for table in tables for tile in table for pair in tile})


def choices_kernel(ch, step, steps, codes, along, cross, after, *outs):
    place = Place()
    code = step_codes(ch, place, step, steps, codes, along, cross)
    code.rank_all(all_pairs(FROM_ABOVE, FROM_BELOW))
    for part, out in zip(PARTS, outs):
        receive_choice(code, *part, out)
    if step + 1 < steps:
        code = step_codes(ch, place, step + 1, steps, codes, along, cross)
        code.rank_all(all_pairs(TO_ABOVE, TO_BELOW))
        for item, out in zip(SENT, outs[len(PARTS) :]):
            send_choice(code, *item, out)


def choice_shapes(width):
    parts = [(len(tiles_of(*part)) * width, len(part[0]) * width) for part in PARTS]
    return parts, [(len(sent_regions(*item)) * width, width) for item in SENT]


def align(ch, feat, recv, aligned, offset, part, choice, only=None):
    dests, bottom = part
    half = HALO * ch
    shift = half if bottom else 0
    width = feat.shape[1]
    left = [
        feat[pl.ds(tile * BS * ch + shift, half), :]
        if isinstance(tile, int)
        else recv[tile[0], pl.ds(tile[1] * half, half), :]
        for tile in tiles_of(dests, bottom)
    ]
    if only is None:
        right = choice[...]
    else:
        right = choice[:, only * width : (only + 1) * width]
        dests = (dests[only],)
    got = jnp.dot(jnp.concatenate(left, axis=1), right, preferred_element_type=F32).astype(BF)
    for n, d in enumerate(dests):
        aligned[pl.ds((d * BS + offset) * ch + shift, half), :] = got[:, n * width : (n + 1) * width]


def pack_messages(ch, fout, par, sent, choices, msg_e, msg_o):
    half = HALO * ch
    strip = BS * ch
    width = fout.shape[1]
    for side, near in ((0, 0), (1, QUAD - 1)):
        shift = half if side == 1 else 0
        sent[side, pl.ds(0, half), :] = fout[pl.ds(near * strip + shift, half), :]
    for (side, tile), choice in zip(SENT, choices):
        left = [
            fout[pl.ds(source * strip + (half if lower else 0), half), :] for source, lower in sent_regions(side, tile)
        ]
        got = jnp.dot(jnp.concatenate(left, axis=1), choice[...], preferred_element_type=F32).astype(BF)
        if tile == 0:
            sent[side, pl.ds(half, half), :] = got
        else:
            lane = lax.broadcasted_iota(jnp.int32, (half // 2, width), 1)
            folded = jnp.where(lane < width // 2, got[: half // 2], pltpu.roll(got[half // 2 :], width // 2, 1))
            sent[side, pl.ds(2 * half, half // 2), :] = folded
    msg_e[...] = sent[1 - par]
    msg_o[...] = sent[par]


def unpack_message(ch, message, recv, side):
    half = HALO * ch
    width = message.shape[1]
    recv[side, pl.ds(0, 2 * half), :] = message[pl.ds(0, 2 * half), :]
    folded = message[pl.ds(2 * half, half // 2), :]
    recv[side, pl.ds(2 * half, half // 2), :] = folded
    recv[side, pl.ds(2 * half + half // 2, half // 2), :] = pltpu.roll(folded, width // 2, 1)


class Rows:
    def __init__(self, ch, width, top_ok, bottom_ok, count):
        lane = lax.broadcasted_iota(jnp.int32, (ch, width), 1)
        self.not_first = lane > 0
        self.not_last = lane < width - 1
        self.zero = jnp.zeros((ch, width), BF)
        self.top_ok = top_ok
        self.bottom_ok = bottom_ok
        self.count = count

    def active(self, value, row):
        act = leaky(value)
        if row < 0:
            act = jnp.where(self.top_ok, act, self.zero)
        if row >= self.count:
            act = jnp.where(self.bottom_ok, act, self.zero)
        return (
            jnp.where(self.not_first, pltpu.roll(act, 1, 1), self.zero),
            act,
            jnp.where(self.not_last, pltpu.roll(act, act.shape[1] - 1, 1), self.zero),
        )

    def put(self, buf, here, value, row):
        for n, act in enumerate(self.active(value, row)):
            buf[n, here, :] = act


OFF = 8


def here_of(row, ch, count=1):
    return pl.ds((row + OFF) * ch, count * ch)


def conv_layer(ch, weight, source, held, start, stop, emit):
    width = held.shape[1]
    for first in range(start, stop, 4):
        sides = [
            jnp.concatenate([source[n, here_of(first + 2 * h - 1, ch, 4), :] for n in range(3)], axis=0)
            for h in range(2)
        ]
        out = jnp.dot(weight, jnp.concatenate(sides, axis=1), preferred_element_type=F32)
        for h in range(2):
            for q in range(2):
                row = first + 2 * h + q
                total = held[here_of(row, ch), :].astype(F32)
                total += out[q * ch : (q + 1) * ch, h * width : (h + 1) * width]
                emit(row, total.astype(BF))


def join_first_rows(ch, join_mat, inp):
    width = inp.shape[1]
    mixed = jnp.dot(
        join_mat, jnp.concatenate([inp[: 2 * ch], inp[2 * ch :]], axis=1), preferred_element_type=F32
    ).astype(BF)
    return [mixed[q * ch : (q + 1) * ch, h * width : (h + 1) * width] for h in range(2) for q in range(2)]


def clear_outside(space, ch, rows, bufs):
    for buf in bufs:
        for row in (-HALO - 1, rows + HALO):
            for n in range(3):
                buf[n, here_of(row, ch), :] = space.zero


def conv_layers(ch, conv, space, rows, act_a, act_b, held, fout):
    layers = conv.shape[0]
    source, target = act_a, act_b
    for layer in range(layers):
        need = layers - 1 - layer
        reach = -(-need // 2) * 2
        start, stop = -reach, rows + reach
        if (stop - start) % 4:
            start, stop = -HALO, rows + HALO

        def emit(row, value, layer=layer, target=target):
            if layer < layers - 1:
                held[here_of(row, ch), :] = value
                space.put(target, here_of(row, ch), value, row)
            else:
                fout[pl.ds(row * ch, ch), :] = value

        conv_layer(ch, conv[layer], source, held, start, stop, emit)
        source, target = target, source


def inner_kernel(ch, xq, join, conv, feat, saved, saved_held, act_a, act_b, held):
    rows = QUAD * BS
    layers = conv.shape[0]
    space = Rows(ch, xq.shape[1], True, True, rows)
    for buf in (act_a, act_b):
        for row in (-1, rows):
            for n in range(3):
                buf[n, here_of(row, ch), :] = space.zero
    join_mat = join[...]
    for first in range(0, rows, 4):
        for n, value in enumerate(join_first_rows(ch, join_mat, xq[pl.ds(first * ch, 4 * ch), :])):
            held[here_of(first + n, ch), :] = value
            space.put(act_a, here_of(first + n, ch), value, first + n)
    source, target = act_a, act_b
    for layer in range(layers):
        for side, row, both in ((0, layer, layer), (1, rows - 1 - layer, rows - 2 - layer)):
            for n in range(3):
                saved[layer, side, n] = source[n, here_of(both, ch, 2), :]
            saved_held[layer, side] = held[here_of(row, ch), :]
        edge = (layer + 1) // 2 * 2

        def emit(row, value, layer=layer, target=target):
            if layer < layers - 1:
                held[here_of(row, ch), :] = value
                space.put(target, here_of(row, ch), value, row)
            else:
                feat[pl.ds(row * ch, ch), :] = value

        conv_layer(ch, conv[layer], source, held, edge, rows - edge, emit)
        source, target = target, source


def outer_kernel(ch, steps, *refs):
    feat_in, saved, saved_held, along, cross, join, conv, codes, far_in, *refs = refs
    fout, msg_e, msg_o, own_out, part_out, far_out, tmp, sent, *choices = refs
    half = HALO * ch
    strip = BS * ch
    rows = QUAD * BS
    place = Place()
    layers = conv.shape[0]
    width = feat_in.shape[1]
    space = Rows(ch, width, jnp.logical_not(place.top), jnp.logical_not(place.bottom), rows)
    code = step_codes(ch, place, 1, steps, codes, along, cross)
    code.rank_all(all_pairs(TO_ABOVE, TO_BELOW))
    for item, out in zip(SENT, choices):
        send_choice(code, *item, out)
    fout[pl.ds(half, (rows - 2 * HALO) * ch), :] = feat_in[pl.ds(half, (rows - 2 * HALO) * ch), :]
    halos = above_below(place, along[pl.ds(0, half), :], cross[pl.ds(0, half), :])
    join_mat = join[...]
    values = [join_first_rows(ch, join_mat, halo) for halo in halos]
    starts = [-HALO, rows]
    for layer in range(layers):
        weight = conv[layer]
        for side in range(2):
            acts = [space.active(value, starts[side] + n) for n, value in enumerate(values[side])]
            kept = [
                tuple(saved[layer, side, n, pl.ds(m * ch, ch), :] for n in range(3)) for m in range(2)
            ]
            beside = saved_held[layer, side]
            if side == 0:
                window, base = acts + kept, values[side][1:] + [beside]
                starts[side] += 1
            else:
                window, base = kept + acts, [beside] + values[side][:3]
                starts[side] -= 1
            halves = [
                jnp.concatenate([window[2 * h + m][n] for n in range(3) for m in range(4)], axis=0) for h in range(2)
            ]
            out = jnp.dot(weight, jnp.concatenate(halves, axis=1), preferred_element_type=F32)
            values[side] = [
                (
                    base[2 * h + q].astype(F32) + out[q * ch : (q + 1) * ch, h * width : (h + 1) * width]
                ).astype(BF)
                for h in range(2)
                for q in range(2)
            ]
    for side in range(2):
        for n, value in enumerate(values[side]):
            fout[pl.ds((starts[side] + n) * ch, ch), :] = value
    pack_messages(ch, fout, place.odd, sent, choices, msg_e, msg_o)
    channels_first(fout, pl.multiple_of(place.strip * strip, strip), own_out, tmp, ch)
    channels_first(fout, pl.multiple_of((place.strip ^ 1) * strip, strip), part_out, tmp, ch)


def step_kernel(ch, step, steps, *refs):
    strip = BS * ch
    half = HALO * ch
    last = step == steps - 1
    refs = list(refs)

    def take(count):
        taken = refs[:count]
        del refs[:count]
        return taken

    xq, halo_e, halo_o, join, conv = take(5)
    feat, feat_e, feat_o = take(3)
    choices = take(len(PARTS) + (0 if last else len(SENT)))
    before, out_a, out_b = take(3)
    backs = take(steps - 1 if last else 0)
    held_back = take(step if step == steps - 2 else 0)
    if last:
        (x_inner,) = take(1)
    else:
        next_edges, fout, msg_e, msg_o = take(4)
    own_out, part_out, out_f, out_g = take(4)
    take(len(held_back))
    tmp, act_a, act_b, held, sems, aligned, recv = take(7)
    if last:
        (fout,) = take(1)
    else:
        (sent,) = take(1)
    width = xq.shape[-1]
    place = Place()
    par = place.odd
    core = place.core
    quad_rows = QUAD * BS
    rows = 2 * BS if last else quad_rows
    right_side = place.side
    own = place.core if last else place.strip

    copies = own_copies(strip, step - 1, steps, before, out_f, out_g, sems.at[0])
    for n, back in enumerate(backs):
        copies += back_copies(strip, n, steps, back, out_f, out_g, sems.at[1 + n])
    for n, copy in copies:
        pl.when(core == n)(copy.start)
    halo_at = 5 * half // 2
    if step == 1:
        over, under = above_below(place, halo_e[pl.ds(half, half), :], halo_o[pl.ds(half, half), :])
    else:
        one, two = halo_e[pl.ds(halo_at, half), :].astype(F32), halo_o[pl.ds(halo_at, half), :].astype(F32)
        over = jnp.where(par == 1, one, two).astype(BF)
        under = jnp.where(par == 1, two, one).astype(BF)
    if last:
        inner = x_inner[...].astype(F32)
        over, under = (
            jnp.where(right_side == 0, over.astype(F32), inner).astype(BF),
            jnp.where(right_side == 0, inner, under.astype(F32)).astype(BF),
        )
    unpack_message(ch, feat_e, recv, 1 - par)
    unpack_message(ch, feat_o, recv, par)
    if last:

        @pl.when(right_side == 0)
        def _():
            for n in range(3):
                align(ch, feat, recv, aligned, HALO, PARTS[n], choices[n])
            align(ch, feat, recv, aligned, HALO, PARTS[3], choices[3], 0)

        @pl.when(right_side == 1)
        def _():
            offset = HALO - 2 * BS
            align(ch, feat, recv, aligned, offset, PARTS[2], choices[2], 1)
            for n in range(3, 6):
                align(ch, feat, recv, aligned, offset, PARTS[n], choices[n])

    else:
        for n, rows_part in enumerate(PARTS):
            align(ch, feat, recv, aligned, HALO, rows_part, choices[n])
        for n in range(2):
            sent[n, pl.ds(halo_at, half), :] = next_edges[n]

    top_ok = jnp.logical_not(place.top)
    bottom_ok = jnp.logical_not(place.bottom)
    if last:
        top_ok = top_ok | (right_side == 1)
        bottom_ok = bottom_ok | (right_side == 0)
    space = Rows(ch, width, top_ok, bottom_ok, rows)
    clear_outside(space, ch, rows, (act_a, act_b))
    join_mat = join[...]
    for g in range((rows + 2 * HALO) // 4):
        first = g * 4 - HALO
        inp = over if first < 0 else under if first >= rows else xq[pl.ds(first * ch, 4 * ch), :]
        al = aligned[pl.ds(g * 4 * ch, 4 * ch), :]
        sides = []
        for h in range(2):
            a, b = 2 * h * ch, (2 * h + 1) * ch
            sides.append(jnp.concatenate([al[a : a + ch], inp[a : a + ch], al[b : b + ch], inp[b : b + ch]], axis=0))
        mixed = jnp.dot(join_mat, jnp.concatenate(sides, axis=1), preferred_element_type=F32).astype(BF)
        for h in range(2):
            for q in range(2):
                row = first + 2 * h + q
                value = mixed[q * ch : (q + 1) * ch, h * width : (h + 1) * width]
                held[here_of(row, ch), :] = value
                space.put(act_a, here_of(row, ch), value, row)

    conv_layers(ch, conv, space, rows, act_a, act_b, held, fout)
    if not last:
        pack_messages(ch, fout, par, sent, choices[-len(SENT) :], msg_e, msg_o)
    channels_first(fout, pl.multiple_of(own * strip, strip), own_out, tmp, ch)
    channels_first(fout, pl.multiple_of((own ^ 1) * strip, strip), part_out, tmp, ch)
    for n, copy in copies:
        pl.when(core == n)(copy.wait)


def own_copies(strip, step, steps, own, out_f, out_g, sem):
    return [
        (0, pltpu.make_async_copy(own, out_f.at[pl.ds(step * strip, strip)], sem)),
        (1, pltpu.make_async_copy(own, out_g.at[pl.ds((steps - 1 - step) * strip, strip)], sem)),
    ]


def back_copies(strip, step, steps, back, out_f, out_g, sem):
    return [
        (0, pltpu.make_async_copy(back, out_g.at[pl.ds((steps - 1 - step) * strip, strip)], sem)),
        (1, pltpu.make_async_copy(back, out_f.at[pl.ds(step * strip, strip)], sem)),
    ]


def finish_kernel(strip, steps, own, back, out_a, out_b, out_f, out_g, sems):
    core = Place().core
    copies = own_copies(strip, steps - 1, steps, own, out_f, out_g, sems.at[0])
    copies += back_copies(strip, steps - 1, steps, back, out_f, out_g, sems.at[1])
    for n, copy in copies:
        pl.when(core == n)(copy.start)
    for n, copy in copies:
        pl.when(core == n)(copy.wait)


def weights_kernel(conv, join, wide, join_both, join_first):
    core = Place().core
    layers, ch = conv.shape[1], conv.shape[3]
    zero = jnp.zeros((ch, ch), BF)
    for layer in range(layers):
        for dx in range(3):
            taps = [conv[core, layer, 3 * dy + dx] for dy in range(3)]
            for q in range(2):
                line = [zero] * q + taps + [zero] * (1 - q)
                wide[layer, pl.ds(q * ch, ch), pl.ds(dx * 4 * ch, 4 * ch)] = jnp.concatenate(line, axis=1)
    both = join[core]
    none = jnp.zeros_like(both)
    join_both[pl.ds(0, ch), :] = jnp.concatenate([both, none], axis=1)
    join_both[pl.ds(ch, ch), :] = jnp.concatenate([none, both], axis=1)
    enter = both[:, ch:]
    join_first[pl.ds(0, ch), :] = jnp.concatenate([enter, zero], axis=1)
    join_first[pl.ds(ch, ch), :] = jnp.concatenate([zero, enter], axis=1)


VMEM = pl.BlockSpec(memory_space=pltpu.VMEM)
ANY = pl.BlockSpec(memory_space=pl.ANY)
HBM = pl.BlockSpec(memory_space=pltpu.HBM)


def call(kernel, name, args, outs, scratch=(), flops=0, in_any=(), out_any=(), aliases=None, in_hbm=(), free=False):
    args = [pltpu.with_memory_space_constraint(a, pltpu.HBM) if n in in_hbm else a for n, a in enumerate(args)]
    return pl.pallas_call(
        kernel,
        out_shape=[jax.ShapeDtypeStruct(o, BF) for o in outs],
        in_specs=[HBM if n in in_hbm else ANY if n in in_any else VMEM for n in range(len(args))],
        out_specs=[ANY if n in out_any else VMEM for n in range(len(outs))],
        scratch_shapes=list(scratch),
        input_output_aliases=aliases or {},
        compiler_params=pltpu.CompilerParams(vmem_limit_bytes=32 << 20),
        cost_estimate=pl.CostEstimate(
            flops=flops,
            bytes_accessed=0 if free else sum(a.size * a.dtype.itemsize for a in args),
            transcendentals=0,
        ),
        name=name,
    )(*args)


def sooner(value):
    return pl.pallas_call(
        lambda given, out: None,
        out_shape=jax.ShapeDtypeStruct(value.shape, value.dtype),
        in_specs=[ANY],
        out_specs=ANY,
        input_output_aliases={0: 0},
        compiler_params=pltpu.CompilerParams(vmem_limit_bytes=1 << 20),
        cost_estimate=pl.CostEstimate(flops=0, bytes_accessed=2 << 20, transcendentals=0),
        name="sooner",
    )(value)


def pairings(count, idle):
    groups = count // QUAD
    out = []
    for parity in range(2):
        pairs = []
        for i in range(count):
            g = i // QUAD
            other = g + 1 if g % 2 == parity else g - 1
            pairs.append((i, i % QUAD + other * QUAD if 0 <= other < groups else i ^ idle))
        out.append(pairs)
    return out


def edge_pairings(count):
    groups = count // QUAD
    along, cross = [], []
    for i in range(count):
        g, side, core = i // QUAD, i % QUAD // 2, i % 2
        if side == 0:
            along += [(i, i - QUAD)] if g > 0 else []
            cross.append((i, i - QUAD + 2 if g > 0 else i ^ 1))
        else:
            along += [(i, i + QUAD)] if g < groups - 1 else []
            cross.append((i, i + QUAD - 2 if g < groups - 1 else i ^ 1))
    return along, cross


def on_device(frames, motion_forward, motion_backward, join_weight, conv_weight):
    steps, ch, strip_rows, width = frames.shape
    strip = strip_rows * ch
    half = HALO * ch
    crow = 16
    count = lax.axis_size("tiles")
    even, odd = pairings(count, 1)
    along_pairs, cross_pairs = edge_pairings(count)

    def near(k):
        return [(i, i ^ k) for i in range(count)]

    def send(value, pairs):
        return lax.ppermute(value, "tiles", pairs)

    tmp = pltpu.VMEM((strip, width), F32)
    piece = (strip, width)
    rows = QUAD * BS
    messages = [(5 * half // 2, width)] + [(7 * half // 2, width)] * (steps - 2)
    feature = (rows * ch, width)
    whole = (steps * strip, width)
    flat = frames.reshape(steps, strip, width)
    later = ((steps - 1) * strip, width)
    mine, other, rest = call(
        functools.partial(pack_first_kernel, ch, crow),
        "pack_first",
        (flat, motion_forward, motion_backward),
        [(strip + crow + half, width)] * 2 + [later],
        [
            pltpu.VMEM((2, *piece), BF),
            pltpu.VMEM((2, *motion_forward.shape), jnp.int32),
            tmp,
            pltpu.SemaphoreType.DMA((5 + steps,)),
        ],
        in_hbm=(0, 1, 2),
        out_any=(2,),
    )
    pair, edge, rest = call(
        functools.partial(pair_first_kernel, ch, crow),
        "pair_first",
        (mine, send(other, near(1)), rest),
        [(2 * (strip + crow), width), (2 * (half + crow), width), later],
        [tmp],
        in_any=(2,),
        out_any=(2,),
        aliases={2: 2},
    )
    received = send(pair, near(2))
    along, cross = sooner(send(edge, along_pairs)), send(edge, cross_pairs)
    swapped = send(rest, near(1))
    far_pairs = 2 * (steps - 3) * strip
    pair_near, pair_far, pair_last = call(
        functools.partial(pair_kernel, ch),
        "pair_rest",
        (flat, swapped),
        [(2 * strip + half, width), (far_pairs + (steps - 2) * half, width), (2 * strip, width)],
        [tmp, pltpu.SemaphoreType.DMA((2 * steps,))],
        in_hbm=(0,),
        in_any=(1,),
    )
    layers = conv_weight.shape[1]
    conv, join_both, join_first = call(
        weights_kernel,
        "weights",
        (conv_weight, join_weight),
        [(layers, 2 * ch, 12 * ch), (2 * ch, 4 * ch), (2 * ch, 2 * ch)],
        free=True,
    )
    xq, codes, pair_near = call(
        functools.partial(gather_first_kernel, ch, crow),
        "gather_first",
        (pair, received, pair_near, conv),
        [feature, (QUAD * crow, width), pair_near.shape],
        [tmp],
        in_any=(2, 3),
        free=True,
        out_any=(2,),
        aliases={2: 2},
    )
    halo_e, halo_o = along, cross

    wide_act = pltpu.VMEM((3, (rows + 16) * ch, width), BF)
    flops = 2 * (rows + 2 * HALO) * width * ch * ch * 9 * layers
    part_shapes, sent_shapes = choice_shapes(width)
    acts = [wide_act, wide_act, pltpu.VMEM(((rows + 16) * ch, width), BF)]
    received_near = send(pair_near, near(2))
    inner, saved, saved_held = call(
        functools.partial(inner_kernel, ch),
        "refine_inner",
        (xq, join_first, conv),
        [feature, (layers, 2, 3, 2 * ch, width), (layers, 2, ch, width)],
        acts,
        free=True,
    )
    feat, msg_e, msg_o, own, part, pair_far = call(
        functools.partial(outer_kernel, ch, steps),
        "refine_outer",
        (inner, saved, saved_held, along, cross, join_first, conv, codes, pair_far),
        [feature, messages[0], messages[0], piece, piece, pair_far.shape],
        [tmp, pltpu.VMEM((2, *messages[0]), BF)] + [pltpu.VMEM(shape, BF) for shape in sent_shapes],
        flops // 4,
        in_any=(8,),
        out_any=(5,),
        aliases={8: 5},
    )
    feat_e, feat_o = sooner(send(msg_e, even)), send(msg_o, odd)
    parts = [part]
    received_far = send(pair_far, near(2))
    outputs = call(lambda after, a, b: None, "results", (part,), [whole, whole], in_any=(0,), out_any=(0, 1), free=True)

    def choices_of(step):
        return call(
            functools.partial(choices_kernel, ch, step, steps),
            "choices",
            (codes, along, cross, msg_e),
            part_shapes + (sent_shapes if step + 1 < steps else []),
            in_any=(3,),
        )

    def frame_of(step):
        if step == steps - 1:
            kernel = functools.partial(gather_last_kernel, ch, far_pairs + (steps - 3) * half)
            args, outs = (pair_last, received_far, msg_e), [(2 * strip, width), (half, width)]
        elif step == 1:
            kernel = functools.partial(gather_kernel, ch, 0, 2 * strip)
            args, outs = (pair_near, received_near, msg_e), [feature, (2, half, width)]
        else:
            kernel = functools.partial(gather_kernel, ch, 2 * (step - 2) * strip, far_pairs + (step - 2) * half)
            args, outs = (pair_far, received_far, msg_e), [feature, (2, half, width)]
        return call(kernel, "gather", args, outs, [tmp], in_any=(2,))

    for step in range(1, steps):
        last = step == steps - 1
        choices = choices_of(step)
        x_now, beside = frame_of(step)
        args = [x_now, halo_e, halo_o, join_both, conv, feat, feat_e, feat_o, *choices, own, *outputs]
        many = len(args)
        outs = [] if last else [feature, messages[step], messages[step]]
        outs += [piece, piece, whole, whole]
        in_any = [many - 3, many - 2, many - 1]
        out_any = [len(outs) - 2, len(outs) - 1]
        aliases = {many - 2: len(outs) - 2, many - 1: len(outs) - 1}
        if last:
            backs = [send(part, near(1)) for part in parts]
            in_any += range(many, many + len(backs))
            args += backs
        elif step == steps - 2:
            for n, part in enumerate(parts):
                aliases[len(args)] = len(outs)
                in_any.append(len(args))
                out_any.append(len(outs))
                args.append(part)
                outs.append(piece)
        args += [beside]
        scratch = [tmp, *acts, pltpu.SemaphoreType.DMA((steps,))]
        scratch += [pltpu.VMEM(((rows + 2 * HALO) * ch, width), BF), pltpu.VMEM((2, 3 * half, width), BF)]
        scratch += [pltpu.VMEM((2 * strip, width) if last else (2, *messages[step]), BF)]
        results = call(
            functools.partial(step_kernel, ch, step, steps),
            "refine",
            args,
            outs,
            scratch,
            flops,
            in_any=in_any,
            out_any=out_any,
            aliases=aliases,
        )
        if not last:
            feat, msg_e, msg_o, *results = results
            halo_e, halo_o = feat_e, feat_o = sooner(send(msg_e, even)), send(msg_o, odd)
        own, part, out_f, out_g, *held_back = results
        outputs = out_f, out_g
        parts = (held_back or parts) + [part]
    back = send(part, near(1))

    outputs = call(
        functools.partial(finish_kernel, strip, steps),
        "finish",
        [own, back, *outputs],
        [whole] * 2,
        [pltpu.SemaphoreType.DMA((2,))],
        in_any=(0, 1, 2, 3),
        out_any=(0, 1),
        aliases={2: 0, 3: 1},
    )
    return tuple(o.reshape(frames.shape) for o in outputs)


def solution(mesh):
    return jax.shard_map(
        on_device,
        mesh=mesh,
        in_specs=(
            P(None, None, ("clips", "tiles"), None),
            P(None, ("clips", "tiles")),
            P(None, ("clips", "tiles")),
            P(),
            P(),
        ),
        out_specs=(
            P(None, None, ("clips", "tiles"), None),
            P(None, None, ("clips", "tiles"), None),
        ),
        check_vma=False,
    )
```

```python
import functools

import jax
import jax.numpy as jnp
from jax import lax
from jax.experimental import pallas as pl
from jax.experimental.pallas import tpu as pltpu
from jax.sharding import PartitionSpec as P

BS = 8
REACH = 2
QUAD = 4
HALO = 4
CAPACITY = 4
BF = jnp.bfloat16
F32 = jnp.float32


class Place:
    def __init__(self):
        me = lax.axis_index("tiles")
        self.me = me
        self.strip = me % QUAD
        self.core = me % 2
        self.side = self.strip // 2
        self.group = me // QUAD
        self.odd = self.group % 2
        self.top = self.group == 0
        self.bottom = self.group == lax.axis_size("tiles") // QUAD - 1


def leaky(value):
    widened = value.astype(F32)
    return jnp.maximum(widened, 0.1 * widened).astype(BF)


def rows_first(src, src_start, dst, dst_start, tmp, ch):
    tmp[...] = src[pl.ds(src_start, BS * ch), :].astype(F32)
    for r in range(BS):
        row = tmp[pl.ds(r, ch, stride=BS), :]
        dst[pl.ds(dst_start + r * ch, ch), :] = row.astype(BF)


def channels_first(src, src_start, dst, tmp, ch):
    for r in range(BS):
        tmp[pl.ds(r, ch, stride=BS), :] = src[pl.ds(src_start + r * ch, ch), :].astype(F32)
    dst[...] = tmp[...].astype(BF)


def pack_first_kernel(ch, crow, frames, motion_f, motion_b, mine, mine_edge, other, rest, following, motion_buf, tmp, sems):
    place = Place()
    steps, strip = frames.shape[:2]
    half = HALO * ch
    core = place.core
    outs = (mine, other)
    lists = [
        pltpu.make_async_copy(motion, motion_buf.at[n], sems.at[4 + n]) for n, motion in enumerate((motion_f, motion_b))
    ]
    copies = []
    for n in range(2):
        back = 1 - core if n else core
        copies.append(frame_copy(frames, 0, back, outs[n].at[pl.ds(0, strip)], sems.at[n]))
        copies.append(frame_copy(frames, 1, back, following.at[n], sems.at[2 + n]))
    later = [
        frame_copy(frames, step, 1 - core, rest.at[pl.ds((step - 1) * strip, strip)], sems.at[5 + step])
        for step in range(1, steps)
    ]
    for copy in lists + copies + later:
        copy.start()
    for copy in lists:
        copy.wait()
    blocks = motion_f.shape[1]
    width = mine.shape[1]
    column = lax.broadcasted_iota(jnp.int32, motion_f.shape, 1)
    spread = jnp.where(
        lax.broadcasted_iota(jnp.int32, (blocks, width), 1) // BS
        == lax.broadcasted_iota(jnp.int32, (blocks, width), 0),
        1.0,
        0.0,
    ).astype(BF)
    wides = []
    for n in range(2):
        taken = motion_buf[n]
        across = taken // blocks
        code = (across - place.me + REACH) * (2 * blocks) + (taken - across * blocks - column + blocks - 1)
        wide = jnp.dot(code.astype(BF), spread, preferred_element_type=F32).astype(BF)
        frames_order = range(steps - 1) if n == 0 else range(steps - 2, -1, -1)
        wides += [wide[frame : frame + 1] for frame in frames_order]
    wides.append(jnp.zeros((crow - len(wides), width), BF))
    code = jnp.concatenate(wides, axis=0)
    for out in outs:
        out[pl.ds(strip, crow), :] = code
    for copy in copies:
        copy.wait()
    for n, (out, start) in enumerate(((mine_edge, 0), (other, strip + crow))):
        edge_of(place.side == 0, ch, following[n], out, start, tmp)
    for copy in later:
        copy.wait()


def edge_of(top, ch, strip_values, out, start, tmp):
    tmp[...] = strip_values.astype(F32)
    for r in range(HALO):
        one, two = tmp[pl.ds(r, ch, stride=BS), :], tmp[pl.ds(BS - HALO + r, ch, stride=BS), :]
        out[pl.ds(start + r * ch, ch), :] = jnp.where(top, one, two).astype(BF)


def pair_first_kernel(ch, crow, mine, mine_edge, partner, rest_in, out, edge, edge_too, rest_out, tmp):
    place = Place()
    strip = BS * ch
    half = HALO * ch
    own = place.core == place.side
    first = jnp.where(own, mine[pl.ds(0, strip), :].astype(F32), partner[pl.ds(0, strip), :].astype(F32))
    edge_of(place.side == 0, ch, first, edge, 0, tmp)
    second = partner[pl.ds(strip + crow, half), :].astype(F32)
    edge[pl.ds(half, half), :] = jnp.where(own, mine_edge[...].astype(F32), second).astype(BF)
    for n, piece in enumerate((mine, partner)):
        at = place.core ^ n
        out[pl.ds(pl.multiple_of(at * strip, strip), strip), :] = piece[pl.ds(0, strip), :]
        for ref, start in ((out, 2 * strip), (edge, 2 * half)):
            ref[pl.ds(pl.multiple_of(start + at * crow, crow), crow), :] = piece[pl.ds(strip, crow), :]
    edge_too[...] = edge[...]


def above_below(place, along, cross):
    left = place.side == 0
    along, cross = along.astype(F32), cross.astype(F32)
    return jnp.where(left, cross, along).astype(BF), jnp.where(left, along, cross).astype(BF)


def frame_copy(frames, step, back, out, sem):
    steps = frames.shape[0]
    return pltpu.make_async_copy(frames.at[step + back * (steps - 1 - 2 * step)], out, sem)


def pair_copies(frames, swapped, core, first, count, out, sems):
    strip = frames.shape[1]
    copies = []
    for n in range(count):
        step = first + n
        own = out.at[pl.ds(pl.multiple_of((2 * n + core) * strip, strip), strip)]
        his = out.at[pl.ds(pl.multiple_of((2 * n + 1 - core) * strip, strip), strip)]
        copies.append(frame_copy(frames, step, core, own, sems.at[2 * n]))
        copies.append(
            pltpu.make_async_copy(swapped.at[pl.ds((step - 1) * strip, strip)], his, sems.at[2 * n + 1])
        )
    return copies


def edge_rows(place, ch, pair, outer, out, start, tmp):
    strip = BS * ch
    one, two = pair[pl.ds(0, strip), :].astype(F32), pair[pl.ds(strip, strip), :].astype(F32)
    left = place.side == 0
    if outer:
        edge_of(left, ch, jnp.where(left, one, two), out, start, tmp)
    else:
        edge_of(jnp.logical_not(left), ch, jnp.where(left, two, one), out, start, tmp)


def pair_kernel(ch, frames, swapped, edge_in, near_out, far_out, last_out, edge_out, tmp, sems):
    place = Place()
    steps, strip = frames.shape[:2]
    half = HALO * ch
    between = range(2, steps - 1)
    pairs = {1: near_out.at[pl.ds(0, 2 * strip)], steps - 1: last_out}
    for n, step in enumerate(between):
        pairs[step] = far_out.at[pl.ds(2 * n * strip, 2 * strip)]
    copies = []
    for step, out in pairs.items():
        copies += pair_copies(frames, swapped, place.core, step, 1, out, sems.at[pl.ds(2 * step, 2)])
    for copy in copies:
        copy.start()
    for copy in copies:
        copy.wait()
    edge_rows(place, ch, pairs[2], True, near_out, 2 * strip, tmp)
    at = 2 * len(between) * strip
    for step in range(3, steps):
        edge_rows(place, ch, pairs[step], True, far_out, at, tmp)
        at += half
    edge_rows(place, ch, last_out, False, far_out, at, tmp)


def gather_first_kernel(ch, crow, pair, received, conv, near_in, xq, codes, near_out, tmp):
    place = Place()
    strip = BS * ch
    for n, piece in enumerate((pair, received)):
        side = place.side ^ n
        for m in range(2):
            at = side * 2 + m
            rows_first(piece, m * strip, xq, pl.multiple_of(at * strip, strip), tmp, ch)
            code_at = pl.multiple_of(at * crow, crow)
            codes[pl.ds(code_at, crow), :] = piece[pl.ds(2 * strip + m * crow, crow), :]


def gather_kernel(ch, pair_at, edge_at, pair, received, feat, xq, edges, own_out, part_out, tmp):
    strip = BS * ch
    half = HALO * ch
    side = Place().side
    for n, piece in enumerate((pair, received)):
        for m in range(2):
            start = ((side + n) % 2 * 2 + m) * strip
            rows_first(piece, pair_at + m * strip, xq, pl.multiple_of(start, strip), tmp, ch)
        edges[side ^ n] = piece[pl.ds(edge_at, half), :]
    split_results(ch, feat, own_out, part_out, tmp)


def split_results(ch, feat, own_out, part_out, tmp):
    strip = BS * ch
    own = Place().strip
    channels_first(feat, pl.multiple_of(own * strip, strip), own_out, tmp, ch)
    channels_first(feat, pl.multiple_of((own ^ 1) * strip, strip), part_out, tmp, ch)


def gather_last_kernel(ch, inner_at, pair, received, feat, xq, inner, own_out, part_out, tmp):
    strip = BS * ch
    for m in range(2):
        rows_first(pair, m * strip, xq, m * strip, tmp, ch)
    inner[...] = received[pl.ds(inner_at, HALO * ch), :]
    split_results(ch, feat, own_out, part_out, tmp)


class Codes:
    def __init__(self, rows):
        width = rows[0].shape[1]
        self.rows = rows
        self.blocks = width // BS
        k_id = lax.broadcasted_iota(jnp.int32, (width, width), 0)
        l_id = lax.broadcasted_iota(jnp.int32, (width, width), 1)
        base = (k_id // BS - l_id // BS + self.blocks - 1).astype(F32)
        self.base = jnp.where(k_id % BS == l_id % BS, base, -1.0e4)
        self.slot = k_id.astype(F32)
        self.before = jnp.where((k_id % BS == 0) & (k_id // BS < l_id // BS), 1.0, 0.0).astype(BF)
        self.lane = (lax.broadcasted_iota(jnp.int32, (1, width), 1) % BS).astype(F32)
        self.zero = jnp.zeros((width, width), BF)
        self.ranks = {}

    def plain(self, dest, source):
        ds = source - dest
        if abs(ds) > REACH:
            return self.zero
        shift = float((ds + REACH) * 2 * self.blocks)
        return jnp.where(self.rows[dest + 2] - shift == self.base, 1.0, 0.0).astype(BF)

    def rank_all(self, wanted):
        rows = []
        for dest, source in wanted:
            low = float((source - dest + REACH) * 2 * self.blocks)
            code = self.rows[dest + 2]
            rows.append(jnp.where((code >= low) & (code < low + 2 * self.blocks), 1.0, 0.0))
        count = len(rows)
        rows += [rows[0]] * (-count % 16)
        stacked = jnp.concatenate(rows, axis=0)
        before = jnp.dot(stacked.astype(BF), self.before, preferred_element_type=F32)
        for n, key in enumerate(wanted):
            self.ranks[key] = jnp.where(
                stacked[n : n + 1] > 0, before[n : n + 1] * BS + self.lane, -1.0e4
            )

    def packed(self, dest, source, region):
        at = self.ranks[dest, source] + float(region * CAPACITY * BS)
        return jnp.where(self.slot == at, 1.0, 0.0).astype(BF)

    def pack(self, dest, source, region):
        return lax.dot_general(
            self.plain(dest, source),
            self.packed(dest, source, region),
            (((1,), (1,)), ((), ())),
            preferred_element_type=F32,
        )


FROM_ABOVE = (((0, -2), (-1, -2), (-1, -3), (1, -1)), ((0, -1), (0, -2)))
FROM_BELOW = (
    ((QUAD - 1, QUAD + 1), (QUAD, QUAD + 1), (QUAD, QUAD + 2), (QUAD - 2, QUAD)),
    ((QUAD - 1, QUAD), (QUAD - 1, QUAD + 1)),
)
TO_BELOW = tuple(tuple((d + QUAD, s + QUAD) for d, s in tile) for tile in FROM_ABOVE)
TO_ABOVE = tuple(tuple((d - QUAD, s - QUAD) for d, s in tile) for tile in FROM_BELOW)


def step_codes(ch, place, step, steps, codes, along, cross):
    crow = codes.shape[0] // QUAD
    width = codes.shape[1]
    pick = place.core * (steps - 1) + step - 1
    row_id = lax.broadcasted_iota(jnp.int32, (crow, width), 0)
    start = 2 * HALO * ch
    above, below = above_below(
        place, along[pl.ds(start, 2 * crow), :], cross[pl.ds(start, 2 * crow), :]
    )

    def row(block):
        return jnp.sum(jnp.where(row_id == pick, block.astype(F32), 0.0), axis=0, keepdims=True)

    rows = [row(above[n * crow : (n + 1) * crow]) for n in range(2)]
    rows += [row(codes[pl.ds(strip * crow, crow), :]) for strip in range(QUAD)]
    rows += [row(below[n * crow : (n + 1) * crow]) for n in range(2)]
    return Codes(rows)


PARTS = (((-1,), True), ((0, 1), False), ((0, 1), True), ((2, 3), False), ((2, 3), True), ((QUAD,), False))


def tiles_of(dests, bottom):
    tiles = [source for source in range(QUAD) if any(abs(source - d) <= REACH for d in dests)]
    for side, near, tables in ((0, -1, FROM_ABOVE), (1, QUAD, FROM_BELOW)):
        if any(abs(near - d) <= REACH for d in dests):
            whole = bottom if side == 0 else not bottom
            tiles += [(side, 0), (side, 1)] if whole else [(side, 1), (side, 2)]
    return tiles


def receive_choice(code, dests, bottom, near, far):
    width = code.zero.shape[0]
    tiles = tiles_of(dests, bottom)
    own = sum(isinstance(tile, int) for tile in tiles)
    for n, tile in enumerate(tiles):
        out, at = (near, n) if n < own else (far, n - own)
        for m, dest in enumerate(dests):
            if isinstance(tile, int):
                value = code.plain(dest, tile)
            elif tile[1] == 0:
                value = code.plain(dest, -1 if tile[0] == 0 else QUAD)
            else:
                side, kind = tile
                regions = list(enumerate((FROM_ABOVE, FROM_BELOW)[side][kind - 1]))
                if kind == 1:
                    regions = regions[:3] if bottom == (side == 0) else regions[3:]
                value = sum((code.packed(d, source, at_) for at_, (d, source) in regions if d == dest), code.zero)
            out[pl.ds(at * width, width), pl.ds(m * width, width)] = value


SENT = tuple((side, tile) for side in range(2) for tile in range(2))


def sent_regions(side, tile):
    picks = {}
    for at, (dest, source) in enumerate((TO_ABOVE, TO_BELOW)[side][tile]):
        lower = (side == 1) == (tile == 0 and at < 3)
        picks.setdefault((source, lower), []).append((at, dest))
    return picks


def send_choice(code, side, tile, out):
    width = out.shape[1]
    for n, ((source, _), regions) in enumerate(sent_regions(side, tile).items()):
        total = sum(code.pack(dest, source, at) for at, dest in regions)
        out[pl.ds(n * width, width), :] = total.astype(BF)


def all_pairs(*tables):
    return sorted({pair for table in tables for tile in table for pair in tile})


def choices_kernel(ch, step, steps, codes, along, cross, feat, local, *refs):
    outs, near = refs[: -len(PARTS)], refs[-len(PARTS) :]
    place = Place()
    code = step_codes(ch, place, step, steps, codes, along, cross)
    code.rank_all(all_pairs(FROM_ABOVE, FROM_BELOW))
    half = HALO * ch
    width = feat.shape[1]
    for (dests, bottom), mine, out in zip(PARTS, near, outs):
        receive_choice(code, dests, bottom, mine, out)
        shift = half if bottom else 0
        left = [feat[pl.ds(t * BS * ch + shift, half), :] for t in tiles_of(dests, bottom) if isinstance(t, int)]
        got = jnp.dot(jnp.concatenate(left, axis=1), mine[...], preferred_element_type=F32).astype(BF)
        for n, dest in enumerate(dests):
            local[pl.ds((dest * BS + HALO) * ch + shift, half), :] = got[:, n * width : (n + 1) * width]
    if step + 1 < steps:
        code = step_codes(ch, place, step + 1, steps, codes, along, cross)
        code.rank_all(all_pairs(TO_ABOVE, TO_BELOW))
        for item, out in zip(SENT, outs[len(PARTS) :]):
            send_choice(code, *item, out)


def choice_shapes(width):
    near, far = [], []
    for dests, bottom in PARTS:
        tiles = tiles_of(dests, bottom)
        own = sum(isinstance(tile, int) for tile in tiles)
        near.append((own * width, len(dests) * width))
        far.append(((len(tiles) - own) * width, len(dests) * width))
    return near, far, [(len(sent_regions(*item)) * width, width) for item in SENT]


def align(ch, local, recv, aligned, offset, part, choice, only=None):
    dests, bottom = part
    half = HALO * ch
    shift = half if bottom else 0
    width = local.shape[1]
    left = [
        recv[tile[0], pl.ds(tile[1] * half, half), :] for tile in tiles_of(dests, bottom) if not isinstance(tile, int)
    ]
    if only is None:
        right = choice[...]
    else:
        right = choice[:, only * width : (only + 1) * width]
        dests = (dests[only],)
    got = jnp.dot(jnp.concatenate(left, axis=1), right, preferred_element_type=F32)
    for n, d in enumerate(dests):
        near = local[pl.ds((d * BS + HALO) * ch + shift, half), :].astype(F32)
        both = got[:, n * width : (n + 1) * width] + near
        aligned[pl.ds((d * BS + offset) * ch + shift, half), :] = both.astype(BF)


def pack_messages(ch, fout, par, sent, choices, msg_e, msg_o):
    half = HALO * ch
    strip = BS * ch
    width = fout.shape[1]
    for side, near in ((0, 0), (1, QUAD - 1)):
        shift = half if side == 1 else 0
        sent[side, pl.ds(0, half), :] = fout[pl.ds(near * strip + shift, half), :]
    for (side, tile), choice in zip(SENT, choices):
        left = [
            fout[pl.ds(source * strip + (half if lower else 0), half), :] for source, lower in sent_regions(side, tile)
        ]
        got = jnp.dot(jnp.concatenate(left, axis=1), choice[...], preferred_element_type=F32).astype(BF)
        if tile == 0:
            sent[side, pl.ds(half, half), :] = got
        else:
            lane = lax.broadcasted_iota(jnp.int32, (half // 2, width), 1)
            folded = jnp.where(lane < width // 2, got[: half // 2], pltpu.roll(got[half // 2 :], width // 2, 1))
            sent[side, pl.ds(2 * half, half // 2), :] = folded
    msg_e[...] = sent[1 - par]
    msg_o[...] = sent[par]


def unpack_message(ch, message, recv, side):
    half = HALO * ch
    width = message.shape[1]
    recv[side, pl.ds(0, 2 * half), :] = message[pl.ds(0, 2 * half), :]
    folded = message[pl.ds(2 * half, half // 2), :]
    recv[side, pl.ds(2 * half, half // 2), :] = folded
    recv[side, pl.ds(2 * half + half // 2, half // 2), :] = pltpu.roll(folded, width // 2, 1)


class Rows:
    def __init__(self, ch, width, top_ok, bottom_ok, count):
        lane = lax.broadcasted_iota(jnp.int32, (ch, width), 1)
        self.not_first = lane > 0
        self.not_last = lane < width - 1
        self.zero = jnp.zeros((ch, width), BF)
        self.top_ok = top_ok
        self.bottom_ok = bottom_ok
        self.count = count

    def active(self, value, row):
        act = leaky(value)
        if row < 0:
            act = jnp.where(self.top_ok, act, self.zero)
        if row >= self.count:
            act = jnp.where(self.bottom_ok, act, self.zero)
        return (
            jnp.where(self.not_first, pltpu.roll(act, 1, 1), self.zero),
            act,
            jnp.where(self.not_last, pltpu.roll(act, act.shape[1] - 1, 1), self.zero),
        )

    def put(self, buf, here, value, row):
        for n, act in enumerate(self.active(value, row)):
            buf[n, here, :] = act


OFF = 8


def here_of(row, ch, count=1):
    return pl.ds((row + OFF) * ch, count * ch)


def conv_layer(ch, weight, source, held, start, stop, emit):
    width = held.shape[1]
    for first in range(start, stop, 4):
        sides = [
            jnp.concatenate([source[n, here_of(first + 2 * h - 1, ch, 4), :] for n in range(3)], axis=0)
            for h in range(2)
        ]
        out = jnp.dot(weight, jnp.concatenate(sides, axis=1), preferred_element_type=F32)
        for h in range(2):
            for q in range(2):
                row = first + 2 * h + q
                total = held[here_of(row, ch), :].astype(F32)
                total += out[q * ch : (q + 1) * ch, h * width : (h + 1) * width]
                emit(row, total.astype(BF))


def join_first_rows(ch, join_mat, inp):
    width = inp.shape[1]
    mixed = jnp.dot(
        join_mat, jnp.concatenate([inp[: 2 * ch], inp[2 * ch :]], axis=1), preferred_element_type=F32
    ).astype(BF)
    return [mixed[q * ch : (q + 1) * ch, h * width : (h + 1) * width] for h in range(2) for q in range(2)]


def clear_outside(space, ch, rows, bufs):
    for buf in bufs:
        for row in (-HALO - 1, rows + HALO):
            for n in range(3):
                buf[n, here_of(row, ch), :] = space.zero


def conv_layers(ch, conv, space, rows, act_a, act_b, held, fout):
    layers = conv.shape[0]
    source, target = act_a, act_b
    for layer in range(layers):
        need = layers - 1 - layer
        reach = -(-need // 2) * 2
        start, stop = -reach, rows + reach
        if (stop - start) % 4:
            start, stop = -HALO, rows + HALO

        def emit(row, value, layer=layer, target=target):
            if layer < layers - 1:
                held[here_of(row, ch), :] = value
                space.put(target, here_of(row, ch), value, row)
            else:
                fout[pl.ds(row * ch, ch), :] = value

        conv_layer(ch, conv[layer], source, held, start, stop, emit)
        source, target = target, source


def inner_kernel(ch, xq, join, conv, feat, saved, saved_held, act_a, act_b, held):
    rows = QUAD * BS
    layers = conv.shape[0]
    space = Rows(ch, xq.shape[1], True, True, rows)
    for buf in (act_a, act_b):
        for row in (-1, rows):
            for n in range(3):
                buf[n, here_of(row, ch), :] = space.zero
    join_mat = join[...]
    for first in range(0, rows, 4):
        for n, value in enumerate(join_first_rows(ch, join_mat, xq[pl.ds(first * ch, 4 * ch), :])):
            held[here_of(first + n, ch), :] = value
            space.put(act_a, here_of(first + n, ch), value, first + n)
    source, target = act_a, act_b
    for layer in range(layers):
        for side, row, both in ((0, layer, layer), (1, rows - 1 - layer, rows - 2 - layer)):
            for n in range(3):
                saved[layer, side, n] = source[n, here_of(both, ch, 2), :]
            saved_held[layer, side] = held[here_of(row, ch), :]
        edge = (layer + 1) // 2 * 2

        def emit(row, value, layer=layer, target=target):
            if layer < layers - 1:
                held[here_of(row, ch), :] = value
                space.put(target, here_of(row, ch), value, row)
            else:
                feat[pl.ds(row * ch, ch), :] = value

        conv_layer(ch, conv[layer], source, held, edge, rows - edge, emit)
        source, target = target, source


def outer_kernel(ch, steps, *refs):
    feat_in, saved, saved_held, along, cross, join, conv, codes, far_in, *refs = refs
    fout, msg_e, msg_o, far_out, sent, *choices = refs
    half = HALO * ch
    rows = QUAD * BS
    place = Place()
    layers = conv.shape[0]
    width = feat_in.shape[1]
    space = Rows(ch, width, jnp.logical_not(place.top), jnp.logical_not(place.bottom), rows)
    code = step_codes(ch, place, 1, steps, codes, along, cross)
    code.rank_all(all_pairs(TO_ABOVE, TO_BELOW))
    for item, out in zip(SENT, choices):
        send_choice(code, *item, out)
    fout[pl.ds(half, (rows - 2 * HALO) * ch), :] = feat_in[pl.ds(half, (rows - 2 * HALO) * ch), :]
    halos = above_below(place, along[pl.ds(0, half), :], cross[pl.ds(0, half), :])
    join_mat = join[...]
    values = [join_first_rows(ch, join_mat, halo) for halo in halos]
    starts = [-HALO, rows]
    for layer in range(layers):
        weight = conv[layer]
        for side in range(2):
            acts = [space.active(value, starts[side] + n) for n, value in enumerate(values[side])]
            kept = [
                tuple(saved[layer, side, n, pl.ds(m * ch, ch), :] for n in range(3)) for m in range(2)
            ]
            beside = saved_held[layer, side]
            if side == 0:
                window, base = acts + kept, values[side][1:] + [beside]
                starts[side] += 1
            else:
                window, base = kept + acts, [beside] + values[side][:3]
                starts[side] -= 1
            halves = [
                jnp.concatenate([window[2 * h + m][n] for n in range(3) for m in range(4)], axis=0) for h in range(2)
            ]
            out = jnp.dot(weight, jnp.concatenate(halves, axis=1), preferred_element_type=F32)
            values[side] = [
                (
                    base[2 * h + q].astype(F32) + out[q * ch : (q + 1) * ch, h * width : (h + 1) * width]
                ).astype(BF)
                for h in range(2)
                for q in range(2)
            ]
    for side in range(2):
        for n, value in enumerate(values[side]):
            fout[pl.ds((starts[side] + n) * ch, ch), :] = value
    pack_messages(ch, fout, place.odd, sent, choices, msg_e, msg_o)


def step_kernel(ch, step, steps, *refs):
    strip = BS * ch
    half = HALO * ch
    last = step == steps - 1
    refs = list(refs)

    def take(count):
        taken = refs[:count]
        del refs[:count]
        return taken

    xq, halo_e, halo_o, join, conv = take(5)
    feat_e, feat_o = take(2)
    choices = take(len(PARTS) + (0 if last else len(SENT)))
    before, out_a, out_b = take(3)
    backs = take(steps - 1 if last else 0)
    held_back = take(step if step == steps - 2 else 0)
    (local,) = take(1)
    if last:
        (x_inner,) = take(1)
    else:
        next_edges, fout, msg_e, msg_o = take(4)
    own_out, part_out = take(2) if last else (None, None)
    out_f, out_g = take(2)
    take(len(held_back))
    tmp, act_a, act_b, held, sems, aligned, recv = take(7)
    if last:
        (fout,) = take(1)
    else:
        (sent,) = take(1)
    width = xq.shape[-1]
    place = Place()
    par = place.odd
    core = place.core
    quad_rows = QUAD * BS
    rows = 2 * BS if last else quad_rows
    right_side = place.side

    copies = own_copies(strip, step - 1, steps, before, out_f, out_g, sems.at[0])
    for n, back in enumerate(backs):
        copies += back_copies(strip, n, steps, back, out_f, out_g, sems.at[1 + n])
    for n, copy in copies:
        pl.when(core == n)(copy.start)
    halo_at = 5 * half // 2
    if step == 1:
        over, under = above_below(place, halo_e[pl.ds(half, half), :], halo_o[pl.ds(half, half), :])
    else:
        one, two = halo_e[pl.ds(halo_at, half), :].astype(F32), halo_o[pl.ds(halo_at, half), :].astype(F32)
        over = jnp.where(par == 1, one, two).astype(BF)
        under = jnp.where(par == 1, two, one).astype(BF)
    if last:
        inner = x_inner[...].astype(F32)
        over, under = (
            jnp.where(right_side == 0, over.astype(F32), inner).astype(BF),
            jnp.where(right_side == 0, inner, under.astype(F32)).astype(BF),
        )
    unpack_message(ch, feat_e, recv, 1 - par)
    unpack_message(ch, feat_o, recv, par)
    if last:

        @pl.when(right_side == 0)
        def _():
            for n in range(3):
                align(ch, local, recv, aligned, HALO, PARTS[n], choices[n])
            align(ch, local, recv, aligned, HALO, PARTS[3], choices[3], 0)

        @pl.when(right_side == 1)
        def _():
            offset = HALO - 2 * BS
            align(ch, local, recv, aligned, offset, PARTS[2], choices[2], 1)
            for n in range(3, 6):
                align(ch, local, recv, aligned, offset, PARTS[n], choices[n])

    else:
        for n, rows_part in enumerate(PARTS):
            align(ch, local, recv, aligned, HALO, rows_part, choices[n])
        for n in range(2):
            sent[n, pl.ds(halo_at, half), :] = next_edges[n]

    top_ok = jnp.logical_not(place.top)
    bottom_ok = jnp.logical_not(place.bottom)
    if last:
        top_ok = top_ok | (right_side == 1)
        bottom_ok = bottom_ok | (right_side == 0)
    space = Rows(ch, width, top_ok, bottom_ok, rows)
    clear_outside(space, ch, rows, (act_a, act_b))
    join_mat = join[...]
    for g in range((rows + 2 * HALO) // 4):
        first = g * 4 - HALO
        inp = over if first < 0 else under if first >= rows else xq[pl.ds(first * ch, 4 * ch), :]
        al = aligned[pl.ds(g * 4 * ch, 4 * ch), :]
        sides = []
        for h in range(2):
            a, b = 2 * h * ch, (2 * h + 1) * ch
            sides.append(jnp.concatenate([al[a : a + ch], inp[a : a + ch], al[b : b + ch], inp[b : b + ch]], axis=0))
        mixed = jnp.dot(join_mat, jnp.concatenate(sides, axis=1), preferred_element_type=F32).astype(BF)
        for h in range(2):
            for q in range(2):
                row = first + 2 * h + q
                value = mixed[q * ch : (q + 1) * ch, h * width : (h + 1) * width]
                held[here_of(row, ch), :] = value
                space.put(act_a, here_of(row, ch), value, row)

    conv_layers(ch, conv, space, rows, act_a, act_b, held, fout)
    if not last:
        pack_messages(ch, fout, par, sent, choices[-len(SENT) :], msg_e, msg_o)
    else:
        channels_first(fout, pl.multiple_of(core * strip, strip), own_out, tmp, ch)
        channels_first(fout, pl.multiple_of((core ^ 1) * strip, strip), part_out, tmp, ch)
    for n, copy in copies:
        pl.when(core == n)(copy.wait)


def own_copies(strip, step, steps, own, out_f, out_g, sem):
    return [
        (0, pltpu.make_async_copy(own, out_f.at[pl.ds(step * strip, strip)], sem)),
        (1, pltpu.make_async_copy(own, out_g.at[pl.ds((steps - 1 - step) * strip, strip)], sem)),
    ]


def back_copies(strip, step, steps, back, out_f, out_g, sem):
    return [
        (0, pltpu.make_async_copy(back, out_g.at[pl.ds((steps - 1 - step) * strip, strip)], sem)),
        (1, pltpu.make_async_copy(back, out_f.at[pl.ds(step * strip, strip)], sem)),
    ]


def finish_kernel(strip, steps, own, back, out_a, out_b, out_f, out_g, sems):
    core = Place().core
    copies = own_copies(strip, steps - 1, steps, own, out_f, out_g, sems.at[0])
    copies += back_copies(strip, steps - 1, steps, back, out_f, out_g, sems.at[1])
    for n, copy in copies:
        pl.when(core == n)(copy.start)
    for n, copy in copies:
        pl.when(core == n)(copy.wait)


def weights_kernel(conv, join, wide, join_both, join_first):
    core = Place().core
    layers, ch = conv.shape[1], conv.shape[3]
    zero = jnp.zeros((ch, ch), BF)
    for layer in range(layers):
        for dx in range(3):
            taps = [conv[core, layer, 3 * dy + dx] for dy in range(3)]
            for q in range(2):
                line = [zero] * q + taps + [zero] * (1 - q)
                wide[layer, pl.ds(q * ch, ch), pl.ds(dx * 4 * ch, 4 * ch)] = jnp.concatenate(line, axis=1)
    both = join[core]
    none = jnp.zeros_like(both)
    join_both[pl.ds(0, ch), :] = jnp.concatenate([both, none], axis=1)
    join_both[pl.ds(ch, ch), :] = jnp.concatenate([none, both], axis=1)
    enter = both[:, ch:]
    join_first[pl.ds(0, ch), :] = jnp.concatenate([enter, zero], axis=1)
    join_first[pl.ds(ch, ch), :] = jnp.concatenate([zero, enter], axis=1)


VMEM = pl.BlockSpec(memory_space=pltpu.VMEM)
ANY = pl.BlockSpec(memory_space=pl.ANY)
HBM = pl.BlockSpec(memory_space=pltpu.HBM)


def call(kernel, name, args, outs, scratch=(), flops=0, in_any=(), out_any=(), aliases=None, in_hbm=(), free=False):
    args = [pltpu.with_memory_space_constraint(a, pltpu.HBM) if n in in_hbm else a for n, a in enumerate(args)]
    return pl.pallas_call(
        kernel,
        out_shape=[jax.ShapeDtypeStruct(o, BF) for o in outs],
        in_specs=[HBM if n in in_hbm else ANY if n in in_any else VMEM for n in range(len(args))],
        out_specs=[ANY if n in out_any else VMEM for n in range(len(outs))],
        scratch_shapes=list(scratch),
        input_output_aliases=aliases or {},
        compiler_params=pltpu.CompilerParams(vmem_limit_bytes=32 << 20),
        cost_estimate=pl.CostEstimate(
            flops=flops,
            bytes_accessed=0 if free else sum(a.size * a.dtype.itemsize for a in args),
            transcendentals=0,
        ),
        name=name,
    )(*args)


def sooner(value):
    return pl.pallas_call(
        lambda given, out: None,
        out_shape=jax.ShapeDtypeStruct(value.shape, value.dtype),
        in_specs=[ANY],
        out_specs=ANY,
        input_output_aliases={0: 0},
        compiler_params=pltpu.CompilerParams(vmem_limit_bytes=1 << 20),
        cost_estimate=pl.CostEstimate(flops=0, bytes_accessed=2 << 20, transcendentals=0),
        name="sooner",
    )(value)


def pairings(count, idle):
    groups = count // QUAD
    out = []
    for parity in range(2):
        pairs = []
        for i in range(count):
            g = i // QUAD
            other = g + 1 if g % 2 == parity else g - 1
            pairs.append((i, i % QUAD + other * QUAD if 0 <= other < groups else i ^ idle))
        out.append(pairs)
    return out


def edge_pairings(count):
    groups = count // QUAD
    along, cross = [], []
    for i in range(count):
        g, side, core = i // QUAD, i % QUAD // 2, i % 2
        if side == 0:
            along += [(i, i - QUAD)] if g > 0 else []
            cross.append((i, i - QUAD + 2 if g > 0 else i ^ 1))
        else:
            along += [(i, i + QUAD)] if g < groups - 1 else []
            cross.append((i, i + QUAD - 2 if g < groups - 1 else i ^ 1))
    return along, cross


def on_device(frames, motion_forward, motion_backward, join_weight, conv_weight):
    steps, ch, strip_rows, width = frames.shape
    strip = strip_rows * ch
    half = HALO * ch
    crow = 16
    count = lax.axis_size("tiles")
    even, odd = pairings(count, 1)
    along_pairs, cross_pairs = edge_pairings(count)

    def near(k):
        return [(i, i ^ k) for i in range(count)]

    def send(value, pairs):
        return lax.ppermute(value, "tiles", pairs)

    tmp = pltpu.VMEM((strip, width), F32)
    piece = (strip, width)
    rows = QUAD * BS
    messages = [(5 * half // 2, width)] + [(7 * half // 2, width)] * (steps - 2)
    feature = (rows * ch, width)
    whole = (steps * strip, width)
    flat = frames.reshape(steps, strip, width)
    later = ((steps - 1) * strip, width)
    first = (strip + crow, width)
    mine, mine_edge, other, rest = call(
        functools.partial(pack_first_kernel, ch, crow),
        "pack_first",
        (flat, motion_forward, motion_backward),
        [first, (half, width), (strip + crow + half, width), later],
        [
            pltpu.VMEM((2, *piece), BF),
            pltpu.VMEM((2, *motion_forward.shape), jnp.int32),
            tmp,
            pltpu.SemaphoreType.DMA((5 + steps,)),
        ],
        in_hbm=(0, 1, 2),
        out_any=(3,),
    )
    pair, edge, edge_too, rest = call(
        functools.partial(pair_first_kernel, ch, crow),
        "pair_first",
        (mine, mine_edge, send(other, near(1)), rest),
        [(2 * (strip + crow), width), (2 * (half + crow), width), (2 * (half + crow), width), later],
        [tmp],
        in_any=(3,),
        out_any=(3,),
        aliases={3: 3},
    )
    received = send(pair, near(2))
    swapped = send(rest, near(1))
    along = send(edge, along_pairs)
    far_pairs = 2 * (steps - 3) * strip
    pair_near, pair_far, pair_last, edge_too = call(
        functools.partial(pair_kernel, ch),
        "pair_rest",
        (flat, swapped, edge_too),
        [(2 * strip + half, width), (far_pairs + (steps - 2) * half, width), (2 * strip, width), edge.shape],
        [tmp, pltpu.SemaphoreType.DMA((2 * steps,))],
        in_hbm=(0,),
        in_any=(1, 2),
        out_any=(3,),
        aliases={2: 3},
    )
    cross = send(edge_too, cross_pairs)
    layers = conv_weight.shape[1]
    conv, join_both, join_first = call(
        weights_kernel,
        "weights",
        (conv_weight, join_weight),
        [(layers, 2 * ch, 12 * ch), (2 * ch, 4 * ch), (2 * ch, 2 * ch)],
        free=True,
    )
    xq, codes, pair_near = call(
        functools.partial(gather_first_kernel, ch, crow),
        "gather_first",
        (pair, received, conv, pair_near),
        [feature, (QUAD * crow, width), pair_near.shape],
        [tmp],
        in_any=(2, 3),
        out_any=(2,),
        aliases={3: 2},
        free=True,
    )
    received_near = send(pair_near, near(2))
    halo_e, halo_o = along, cross

    wide_act = pltpu.VMEM((3, (rows + 16) * ch, width), BF)
    flops = 2 * (rows + 2 * HALO) * width * ch * ch * 9 * layers
    near_shapes, part_shapes, sent_shapes = choice_shapes(width)
    acts = [wide_act, wide_act, pltpu.VMEM(((rows + 16) * ch, width), BF)]
    inner, saved, saved_held = call(
        functools.partial(inner_kernel, ch),
        "refine_inner",
        (xq, join_first, conv),
        [feature, (layers, 2, 3, 2 * ch, width), (layers, 2, ch, width)],
        acts,
        free=True,
    )
    feat, msg_e, msg_o, pair_far = call(
        functools.partial(outer_kernel, ch, steps),
        "refine_outer",
        (inner, saved, saved_held, along, cross, join_first, conv, codes, pair_far),
        [feature, messages[0], messages[0], pair_far.shape],
        [pltpu.VMEM((2, *messages[0]), BF)] + [pltpu.VMEM(shape, BF) for shape in sent_shapes],
        flops // 4,
        in_any=(8,),
        out_any=(3,),
        aliases={8: 3},
    )
    feat_e, feat_o = sooner(send(msg_e, even)), send(msg_o, odd)
    parts = []
    received_far = send(pair_far, near(2))
    outputs = call(lambda after, a, b: None, "results", (feat,), [whole, whole], in_any=(0,), out_any=(0, 1), free=True)

    def choices_of(step):
        return call(
            functools.partial(choices_kernel, ch, step, steps),
            "choices",
            (codes, along, cross, feat),
            [((rows + 2 * HALO) * ch, width)] + part_shapes + (sent_shapes if step + 1 < steps else []),
            [pltpu.VMEM(shape, BF) for shape in near_shapes],
        )

    def frame_of(step):
        if step == steps - 1:
            kernel = functools.partial(gather_last_kernel, ch, far_pairs + (steps - 3) * half)
            args, outs = (pair_last, received_far, feat), [(2 * strip, width), (half, width)]
        elif step == 1:
            kernel = functools.partial(gather_kernel, ch, 0, 2 * strip)
            args, outs = (pair_near, received_near, feat), [feature, (2, half, width)]
        else:
            kernel = functools.partial(gather_kernel, ch, 2 * (step - 2) * strip, far_pairs + (step - 2) * half)
            args, outs = (pair_far, received_far, feat), [feature, (2, half, width)]
        return call(kernel, "gather", args, outs + [piece, piece], [tmp])

    for step in range(1, steps):
        last = step == steps - 1
        local, *choices = choices_of(step)
        x_now, beside, own, part = frame_of(step)
        parts = parts + [part]
        args = [x_now, halo_e, halo_o, join_both, conv, feat_e, feat_o, *choices, own, *outputs]
        many = len(args)
        outs = [] if last else [feature, messages[step], messages[step]]
        outs += [piece, piece, whole, whole] if last else [whole, whole]
        in_any = [many - 3, many - 2, many - 1]
        out_any = [len(outs) - 2, len(outs) - 1]
        aliases = {many - 2: len(outs) - 2, many - 1: len(outs) - 1}
        if last:
            backs = [send(part, near(1)) for part in parts]
            in_any += range(many, many + len(backs))
            args += backs
        elif step == steps - 2:
            for part in parts:
                aliases[len(args)] = len(outs)
                in_any.append(len(args))
                out_any.append(len(outs))
                args.append(part)
                outs.append(piece)
        args += [local, beside]
        scratch = [tmp, *acts, pltpu.SemaphoreType.DMA((steps,))]
        scratch += [pltpu.VMEM(((rows + 2 * HALO) * ch, width), BF), pltpu.VMEM((2, 3 * half, width), BF)]
        scratch += [pltpu.VMEM((2 * strip, width) if last else (2, *messages[step]), BF)]
        results = call(
            functools.partial(step_kernel, ch, step, steps),
            "refine",
            args,
            outs,
            scratch,
            flops,
            in_any=in_any,
            out_any=out_any,
            aliases=aliases,
        )
        if not last:
            feat, msg_e, msg_o, *results = results
            halo_e, halo_o = feat_e, feat_o = sooner(send(msg_e, even)), send(msg_o, odd)
        if last:
            own, part, *results = results
        out_f, out_g, *passed = results
        outputs = out_f, out_g
        parts = passed or parts
    back = send(part, near(1))

    outputs = call(
        functools.partial(finish_kernel, strip, steps),
        "finish",
        [own, back, *outputs],
        [whole] * 2,
        [pltpu.SemaphoreType.DMA((2,))],
        in_any=(0, 1, 2, 3),
        out_any=(0, 1),
        aliases={2: 0, 3: 1},
    )
    return tuple(o.reshape(frames.shape) for o in outputs)


def solution(mesh):
    return jax.shard_map(
        on_device,
        mesh=mesh,
        in_specs=(
            P(None, None, ("clips", "tiles"), None),
            P(None, ("clips", "tiles")),
            P(None, ("clips", "tiles")),
            P(),
            P(),
        ),
        out_specs=(
            P(None, None, ("clips", "tiles"), None),
            P(None, None, ("clips", "tiles"), None),
        ),
        check_vma=False,
    )
```

```python
import functools

import jax
import jax.numpy as jnp
from jax import lax
from jax.experimental import pallas as pl
from jax.experimental.pallas import tpu as pltpu
from jax.sharding import PartitionSpec as P

BS = 8
REACH = 2
QUAD = 4
HALO = 4
CAPACITY = 4
BF = jnp.bfloat16
F32 = jnp.float32


class Place:
    def __init__(self):
        me = lax.axis_index("tiles")
        self.me = me
        self.strip = me % QUAD
        self.core = me % 2
        self.side = self.strip // 2
        self.group = me // QUAD
        self.odd = self.group % 2
        self.top = self.group == 0
        self.bottom = self.group == lax.axis_size("tiles") // QUAD - 1


def leaky(value):
    widened = value.astype(F32)
    return jnp.maximum(widened, 0.1 * widened).astype(BF)


def rows_first(src, src_start, dst, dst_start, tmp, ch):
    tmp[...] = src[pl.ds(src_start, BS * ch), :].astype(F32)
    for r in range(BS):
        row = tmp[pl.ds(r, ch, stride=BS), :]
        dst[pl.ds(dst_start + r * ch, ch), :] = row.astype(BF)


def channels_first(src, src_start, dst, tmp, ch):
    for r in range(BS):
        tmp[pl.ds(r, ch, stride=BS), :] = src[pl.ds(src_start + r * ch, ch), :].astype(F32)
    dst[...] = tmp[...].astype(BF)


def pack_first_kernel(ch, crow, frames, motion_f, motion_b, mine, mine_edge, other, rest, following, motion_buf, tmp, sems):
    place = Place()
    steps, strip = frames.shape[:2]
    half = HALO * ch
    core = place.core
    outs = (mine, other)
    lists = [
        pltpu.make_async_copy(motion, motion_buf.at[n], sems.at[4 + n]) for n, motion in enumerate((motion_f, motion_b))
    ]
    copies = []
    for n in range(2):
        back = 1 - core if n else core
        copies.append(frame_copy(frames, 0, back, outs[n].at[pl.ds(0, strip)], sems.at[n]))
        copies.append(frame_copy(frames, 1, back, following.at[n], sems.at[2 + n]))
    later = [
        frame_copy(frames, step, 1 - core, rest.at[pl.ds((step - 1) * strip, strip)], sems.at[5 + step])
        for step in range(1, steps)
    ]
    for copy in lists + copies + later:
        copy.start()
    for copy in lists:
        copy.wait()
    blocks = motion_f.shape[1]
    width = mine.shape[1]
    column = lax.broadcasted_iota(jnp.int32, motion_f.shape, 1)
    spread = jnp.where(
        lax.broadcasted_iota(jnp.int32, (blocks, width), 1) // BS
        == lax.broadcasted_iota(jnp.int32, (blocks, width), 0),
        1.0,
        0.0,
    ).astype(BF)
    wides = []
    for n in range(2):
        taken = motion_buf[n]
        across = taken // blocks
        code = (across - place.me + REACH) * (2 * blocks) + (taken - across * blocks - column + blocks - 1)
        wide = jnp.dot(code.astype(BF), spread, preferred_element_type=F32).astype(BF)
        frames_order = range(steps - 1) if n == 0 else range(steps - 2, -1, -1)
        wides += [wide[frame : frame + 1] for frame in frames_order]
    wides.append(jnp.zeros((crow - len(wides), width), BF))
    code = jnp.concatenate(wides, axis=0)
    for out in outs:
        out[pl.ds(strip, crow), :] = code
    for copy in copies:
        copy.wait()
    for n, (out, start) in enumerate(((mine_edge, 0), (other, strip + crow))):
        edge_of(place.side == 0, ch, following[n], out, start, tmp)
    for copy in later:
        copy.wait()


def edge_of(top, ch, strip_values, out, start, tmp):
    tmp[...] = strip_values.astype(F32)
    for r in range(HALO):
        one, two = tmp[pl.ds(r, ch, stride=BS), :], tmp[pl.ds(BS - HALO + r, ch, stride=BS), :]
        out[pl.ds(start + r * ch, ch), :] = jnp.where(top, one, two).astype(BF)


def pair_first_kernel(ch, crow, mine, mine_edge, partner, rest_in, out, edge, edge_too, rest_out, tmp):
    place = Place()
    strip = BS * ch
    half = HALO * ch
    own = place.core == place.side
    first = jnp.where(own, mine[pl.ds(0, strip), :].astype(F32), partner[pl.ds(0, strip), :].astype(F32))
    edge_of(place.side == 0, ch, first, edge, 0, tmp)
    second = partner[pl.ds(strip + crow, half), :].astype(F32)
    edge[pl.ds(half, half), :] = jnp.where(own, mine_edge[...].astype(F32), second).astype(BF)
    for n, piece in enumerate((mine, partner)):
        at = place.core ^ n
        out[pl.ds(pl.multiple_of(at * strip, strip), strip), :] = piece[pl.ds(0, strip), :]
        for ref, start in ((out, 2 * strip), (edge, 2 * half)):
            ref[pl.ds(pl.multiple_of(start + at * crow, crow), crow), :] = piece[pl.ds(strip, crow), :]
    edge_too[...] = edge[...]


def above_below(place, along, cross):
    left = place.side == 0
    along, cross = along.astype(F32), cross.astype(F32)
    return jnp.where(left, cross, along).astype(BF), jnp.where(left, along, cross).astype(BF)


def frame_copy(frames, step, back, out, sem):
    steps = frames.shape[0]
    return pltpu.make_async_copy(frames.at[step + back * (steps - 1 - 2 * step)], out, sem)


def pair_copies(frames, swapped, core, first, count, out, sems):
    strip = frames.shape[1]
    copies = []
    for n in range(count):
        step = first + n
        own = out.at[pl.ds(pl.multiple_of((2 * n + core) * strip, strip), strip)]
        his = out.at[pl.ds(pl.multiple_of((2 * n + 1 - core) * strip, strip), strip)]
        copies.append(frame_copy(frames, step, core, own, sems.at[2 * n]))
        copies.append(
            pltpu.make_async_copy(swapped.at[pl.ds((step - 1) * strip, strip)], his, sems.at[2 * n + 1])
        )
    return copies


def edge_rows(place, ch, pair, outer, out, start, tmp):
    strip = BS * ch
    one, two = pair[pl.ds(0, strip), :].astype(F32), pair[pl.ds(strip, strip), :].astype(F32)
    left = place.side == 0
    if outer:
        edge_of(left, ch, jnp.where(left, one, two), out, start, tmp)
    else:
        edge_of(jnp.logical_not(left), ch, jnp.where(left, two, one), out, start, tmp)


def pair_kernel(ch, frames, swapped, edge_in, near_out, far_out, last_out, edge_out, tmp, sems):
    place = Place()
    steps, strip = frames.shape[:2]
    half = HALO * ch
    between = range(2, steps - 1)
    pairs = {1: near_out.at[pl.ds(0, 2 * strip)], steps - 1: last_out}
    for n, step in enumerate(between):
        pairs[step] = far_out.at[pl.ds(2 * n * strip, 2 * strip)]
    copies = []
    for step, out in pairs.items():
        copies += pair_copies(frames, swapped, place.core, step, 1, out, sems.at[pl.ds(2 * step, 2)])
    for copy in copies:
        copy.start()
    for copy in copies:
        copy.wait()
    edge_rows(place, ch, pairs[2], True, near_out, 2 * strip, tmp)
    at = 2 * len(between) * strip
    for step in range(3, steps):
        edge_rows(place, ch, pairs[step], True, far_out, at, tmp)
        at += half
    edge_rows(place, ch, last_out, False, far_out, at, tmp)


def gather_first_kernel(ch, crow, pair, received, conv, near_in, xq, codes, near_out, tmp):
    place = Place()
    strip = BS * ch
    for n, piece in enumerate((pair, received)):
        side = place.side ^ n
        for m in range(2):
            at = side * 2 + m
            rows_first(piece, m * strip, xq, pl.multiple_of(at * strip, strip), tmp, ch)
            code_at = pl.multiple_of(at * crow, crow)
            codes[pl.ds(code_at, crow), :] = piece[pl.ds(2 * strip + m * crow, crow), :]


def gather_kernel(ch, pair_at, edge_at, pair, received, after, xq, edges, tmp):
    strip = BS * ch
    half = HALO * ch
    side = Place().side
    for n, piece in enumerate((pair, received)):
        for m in range(2):
            start = ((side + n) % 2 * 2 + m) * strip
            rows_first(piece, pair_at + m * strip, xq, pl.multiple_of(start, strip), tmp, ch)
        edges[side ^ n] = piece[pl.ds(edge_at, half), :]


def split_results(ch, feat, own_out, part_out, tmp):
    strip = BS * ch
    own = Place().strip
    channels_first(feat, pl.multiple_of(own * strip, strip), own_out, tmp, ch)
    channels_first(feat, pl.multiple_of((own ^ 1) * strip, strip), part_out, tmp, ch)


def gather_last_kernel(ch, inner_at, pair, received, after, xq, inner, tmp):
    strip = BS * ch
    for m in range(2):
        rows_first(pair, m * strip, xq, m * strip, tmp, ch)
    inner[...] = received[pl.ds(inner_at, HALO * ch), :]


class Codes:
    def __init__(self, rows):
        width = rows[0].shape[1]
        self.rows = rows
        self.blocks = width // BS
        k_id = lax.broadcasted_iota(jnp.int32, (width, width), 0)
        l_id = lax.broadcasted_iota(jnp.int32, (width, width), 1)
        base = (k_id // BS - l_id // BS + self.blocks - 1).astype(F32)
        self.base = jnp.where(k_id % BS == l_id % BS, base, -1.0e4)
        self.slot = k_id.astype(F32)
        self.before = jnp.where((k_id % BS == 0) & (k_id // BS < l_id // BS), 1.0, 0.0).astype(BF)
        self.lane = (lax.broadcasted_iota(jnp.int32, (1, width), 1) % BS).astype(F32)
        self.zero = jnp.zeros((width, width), BF)
        self.ranks = {}

    def plain(self, dest, source):
        ds = source - dest
        if abs(ds) > REACH:
            return self.zero
        shift = float((ds + REACH) * 2 * self.blocks)
        return jnp.where(self.rows[dest + 2] - shift == self.base, 1.0, 0.0).astype(BF)

    def rank_all(self, wanted):
        rows = []
        for dest, source in wanted:
            low = float((source - dest + REACH) * 2 * self.blocks)
            code = self.rows[dest + 2]
            rows.append(jnp.where((code >= low) & (code < low + 2 * self.blocks), 1.0, 0.0))
        count = len(rows)
        rows += [rows[0]] * (-count % 16)
        stacked = jnp.concatenate(rows, axis=0)
        before = jnp.dot(stacked.astype(BF), self.before, preferred_element_type=F32)
        for n, key in enumerate(wanted):
            self.ranks[key] = jnp.where(
                stacked[n : n + 1] > 0, before[n : n + 1] * BS + self.lane, -1.0e4
            )

    def packed(self, dest, source, region):
        at = self.ranks[dest, source] + float(region * CAPACITY * BS)
        return jnp.where(self.slot == at, 1.0, 0.0).astype(BF)

    def pack(self, dest, source, region):
        return lax.dot_general(
            self.plain(dest, source),
            self.packed(dest, source, region),
            (((1,), (1,)), ((), ())),
            preferred_element_type=F32,
        )


FROM_ABOVE = ((0, -1), (0, -2), (1, -1))
FROM_BELOW = ((QUAD - 1, QUAD), (QUAD - 1, QUAD + 1), (QUAD - 2, QUAD))
TO_BELOW = tuple((d + QUAD, s + QUAD) for d, s in FROM_ABOVE)
TO_ABOVE = tuple((d - QUAD, s - QUAD) for d, s in FROM_BELOW)
TAKEN = (FROM_ABOVE, FROM_BELOW)
GIVEN = (TO_ABOVE, TO_BELOW)
REGIONS = len(FROM_ABOVE)


def step_codes(ch, place, step, steps, codes, along, cross):
    crow = codes.shape[0] // QUAD
    width = codes.shape[1]
    pick = place.core * (steps - 1) + step - 1
    row_id = lax.broadcasted_iota(jnp.int32, (crow, width), 0)
    start = 2 * HALO * ch
    above, below = above_below(
        place, along[pl.ds(start, 2 * crow), :], cross[pl.ds(start, 2 * crow), :]
    )

    def row(block):
        return jnp.sum(jnp.where(row_id == pick, block.astype(F32), 0.0), axis=0, keepdims=True)

    rows = [row(above[n * crow : (n + 1) * crow]) for n in range(2)]
    rows += [row(codes[pl.ds(strip * crow, crow), :]) for strip in range(QUAD)]
    rows += [row(below[n * crow : (n + 1) * crow]) for n in range(2)]
    return Codes(rows)


def own_sources(dest):
    return [source for source in range(QUAD) if abs(source - dest) <= REACH]


def choices_kernel(ch, step, steps, codes, along, cross, feat, local, own_out, part_out, *refs):
    place = Place()
    code = step_codes(ch, place, step, steps, codes, along, cross)
    code.rank_all(FROM_ABOVE + FROM_BELOW)
    half = HALO * ch
    strip = BS * ch
    width = feat.shape[1]
    for pair in range(0, QUAD, 2):
        left = [feat[pl.ds(source * strip, strip), :] for source in range(QUAD)]
        right = [
            jnp.concatenate([code.plain(pair + m, source) for m in range(2)], axis=1) for source in range(QUAD)
        ]
        got = jnp.dot(
            jnp.concatenate(left, axis=1), jnp.concatenate(right, axis=0), preferred_element_type=F32
        ).astype(BF)
        for m in range(2):
            local[pl.ds(half + (pair + m) * strip, strip), :] = got[:, m * width : (m + 1) * width]
    for dest, shift, at in ((-1, half, 0), (QUAD, 0, half + QUAD * strip)):
        sources = own_sources(dest)
        left = [feat[pl.ds(source * strip + shift, half), :] for source in sources]
        right = [code.plain(dest, source) for source in sources]
        local[pl.ds(at, half), :] = jnp.dot(
            jnp.concatenate(left, axis=1), jnp.concatenate(right, axis=0), preferred_element_type=F32
        ).astype(BF)
    for side in range(2):
        for m in range(2):
            value = [
                code.packed(dest, source, n) for n, (dest, source) in enumerate(TAKEN[side]) if dest == 2 * side + m
            ]
            refs[side][:, pl.ds(m * width, width)] = sum(value[1:], value[0])
    if step + 1 < steps:
        send_choices(code_of_next(ch, place, step, steps, codes, along, cross), refs[2:-1])
    split_results(ch, feat, own_out, part_out, refs[-1])


def code_of_next(ch, place, step, steps, codes, along, cross):
    code = step_codes(ch, place, step + 1, steps, codes, along, cross)
    code.rank_all(TO_ABOVE + TO_BELOW)
    return code


def given_sources(side):
    return sorted({source for _, source in GIVEN[side]})


def send_choices(code, outs):
    width = code.zero.shape[0]
    for side in range(2):
        blocks, edge = outs[2 * side : 2 * side + 2]
        for n, source in enumerate(given_sources(side)):
            total = sum(code.pack(d, source, at) for at, (d, origin) in enumerate(GIVEN[side]) if origin == source)
            blocks[pl.ds(n * width, width), :] = total.astype(BF)
        dest = side * (QUAD - 1)
        for n, source in enumerate(own_sources(dest)):
            edge[pl.ds(n * width, width), :] = code.plain(dest, source)


def choice_shapes(width):
    sent = []
    for side in range(2):
        sent += [(len(given_sources(side)) * width, width), (len(own_sources(side * (QUAD - 1))) * width, width)]
    return [(width, 2 * width)] * 2, sent


def join_rows(ch, join_mat, al, inp, extra=None):
    width = al.shape[1]
    sides = []
    for h in range(2):
        a, b = 2 * h * ch, (2 * h + 1) * ch
        sides.append(jnp.concatenate([al[a : a + ch], inp[a : a + ch], al[b : b + ch], inp[b : b + ch]], axis=0))
    mixed = jnp.dot(join_mat, jnp.concatenate(sides, axis=1), preferred_element_type=F32)
    rows = [mixed[q * ch : (q + 1) * ch, h * width : (h + 1) * width] for h in range(2) for q in range(2)]
    if extra is not None:
        rows = [row + extra[n * ch : (n + 1) * ch].astype(F32) for n, row in enumerate(rows)]
    return [row.astype(BF) for row in rows]


def fold_rows(ch):
    return BS * ch * REGIONS // (REGIONS + 1)


def pack_messages(ch, fout, par, join_mat, choices, inputs, sent, msg_e, msg_o):
    half = HALO * ch
    strip = BS * ch
    width = fout.shape[1]
    fold = fold_rows(ch)
    piece = strip - fold
    group = width // (REGIONS + 1)
    lane = lax.broadcasted_iota(jnp.int32, (piece, width), 1)
    for side in range(2):
        blocks, edge = choices[2 * side : 2 * side + 2]
        left = [fout[pl.ds(source * strip, strip), :] for source in given_sources(side)]
        got = jnp.dot(jnp.concatenate(left, axis=1), blocks[...], preferred_element_type=F32).astype(BF)
        for n in range(REGIONS):
            rolled = pltpu.roll(got[fold:], (REGIONS - n) * group, 1)
            sent[side, pl.ds(n * piece, piece), :] = jnp.where(
                lane < REGIONS * group, got[n * piece : (n + 1) * piece], rolled
            )
        shift = side * half
        left = [fout[pl.ds(source * strip + shift, half), :] for source in own_sources(side * (QUAD - 1))]
        al = jnp.dot(jnp.concatenate(left, axis=1), edge[...], preferred_element_type=F32).astype(BF)
        inp = jnp.zeros((half, width), BF) if inputs is None else inputs[side]
        for n, row in enumerate(join_rows(ch, join_mat, al, inp)):
            sent[side, pl.ds(fold + n * ch, ch), :] = row
    msg_e[...] = sent[1 - par]
    msg_o[...] = sent[par]


def unpack_message(ch, message, recv, side):
    strip = BS * ch
    width = message.shape[1]
    fold = fold_rows(ch)
    piece = strip - fold
    group = width // (REGIONS + 1)
    lane = lax.broadcasted_iota(jnp.int32, (piece, width), 1)
    recv[side, pl.ds(0, fold), :] = message[pl.ds(0, fold), :]
    total = None
    for n in range(REGIONS):
        rolled = pltpu.roll(message[pl.ds(n * piece, piece), :], (n + 1) * group, 1)
        total = rolled if total is None else jnp.where(lane < n * group, total, rolled)
    recv[side, pl.ds(fold, piece), :] = total


class Rows:
    def __init__(self, ch, width, top_ok, bottom_ok, count):
        lane = lax.broadcasted_iota(jnp.int32, (ch, width), 1)
        self.not_first = lane > 0
        self.not_last = lane < width - 1
        self.zero = jnp.zeros((ch, width), BF)
        self.top_ok = top_ok
        self.bottom_ok = bottom_ok
        self.count = count

    def active(self, value, row):
        act = leaky(value)
        if row < 0:
            act = jnp.where(self.top_ok, act, self.zero)
        if row >= self.count:
            act = jnp.where(self.bottom_ok, act, self.zero)
        return (
            jnp.where(self.not_first, pltpu.roll(act, 1, 1), self.zero),
            act,
            jnp.where(self.not_last, pltpu.roll(act, act.shape[1] - 1, 1), self.zero),
        )

    def put(self, buf, here, value, row):
        for n, act in enumerate(self.active(value, row)):
            buf[n, here, :] = act


OFF = 8


def here_of(row, ch, count=1):
    return pl.ds((row + OFF) * ch, count * ch)


def conv_layer(ch, weight, source, held, start, stop, emit):
    width = held.shape[1]
    for first in range(start, stop, 4):
        sides = [
            jnp.concatenate([source[n, here_of(first + 2 * h - 1, ch, 4), :] for n in range(3)], axis=0)
            for h in range(2)
        ]
        out = jnp.dot(weight, jnp.concatenate(sides, axis=1), preferred_element_type=F32)
        for h in range(2):
            for q in range(2):
                row = first + 2 * h + q
                total = held[here_of(row, ch), :].astype(F32)
                total += out[q * ch : (q + 1) * ch, h * width : (h + 1) * width]
                emit(row, total.astype(BF))


def join_first_rows(ch, join_mat, inp):
    width = inp.shape[1]
    mixed = jnp.dot(
        join_mat, jnp.concatenate([inp[: 2 * ch], inp[2 * ch :]], axis=1), preferred_element_type=F32
    ).astype(BF)
    return [mixed[q * ch : (q + 1) * ch, h * width : (h + 1) * width] for h in range(2) for q in range(2)]


def clear_outside(space, ch, rows, bufs):
    for buf in bufs:
        for row in (-HALO - 1, rows + HALO):
            for n in range(3):
                buf[n, here_of(row, ch), :] = space.zero


def conv_layers(ch, conv, space, rows, act_a, act_b, held, fout):
    layers = conv.shape[0]
    source, target = act_a, act_b
    for layer in range(layers):
        need = layers - 1 - layer
        reach = -(-need // 2) * 2
        start, stop = -reach, rows + reach
        if (stop - start) % 4:
            start, stop = -HALO, rows + HALO

        def emit(row, value, layer=layer, target=target):
            if layer < layers - 1:
                held[here_of(row, ch), :] = value
                space.put(target, here_of(row, ch), value, row)
            else:
                fout[pl.ds(row * ch, ch), :] = value

        conv_layer(ch, conv[layer], source, held, start, stop, emit)
        source, target = target, source


def inner_kernel(ch, xq, join, conv, feat, saved, saved_held, act_a, act_b, held):
    rows = QUAD * BS
    layers = conv.shape[0]
    space = Rows(ch, xq.shape[1], True, True, rows)
    for buf in (act_a, act_b):
        for row in (-1, rows):
            for n in range(3):
                buf[n, here_of(row, ch), :] = space.zero
    join_mat = join[...]
    for first in range(0, rows, 4):
        for n, value in enumerate(join_first_rows(ch, join_mat, xq[pl.ds(first * ch, 4 * ch), :])):
            held[here_of(first + n, ch), :] = value
            space.put(act_a, here_of(first + n, ch), value, first + n)
    source, target = act_a, act_b
    for layer in range(layers):
        for side, row, both in ((0, layer, layer), (1, rows - 1 - layer, rows - 2 - layer)):
            for n in range(3):
                saved[layer, side, n] = source[n, here_of(both, ch, 2), :]
            saved_held[layer, side] = held[here_of(row, ch), :]
        edge = (layer + 1) // 2 * 2

        def emit(row, value, layer=layer, target=target):
            if layer < layers - 1:
                held[here_of(row, ch), :] = value
                space.put(target, here_of(row, ch), value, row)
            else:
                feat[pl.ds(row * ch, ch), :] = value

        conv_layer(ch, conv[layer], source, held, edge, rows - edge, emit)
        source, target = target, source


def outer_kernel(ch, steps, *refs):
    feat_in, saved, saved_held, along, cross, join, join_both, conv, codes, far_in, *refs = refs
    fout, msg_e, msg_o, far_out, sent, *choices = refs
    half = HALO * ch
    rows = QUAD * BS
    place = Place()
    layers = conv.shape[0]
    width = feat_in.shape[1]
    space = Rows(ch, width, jnp.logical_not(place.top), jnp.logical_not(place.bottom), rows)
    send_choices(code_of_next(ch, place, 0, steps, codes, along, cross), choices)
    fout[pl.ds(half, (rows - 2 * HALO) * ch), :] = feat_in[pl.ds(half, (rows - 2 * HALO) * ch), :]
    halos = above_below(place, along[pl.ds(0, half), :], cross[pl.ds(0, half), :])
    join_mat = join[...]
    values = [join_first_rows(ch, join_mat, halo) for halo in halos]
    starts = [-HALO, rows]
    for layer in range(layers):
        weight = conv[layer]
        for side in range(2):
            acts = [space.active(value, starts[side] + n) for n, value in enumerate(values[side])]
            kept = [
                tuple(saved[layer, side, n, pl.ds(m * ch, ch), :] for n in range(3)) for m in range(2)
            ]
            beside = saved_held[layer, side]
            if side == 0:
                window, base = acts + kept, values[side][1:] + [beside]
                starts[side] += 1
            else:
                window, base = kept + acts, [beside] + values[side][:3]
                starts[side] -= 1
            halves = [
                jnp.concatenate([window[2 * h + m][n] for n in range(3) for m in range(4)], axis=0) for h in range(2)
            ]
            out = jnp.dot(weight, jnp.concatenate(halves, axis=1), preferred_element_type=F32)
            values[side] = [
                (
                    base[2 * h + q].astype(F32) + out[q * ch : (q + 1) * ch, h * width : (h + 1) * width]
                ).astype(BF)
                for h in range(2)
                for q in range(2)
            ]
    for side in range(2):
        for n, value in enumerate(values[side]):
            fout[pl.ds((starts[side] + n) * ch, ch), :] = value
    pack_messages(ch, fout, place.odd, join_both[...], choices, None, sent, msg_e, msg_o)


def step_kernel(ch, step, steps, *refs):
    strip = BS * ch
    half = HALO * ch
    last = step == steps - 1
    refs = list(refs)

    def take(count):
        taken = refs[:count]
        del refs[:count]
        return taken

    xq, along, cross, join, conv = take(5)
    feat_e, feat_o = take(2)
    choices = take(2 if last else 6)
    before, out_a, out_b = take(3)
    (local,) = take(1)
    if last:
        (x_inner,) = take(1)
    else:
        next_edges, fout, msg_e, msg_o = take(4)
    own_out, part_out = take(2) if last else (None, None)
    out_f, out_g = take(2)
    tmp, act_a, act_b, held, sems, aligned, recv = take(7)
    if last:
        (fout,) = take(1)
    else:
        (sent,) = take(1)
    width = xq.shape[-1]
    place = Place()
    par = place.odd
    core = place.core
    rows = 2 * BS if last else QUAD * BS
    left_side = place.side == 0

    copies = own_copies(strip, step - 1, steps, before, out_f, out_g, sems.at[0])
    for n, copy in copies:
        pl.when(core == n)(copy.start)

    def choose(which, one, two):
        return jnp.where(which, one.astype(F32), two.astype(F32)).astype(BF)

    fold = fold_rows(ch)
    zero = jnp.zeros((half, width), BF)
    one, two = feat_e[pl.ds(fold, half), :], feat_o[pl.ds(fold, half), :]
    over_sent, under_sent = choose(par == 1, one, two), choose(par == 1, two, one)
    over, under = zero, zero
    if step == 1:
        over, under = above_below(place, along[pl.ds(half, half), :], cross[pl.ds(half, half), :])
    if last:
        inner = x_inner[...]
        over, under = choose(left_side, zero, inner), choose(left_side, inner, zero)
        over_sent, under_sent = choose(left_side, over_sent, zero), choose(left_side, zero, under_sent)
    unpack_message(ch, feat_e, recv, 1 - par)
    unpack_message(ch, feat_o, recv, par)
    for edge in (0, half + QUAD * strip):
        aligned[pl.ds(edge, half), :] = local[pl.ds(edge, half), :]
    for side in range(2):
        got = jnp.dot(recv[side], choices[side][...], preferred_element_type=F32)
        for m in range(2):
            here = pl.ds(half + (2 * side + m) * strip, strip)
            both = got[:, m * width : (m + 1) * width] + local[here, :].astype(F32)
            aligned[here, :] = both.astype(BF)

    space = Rows(ch, width, jnp.logical_not(place.top), jnp.logical_not(place.bottom), rows)
    if last:
        space.top_ok = space.top_ok | (place.side == 1)
        space.bottom_ok = space.bottom_ok | left_side
    clear_outside(space, ch, rows, (act_a, act_b))
    join_mat = join[...]
    for first in range(-HALO, rows + HALO, 4):
        inp, extra = xq, None
        if first < 0:
            inp, extra = over, over_sent
        elif first >= rows:
            inp, extra = under, under_sent
        else:
            inp = xq[pl.ds(first * ch, 4 * ch), :]
        at = (first + HALO) * ch
        if last:
            at = pl.multiple_of(place.side * (2 * strip) + at, half)
        al = aligned[pl.ds(at, half), :]
        for n, value in enumerate(join_rows(ch, join_mat, al, inp, extra)):
            held[here_of(first + n, ch), :] = value
            space.put(act_a, here_of(first + n, ch), value, first + n)

    conv_layers(ch, conv, space, rows, act_a, act_b, held, fout)
    if not last:
        pack_messages(ch, fout, par, join_mat, choices[2:], next_edges, sent, msg_e, msg_o)
    else:
        channels_first(fout, pl.multiple_of(core * strip, strip), own_out, tmp, ch)
        channels_first(fout, pl.multiple_of((core ^ 1) * strip, strip), part_out, tmp, ch)
    for n, copy in copies:
        pl.when(core == n)(copy.wait)


def parts_kernel(*refs):
    out = refs[-1]
    strip = refs[0].shape[0]
    for n in range(out.shape[0] // strip):
        out[pl.ds(n * strip, strip), :] = refs[n][...]


def own_copies(strip, step, steps, own, out_f, out_g, sem):
    return [
        (0, pltpu.make_async_copy(own, out_f.at[pl.ds(step * strip, strip)], sem)),
        (1, pltpu.make_async_copy(own, out_g.at[pl.ds((steps - 1 - step) * strip, strip)], sem)),
    ]


def back_copies(strip, step, steps, back, out_f, out_g, sem):
    return [
        (0, pltpu.make_async_copy(back, out_g.at[pl.ds((steps - 1 - step) * strip, strip)], sem)),
        (1, pltpu.make_async_copy(back, out_f.at[pl.ds(step * strip, strip)], sem)),
    ]


def run_copies(copies):
    core = Place().core
    for n, copy in copies:
        pl.when(core == n)(copy.start)
    for n, copy in copies:
        pl.when(core == n)(copy.wait)


def finish_own_kernel(strip, steps, own, backs, out_a, out_b, out_f, out_g, sems):
    copies = own_copies(strip, steps - 1, steps, own, out_f, out_g, sems.at[0])
    for step in range(steps - 1):
        before = backs.at[pl.ds(step * strip, strip)]
        copies += back_copies(strip, step, steps, before, out_f, out_g, sems.at[1 + step])
    run_copies(copies)


def finish_kernel(strip, steps, back, out_a, out_b, out_f, out_g, sem):
    run_copies(back_copies(strip, steps - 1, steps, back, out_f, out_g, sem))


def weights_kernel(conv, join, wide, join_both, join_first):
    core = Place().core
    layers, ch = conv.shape[1], conv.shape[3]
    zero = jnp.zeros((ch, ch), BF)
    for layer in range(layers):
        for dx in range(3):
            taps = [conv[core, layer, 3 * dy + dx] for dy in range(3)]
            for q in range(2):
                line = [zero] * q + taps + [zero] * (1 - q)
                wide[layer, pl.ds(q * ch, ch), pl.ds(dx * 4 * ch, 4 * ch)] = jnp.concatenate(line, axis=1)
    both = join[core]
    none = jnp.zeros_like(both)
    join_both[pl.ds(0, ch), :] = jnp.concatenate([both, none], axis=1)
    join_both[pl.ds(ch, ch), :] = jnp.concatenate([none, both], axis=1)
    enter = both[:, ch:]
    join_first[pl.ds(0, ch), :] = jnp.concatenate([enter, zero], axis=1)
    join_first[pl.ds(ch, ch), :] = jnp.concatenate([zero, enter], axis=1)


VMEM = pl.BlockSpec(memory_space=pltpu.VMEM)
ANY = pl.BlockSpec(memory_space=pl.ANY)
HBM = pl.BlockSpec(memory_space=pltpu.HBM)


def call(kernel, name, args, outs, scratch=(), flops=0, in_any=(), out_any=(), aliases=None, in_hbm=(), free=False):
    args = [pltpu.with_memory_space_constraint(a, pltpu.HBM) if n in in_hbm else a for n, a in enumerate(args)]
    return pl.pallas_call(
        kernel,
        out_shape=[jax.ShapeDtypeStruct(o, BF) for o in outs],
        in_specs=[HBM if n in in_hbm else ANY if n in in_any else VMEM for n in range(len(args))],
        out_specs=[ANY if n in out_any else VMEM for n in range(len(outs))],
        scratch_shapes=list(scratch),
        input_output_aliases=aliases or {},
        compiler_params=pltpu.CompilerParams(vmem_limit_bytes=32 << 20),
        cost_estimate=pl.CostEstimate(
            flops=flops,
            bytes_accessed=0 if free else sum(a.size * a.dtype.itemsize for a in args),
            transcendentals=0,
        ),
        name=name,
    )(*args)


def sooner(value, *after):
    return pl.pallas_call(
        lambda *refs: None,
        out_shape=jax.ShapeDtypeStruct(value.shape, value.dtype),
        in_specs=[ANY] * (1 + len(after)),
        out_specs=ANY,
        input_output_aliases={0: 0},
        compiler_params=pltpu.CompilerParams(vmem_limit_bytes=1 << 20),
        cost_estimate=pl.CostEstimate(flops=0, bytes_accessed=2 << 20, transcendentals=0),
        name="sooner",
    )(value, *after)


def pairings(count, idle):
    groups = count // QUAD
    out = []
    for parity in range(2):
        pairs = []
        for i in range(count):
            g = i // QUAD
            other = g + 1 if g % 2 == parity else g - 1
            pairs.append((i, i % QUAD + other * QUAD if 0 <= other < groups else i ^ idle))
        out.append(pairs)
    return out


def edge_pairings(count):
    groups = count // QUAD
    along, cross = [], []
    for i in range(count):
        g, side, core = i // QUAD, i % QUAD // 2, i % 2
        if side == 0:
            along += [(i, i - QUAD)] if g > 0 else []
            cross.append((i, i - QUAD + 2 if g > 0 else i ^ 1))
        else:
            along += [(i, i + QUAD)] if g < groups - 1 else []
            cross.append((i, i + QUAD - 2 if g < groups - 1 else i ^ 1))
    return along, cross


def on_device(frames, motion_forward, motion_backward, join_weight, conv_weight):
    steps, ch, strip_rows, width = frames.shape
    strip = strip_rows * ch
    half = HALO * ch
    crow = 16
    count = lax.axis_size("tiles")
    even, odd = pairings(count, 1)
    along_pairs, cross_pairs = edge_pairings(count)

    def near(k):
        return [(i, i ^ k) for i in range(count)]

    def send(value, pairs):
        return lax.ppermute(value, "tiles", pairs)

    tmp = pltpu.VMEM((strip, width), F32)
    piece = (strip, width)
    rows = QUAD * BS
    message = (fold_rows(ch) + half, width)
    feature = (rows * ch, width)
    whole = (steps * strip, width)
    flat = frames.reshape(steps, strip, width)
    later = ((steps - 1) * strip, width)
    first = (strip + crow, width)
    mine, mine_edge, other, rest = call(
        functools.partial(pack_first_kernel, ch, crow),
        "pack_first",
        (flat, motion_forward, motion_backward),
        [first, (half, width), (strip + crow + half, width), later],
        [
            pltpu.VMEM((2, *piece), BF),
            pltpu.VMEM((2, *motion_forward.shape), jnp.int32),
            tmp,
            pltpu.SemaphoreType.DMA((5 + steps,)),
        ],
        in_hbm=(0, 1, 2),
        out_any=(3,),
    )
    pair, edge, edge_too, rest = call(
        functools.partial(pair_first_kernel, ch, crow),
        "pair_first",
        (mine, mine_edge, send(other, near(1)), rest),
        [(2 * (strip + crow), width), (2 * (half + crow), width), (2 * (half + crow), width), later],
        [tmp],
        in_any=(3,),
        out_any=(3,),
        aliases={3: 3},
    )
    received = send(pair, near(2))
    swapped = send(rest, near(1))
    along = send(edge, along_pairs)
    far_pairs = 2 * (steps - 3) * strip
    pair_near, pair_far, pair_last, edge_too = call(
        functools.partial(pair_kernel, ch),
        "pair_rest",
        (flat, swapped, edge_too),
        [(2 * strip + half, width), (far_pairs + (steps - 2) * half, width), (2 * strip, width), edge.shape],
        [tmp, pltpu.SemaphoreType.DMA((2 * steps,))],
        in_hbm=(0,),
        in_any=(1, 2),
        out_any=(3,),
        aliases={2: 3},
    )
    cross = send(edge_too, cross_pairs)
    layers = conv_weight.shape[1]
    conv, join_both, join_first = call(
        weights_kernel,
        "weights",
        (conv_weight, join_weight),
        [(layers, 2 * ch, 12 * ch), (2 * ch, 4 * ch), (2 * ch, 2 * ch)],
        free=True,
    )
    xq, codes, pair_near = call(
        functools.partial(gather_first_kernel, ch, crow),
        "gather_first",
        (pair, received, conv, pair_near),
        [feature, (QUAD * crow, width), pair_near.shape],
        [tmp],
        in_any=(2, 3),
        out_any=(2,),
        aliases={3: 2},
        free=True,
    )
    received_near = send(pair_near, near(2))

    wide_act = pltpu.VMEM((3, (rows + 16) * ch, width), BF)
    flops = 2 * (rows + 2 * HALO) * width * ch * ch * 9 * layers
    part_shapes, sent_shapes = choice_shapes(width)
    acts = [wide_act, wide_act, pltpu.VMEM(((rows + 16) * ch, width), BF)]
    inner, saved, saved_held = call(
        functools.partial(inner_kernel, ch),
        "refine_inner",
        (xq, join_first, conv),
        [feature, (layers, 2, 3, 2 * ch, width), (layers, 2, ch, width)],
        acts,
        free=True,
    )
    feat, msg_e, msg_o, pair_far = call(
        functools.partial(outer_kernel, ch, steps),
        "refine_outer",
        (inner, saved, saved_held, along, cross, join_first, join_both, conv, codes, pair_far),
        [feature, message, message, pair_far.shape],
        [pltpu.VMEM((2, *message), BF)] + [pltpu.VMEM(shape, BF) for shape in sent_shapes],
        flops // 4,
        in_any=(9,),
        out_any=(3,),
        aliases={9: 3},
    )
    feat_e, feat_o = send(msg_e, even), send(msg_o, odd)
    parts = []
    received_far = send(pair_far, near(2))
    outputs = call(lambda after, a, b: None, "results", (feat,), [whole, whole], in_any=(0,), out_any=(0, 1), free=True)

    def choices_of(step):
        return call(
            functools.partial(choices_kernel, ch, step, steps),
            "choices",
            (codes, along, cross, feat),
            [((rows + 2 * HALO) * ch, width), piece, piece] + part_shapes + (sent_shapes if step + 1 < steps else []),
            [tmp],
        )

    def frame_of(step):
        if step == steps - 1:
            kernel = functools.partial(gather_last_kernel, ch, far_pairs + (steps - 3) * half)
            args, outs = (pair_last, received_far, feat), [(2 * strip, width), (half, width)]
        elif step == 1:
            kernel = functools.partial(gather_kernel, ch, 0, 2 * strip)
            args, outs = (pair_near, received_near, feat), [feature, (2, half, width)]
        else:
            kernel = functools.partial(gather_kernel, ch, 2 * (step - 2) * strip, far_pairs + (step - 2) * half)
            args, outs = (pair_far, received_far, feat), [feature, (2, half, width)]
        return call(kernel, "gather", args, outs, [tmp], in_any=(2,))

    for step in range(1, steps):
        last = step == steps - 1
        local, own, part, *choices = choices_of(step)
        x_now, beside = frame_of(step)
        feat_e = sooner(feat_e, x_now) if step > 1 else sooner(feat_e)
        parts = parts + [part]
        args = [x_now, along, cross, join_both, conv, feat_e, feat_o, *choices, own, *outputs]
        many = len(args)
        outs = [] if last else [feature, message, message]
        outs += [piece, piece, whole, whole] if last else [whole, whole]
        in_any = [many - 3, many - 2, many - 1]
        out_any = [len(outs) - 2, len(outs) - 1]
        aliases = {many - 2: len(outs) - 2, many - 1: len(outs) - 1}
        args += [local, beside]
        scratch = [tmp, *acts, pltpu.SemaphoreType.DMA((1,))]
        scratch += [pltpu.VMEM(((rows + 2 * HALO) * ch, width), BF), pltpu.VMEM((2, strip, width), BF)]
        scratch += [pltpu.VMEM((2 * strip, width) if last else (2, *message), BF)]
        if last:
            (before,) = call(
                parts_kernel,
                "parts",
                (*parts, feat_e, feat_o),
                [(len(parts) * strip, width)],
                in_any=(len(parts), len(parts) + 1),
            )
            backs = send(before, near(1))
        results = call(
            functools.partial(step_kernel, ch, step, steps),
            "refine",
            args,
            outs,
            scratch,
            flops,
            in_any=in_any,
            out_any=out_any,
            aliases=aliases,
        )
        if not last:
            feat, msg_e, msg_o, *results = results
            feat_e, feat_o = send(msg_e, even), send(msg_o, odd)
        if last:
            own, part, *results = results
        outputs = results
    back = send(part, near(1))

    outputs = call(
        functools.partial(finish_own_kernel, strip, steps),
        "finish_own",
        [own, backs, *outputs],
        [whole] * 2,
        [pltpu.SemaphoreType.DMA((steps,))],
        in_any=(0, 1, 2, 3),
        out_any=(0, 1),
        aliases={2: 0, 3: 1},
    )
    outputs = call(
        functools.partial(finish_kernel, strip, steps),
        "finish",
        [back, *outputs],
        [whole] * 2,
        [pltpu.SemaphoreType.DMA],
        in_any=(0, 1, 2),
        out_any=(0, 1),
        aliases={1: 0, 2: 1},
    )
    return tuple(o.reshape(frames.shape) for o in outputs)


def solution(mesh):
    return jax.shard_map(
        on_device,
        mesh=mesh,
        in_specs=(
            P(None, None, ("clips", "tiles"), None),
            P(None, ("clips", "tiles")),
            P(None, ("clips", "tiles")),
            P(),
            P(),
        ),
        out_specs=(
            P(None, None, ("clips", "tiles"), None),
            P(None, None, ("clips", "tiles"), None),
        ),
        check_vma=False,
    )
```

```python
import functools

import jax
import jax.numpy as jnp
from jax import lax
from jax.experimental import pallas as pl
from jax.experimental.pallas import tpu as pltpu
from jax.sharding import PartitionSpec as P

BS = 8
REACH = 2
QUAD = 4
HALO = 4
CAPACITY = 4
BF = jnp.bfloat16
F32 = jnp.float32


class Place:
    def __init__(self):
        me = lax.axis_index("tiles")
        self.me = me
        self.strip = me % QUAD
        self.core = me % 2
        self.side = self.strip // 2
        self.group = me // QUAD
        self.odd = self.group % 2
        self.top = self.group == 0
        self.bottom = self.group == lax.axis_size("tiles") // QUAD - 1


def leaky(value):
    widened = value.astype(F32)
    return jnp.maximum(widened, 0.1 * widened).astype(BF)


def rows_first(src, src_start, dst, dst_start, tmp, ch):
    tmp[...] = src[pl.ds(src_start, BS * ch), :].astype(F32)
    for r in range(BS):
        row = tmp[pl.ds(r, ch, stride=BS), :]
        dst[pl.ds(dst_start + r * ch, ch), :] = row.astype(BF)


def channels_first(src, src_start, dst, tmp, ch):
    for r in range(BS):
        tmp[pl.ds(r, ch, stride=BS), :] = src[pl.ds(src_start + r * ch, ch), :].astype(F32)
    dst[...] = tmp[...].astype(BF)


def pack_first_kernel(ch, crow, frames, motion_f, motion_b, mine, mine_edge, other, rest, following, motion_buf, tmp, sems):
    place = Place()
    steps, strip = frames.shape[:2]
    half = HALO * ch
    core = place.core
    outs = (mine, other)
    lists = [
        pltpu.make_async_copy(motion, motion_buf.at[n], sems.at[4 + n]) for n, motion in enumerate((motion_f, motion_b))
    ]
    copies = []
    for n in range(2):
        back = 1 - core if n else core
        copies.append(frame_copy(frames, 0, back, outs[n].at[pl.ds(0, strip)], sems.at[n]))
        copies.append(frame_copy(frames, 1, back, following.at[n], sems.at[2 + n]))
    later = [
        frame_copy(frames, step, 1 - core, rest.at[pl.ds((step - 1) * strip, strip)], sems.at[5 + step])
        for step in range(1, steps)
    ]
    for copy in lists + copies + later:
        copy.start()
    for copy in lists:
        copy.wait()
    blocks = motion_f.shape[1]
    width = mine.shape[1]
    column = lax.broadcasted_iota(jnp.int32, motion_f.shape, 1)
    spread = jnp.where(
        lax.broadcasted_iota(jnp.int32, (blocks, width), 1) // BS
        == lax.broadcasted_iota(jnp.int32, (blocks, width), 0),
        1.0,
        0.0,
    ).astype(BF)
    wides = []
    for n in range(2):
        taken = motion_buf[n]
        across = taken // blocks
        code = (across - place.me + REACH) * (2 * blocks) + (taken - across * blocks - column + blocks - 1)
        wide = jnp.dot(code.astype(BF), spread, preferred_element_type=F32).astype(BF)
        frames_order = range(steps - 1) if n == 0 else range(steps - 2, -1, -1)
        wides += [wide[frame : frame + 1] for frame in frames_order]
    wides.append(jnp.zeros((crow - len(wides), width), BF))
    code = jnp.concatenate(wides, axis=0)
    for out in outs:
        out[pl.ds(strip, crow), :] = code
    for copy in copies:
        copy.wait()
    for n, (out, start) in enumerate(((mine_edge, 0), (other, strip + crow))):
        edge_of(place.side == 0, ch, following[n], out, start, tmp)
    for copy in later:
        copy.wait()


def edge_of(top, ch, strip_values, out, start, tmp):
    tmp[...] = strip_values.astype(F32)
    for r in range(HALO):
        one, two = tmp[pl.ds(r, ch, stride=BS), :], tmp[pl.ds(BS - HALO + r, ch, stride=BS), :]
        out[pl.ds(start + r * ch, ch), :] = jnp.where(top, one, two).astype(BF)


def pair_first_kernel(ch, crow, mine, mine_edge, partner, rest_in, out, edge, rest_out, tmp):
    place = Place()
    strip = BS * ch
    half = HALO * ch
    own = place.core == place.side
    first = jnp.where(own, mine[pl.ds(0, strip), :].astype(F32), partner[pl.ds(0, strip), :].astype(F32))
    edge_of(place.side == 0, ch, first, edge, 0, tmp)
    second = partner[pl.ds(strip + crow, half), :].astype(F32)
    edge[pl.ds(half, half), :] = jnp.where(own, mine_edge[...].astype(F32), second).astype(BF)
    for n, piece in enumerate((mine, partner)):
        at = place.core ^ n
        out[pl.ds(pl.multiple_of(at * strip, strip), strip), :] = piece[pl.ds(0, strip), :]
        for ref, start in ((out, 2 * strip), (edge, 2 * half)):
            ref[pl.ds(pl.multiple_of(start + at * crow, crow), crow), :] = piece[pl.ds(strip, crow), :]


def above_below(place, along, cross):
    left = place.side == 0
    along, cross = along.astype(F32), cross.astype(F32)
    return jnp.where(left, cross, along).astype(BF), jnp.where(left, along, cross).astype(BF)


def frame_copy(frames, step, back, out, sem):
    steps = frames.shape[0]
    return pltpu.make_async_copy(frames.at[step + back * (steps - 1 - 2 * step)], out, sem)


def pair_copies(frames, swapped, core, first, count, out, sems):
    strip = frames.shape[1]
    copies = []
    for n in range(count):
        step = first + n
        own = out.at[pl.ds(pl.multiple_of((2 * n + core) * strip, strip), strip)]
        his = out.at[pl.ds(pl.multiple_of((2 * n + 1 - core) * strip, strip), strip)]
        copies.append(frame_copy(frames, step, core, own, sems.at[2 * n]))
        copies.append(
            pltpu.make_async_copy(swapped.at[pl.ds((step - 1) * strip, strip)], his, sems.at[2 * n + 1])
        )
    return copies


def edge_rows(place, ch, pair, outer, out, start, tmp):
    strip = BS * ch
    one, two = pair[pl.ds(0, strip), :].astype(F32), pair[pl.ds(strip, strip), :].astype(F32)
    left = place.side == 0
    if outer:
        edge_of(left, ch, jnp.where(left, one, two), out, start, tmp)
    else:
        edge_of(jnp.logical_not(left), ch, jnp.where(left, two, one), out, start, tmp)


def pair_kernel(ch, frames, swapped, near_out, far_out, last_out, tmp, sems):
    place = Place()
    steps, strip = frames.shape[:2]
    half = HALO * ch
    between = range(2, steps - 1)
    pairs = {1: near_out.at[pl.ds(0, 2 * strip)], steps - 1: last_out}
    for n, step in enumerate(between):
        pairs[step] = far_out.at[pl.ds(2 * n * strip, 2 * strip)]
    copies = []
    for step, out in pairs.items():
        copies += pair_copies(frames, swapped, place.core, step, 1, out, sems.at[pl.ds(2 * step, 2)])
    for copy in copies:
        copy.start()
    for copy in copies:
        copy.wait()
    edge_rows(place, ch, pairs[2], True, near_out, 2 * strip, tmp)
    at = 2 * len(between) * strip
    for step in range(3, steps):
        edge_rows(place, ch, pairs[step], True, far_out, at, tmp)
        at += half
    edge_rows(place, ch, last_out, False, far_out, at, tmp)


def gather_first_kernel(ch, crow, pair, received, conv, near_in, xq, codes, near_out, tmp):
    place = Place()
    strip = BS * ch
    for n, piece in enumerate((pair, received)):
        side = place.side ^ n
        for m in range(2):
            at = side * 2 + m
            rows_first(piece, m * strip, xq, pl.multiple_of(at * strip, strip), tmp, ch)
            code_at = pl.multiple_of(at * crow, crow)
            codes[pl.ds(code_at, crow), :] = piece[pl.ds(2 * strip + m * crow, crow), :]


def gather_kernel(ch, pair_at, edge_at, pair, received, after, xq, edges, tmp):
    strip = BS * ch
    half = HALO * ch
    side = Place().side
    for n, piece in enumerate((pair, received)):
        for m in range(2):
            start = ((side + n) % 2 * 2 + m) * strip
            rows_first(piece, pair_at + m * strip, xq, pl.multiple_of(start, strip), tmp, ch)
        edges[side ^ n] = piece[pl.ds(edge_at, half), :]


def split_results(ch, feat, own_out, part_out, tmp):
    strip = BS * ch
    own = Place().strip
    channels_first(feat, pl.multiple_of(own * strip, strip), own_out, tmp, ch)
    channels_first(feat, pl.multiple_of((own ^ 1) * strip, strip), part_out, tmp, ch)


def gather_last_kernel(ch, inner_at, pair, received, after, xq, inner, tmp):
    strip = BS * ch
    for m in range(2):
        rows_first(pair, m * strip, xq, m * strip, tmp, ch)
    inner[...] = received[pl.ds(inner_at, HALO * ch), :]


class Codes:
    def __init__(self, rows):
        width = rows[0].shape[1]
        self.rows = rows
        self.blocks = width // BS
        k_id = lax.broadcasted_iota(jnp.int32, (width, width), 0)
        l_id = lax.broadcasted_iota(jnp.int32, (width, width), 1)
        base = (k_id // BS - l_id // BS + self.blocks - 1).astype(F32)
        self.base = jnp.where(k_id % BS == l_id % BS, base, -1.0e4)
        self.slot = k_id.astype(F32)
        self.before = jnp.where((k_id % BS == 0) & (k_id // BS < l_id // BS), 1.0, 0.0).astype(BF)
        self.lane = (lax.broadcasted_iota(jnp.int32, (1, width), 1) % BS).astype(F32)
        self.zero = jnp.zeros((width, width), BF)
        self.ranks = {}

    def plain(self, dest, source):
        ds = source - dest
        if abs(ds) > REACH:
            return self.zero
        shift = float((ds + REACH) * 2 * self.blocks)
        return jnp.where(self.rows[dest + 2] - shift == self.base, 1.0, 0.0).astype(BF)

    def rank_all(self, wanted):
        rows = []
        for dest, source in wanted:
            low = float((source - dest + REACH) * 2 * self.blocks)
            code = self.rows[dest + 2]
            rows.append(jnp.where((code >= low) & (code < low + 2 * self.blocks), 1.0, 0.0))
        count = len(rows)
        rows += [rows[0]] * (-count % 16)
        stacked = jnp.concatenate(rows, axis=0)
        before = jnp.dot(stacked.astype(BF), self.before, preferred_element_type=F32)
        for n, key in enumerate(wanted):
            self.ranks[key] = jnp.where(
                stacked[n : n + 1] > 0, before[n : n + 1] * BS + self.lane, -1.0e4
            )

    def packed(self, dest, source, region):
        at = self.ranks[dest, source] + float(region * CAPACITY * BS)
        return jnp.where(self.slot == at, 1.0, 0.0).astype(BF)

    def pack(self, dest, source, region):
        return lax.dot_general(
            self.plain(dest, source),
            self.packed(dest, source, region),
            (((1,), (1,)), ((), ())),
            preferred_element_type=F32,
        )


FROM_ABOVE = ((0, -1), (0, -2), (1, -1))
FROM_BELOW = ((QUAD - 1, QUAD), (QUAD - 1, QUAD + 1), (QUAD - 2, QUAD))
TO_BELOW = tuple((d + QUAD, s + QUAD) for d, s in FROM_ABOVE)
TO_ABOVE = tuple((d - QUAD, s - QUAD) for d, s in FROM_BELOW)
TAKEN = (FROM_ABOVE, FROM_BELOW)
GIVEN = (TO_ABOVE, TO_BELOW)
REGIONS = len(FROM_ABOVE)


def step_codes(ch, place, step, steps, codes, along, cross):
    crow = codes.shape[0] // QUAD
    width = codes.shape[1]
    pick = place.core * (steps - 1) + step - 1
    row_id = lax.broadcasted_iota(jnp.int32, (crow, width), 0)
    start = 2 * HALO * ch
    above, below = above_below(
        place, along[pl.ds(start, 2 * crow), :], cross[pl.ds(start, 2 * crow), :]
    )

    def row(block):
        return jnp.sum(jnp.where(row_id == pick, block.astype(F32), 0.0), axis=0, keepdims=True)

    rows = [row(above[n * crow : (n + 1) * crow]) for n in range(2)]
    rows += [row(codes[pl.ds(strip * crow, crow), :]) for strip in range(QUAD)]
    rows += [row(below[n * crow : (n + 1) * crow]) for n in range(2)]
    return Codes(rows)


def own_sources(dest):
    return [source for source in range(QUAD) if abs(source - dest) <= REACH]


def choices_kernel(ch, step, steps, codes, along, cross, feat, local, own_out, part_out, *refs):
    place = Place()
    code = step_codes(ch, place, step, steps, codes, along, cross)
    code.rank_all(FROM_ABOVE + FROM_BELOW)
    half = HALO * ch
    strip = BS * ch
    width = feat.shape[1]
    for pair in range(0, QUAD, 2):
        left = [feat[pl.ds(source * strip, strip), :] for source in range(QUAD)]
        right = [
            jnp.concatenate([code.plain(pair + m, source) for m in range(2)], axis=1) for source in range(QUAD)
        ]
        got = jnp.dot(
            jnp.concatenate(left, axis=1), jnp.concatenate(right, axis=0), preferred_element_type=F32
        ).astype(BF)
        for m in range(2):
            local[pl.ds(half + (pair + m) * strip, strip), :] = got[:, m * width : (m + 1) * width]
    for dest, shift, at in ((-1, half, 0), (QUAD, 0, half + QUAD * strip)):
        sources = own_sources(dest)
        left = [feat[pl.ds(source * strip + shift, half), :] for source in sources]
        right = [code.plain(dest, source) for source in sources]
        local[pl.ds(at, half), :] = jnp.dot(
            jnp.concatenate(left, axis=1), jnp.concatenate(right, axis=0), preferred_element_type=F32
        ).astype(BF)
    for side in range(2):
        for m in range(2):
            value = [
                code.packed(dest, source, n) for n, (dest, source) in enumerate(TAKEN[side]) if dest == 2 * side + m
            ]
            refs[side][:, pl.ds(m * width, width)] = sum(value[1:], value[0])
    if step + 1 < steps:
        send_choices(code_of_next(ch, place, step, steps, codes, along, cross), refs[2:-1])
    split_results(ch, feat, own_out, part_out, refs[-1])


def code_of_next(ch, place, step, steps, codes, along, cross):
    code = step_codes(ch, place, step + 1, steps, codes, along, cross)
    code.rank_all(TO_ABOVE + TO_BELOW)
    return code


def given_sources(side):
    return sorted({source for _, source in GIVEN[side]})


def send_choices(code, outs):
    width = code.zero.shape[0]
    for side in range(2):
        blocks, edge = outs[2 * side : 2 * side + 2]
        for n, source in enumerate(given_sources(side)):
            total = sum(code.pack(d, source, at) for at, (d, origin) in enumerate(GIVEN[side]) if origin == source)
            blocks[pl.ds(n * width, width), :] = total.astype(BF)
        dest = side * (QUAD - 1)
        for n, source in enumerate(own_sources(dest)):
            edge[pl.ds(n * width, width), :] = code.plain(dest, source)


def choice_shapes(width):
    sent = []
    for side in range(2):
        sent += [(len(given_sources(side)) * width, width), (len(own_sources(side * (QUAD - 1))) * width, width)]
    return [(width, 2 * width)] * 2, sent


def join_rows(ch, join_mat, al, inp, extra=None):
    width = al.shape[1]
    sides = []
    for h in range(2):
        a, b = 2 * h * ch, (2 * h + 1) * ch
        sides.append(jnp.concatenate([al[a : a + ch], inp[a : a + ch], al[b : b + ch], inp[b : b + ch]], axis=0))
    mixed = jnp.dot(join_mat, jnp.concatenate(sides, axis=1), preferred_element_type=F32)
    rows = [mixed[q * ch : (q + 1) * ch, h * width : (h + 1) * width] for h in range(2) for q in range(2)]
    if extra is not None:
        rows = [row + extra[n * ch : (n + 1) * ch].astype(F32) for n, row in enumerate(rows)]
    return [row.astype(BF) for row in rows]


def fold_rows(ch):
    return BS * ch * REGIONS // (REGIONS + 1)


def pack_messages(ch, fout, par, join_mat, choices, inputs, sent, msg_e, msg_o):
    half = HALO * ch
    strip = BS * ch
    width = fout.shape[1]
    fold = fold_rows(ch)
    piece = strip - fold
    group = width // (REGIONS + 1)
    lane = lax.broadcasted_iota(jnp.int32, (piece, width), 1)
    for side in range(2):
        blocks, edge = choices[2 * side : 2 * side + 2]
        left = [fout[pl.ds(source * strip, strip), :] for source in given_sources(side)]
        got = jnp.dot(jnp.concatenate(left, axis=1), blocks[...], preferred_element_type=F32).astype(BF)
        for n in range(REGIONS):
            rolled = pltpu.roll(got[fold:], (REGIONS - n) * group, 1)
            sent[side, pl.ds(n * piece, piece), :] = jnp.where(
                lane < REGIONS * group, got[n * piece : (n + 1) * piece], rolled
            )
        shift = side * half
        left = [fout[pl.ds(source * strip + shift, half), :] for source in own_sources(side * (QUAD - 1))]
        al = jnp.dot(jnp.concatenate(left, axis=1), edge[...], preferred_element_type=F32).astype(BF)
        inp = jnp.zeros((half, width), BF) if inputs is None else inputs[side]
        for n, row in enumerate(join_rows(ch, join_mat, al, inp)):
            sent[side, pl.ds(fold + n * ch, ch), :] = row
    msg_e[...] = sent[1 - par]
    msg_o[...] = sent[par]


def unpack_message(ch, message, recv, side):
    strip = BS * ch
    width = message.shape[1]
    fold = fold_rows(ch)
    piece = strip - fold
    group = width // (REGIONS + 1)
    lane = lax.broadcasted_iota(jnp.int32, (piece, width), 1)
    recv[side, pl.ds(0, fold), :] = message[pl.ds(0, fold), :]
    total = None
    for n in range(REGIONS):
        rolled = pltpu.roll(message[pl.ds(n * piece, piece), :], (n + 1) * group, 1)
        total = rolled if total is None else jnp.where(lane < n * group, total, rolled)
    recv[side, pl.ds(fold, piece), :] = total


class Rows:
    def __init__(self, ch, width, top_ok, bottom_ok, count):
        lane = lax.broadcasted_iota(jnp.int32, (ch, width), 1)
        self.not_first = lane > 0
        self.not_last = lane < width - 1
        self.zero = jnp.zeros((ch, width), BF)
        self.top_ok = top_ok
        self.bottom_ok = bottom_ok
        self.count = count

    def active(self, value, row):
        act = leaky(value)
        if row < 0:
            act = jnp.where(self.top_ok, act, self.zero)
        if row >= self.count:
            act = jnp.where(self.bottom_ok, act, self.zero)
        return (
            jnp.where(self.not_first, pltpu.roll(act, 1, 1), self.zero),
            act,
            jnp.where(self.not_last, pltpu.roll(act, act.shape[1] - 1, 1), self.zero),
        )

    def put(self, buf, here, value, row):
        for n, act in enumerate(self.active(value, row)):
            buf[n, here, :] = act


OFF = 8


def here_of(row, ch, count=1):
    return pl.ds((row + OFF) * ch, count * ch)


def conv_layer(ch, weight, source, held, start, stop, emit):
    width = held.shape[1]
    for first in range(start, stop, 4):
        sides = [
            jnp.concatenate([source[n, here_of(first + 2 * h - 1, ch, 4), :] for n in range(3)], axis=0)
            for h in range(2)
        ]
        out = jnp.dot(weight, jnp.concatenate(sides, axis=1), preferred_element_type=F32)
        for h in range(2):
            for q in range(2):
                row = first + 2 * h + q
                total = held[here_of(row, ch), :].astype(F32)
                total += out[q * ch : (q + 1) * ch, h * width : (h + 1) * width]
                emit(row, total.astype(BF))


def join_first_rows(ch, join_mat, inp):
    width = inp.shape[1]
    mixed = jnp.dot(
        join_mat, jnp.concatenate([inp[: 2 * ch], inp[2 * ch :]], axis=1), preferred_element_type=F32
    ).astype(BF)
    return [mixed[q * ch : (q + 1) * ch, h * width : (h + 1) * width] for h in range(2) for q in range(2)]


def clear_outside(space, ch, rows, bufs):
    for buf in bufs:
        for row in (-HALO - 1, rows + HALO):
            for n in range(3):
                buf[n, here_of(row, ch), :] = space.zero


def conv_layers(ch, conv, space, rows, act_a, act_b, held, fout):
    layers = conv.shape[0]
    source, target = act_a, act_b
    for layer in range(layers):
        need = layers - 1 - layer
        reach = -(-need // 2) * 2
        start, stop = -reach, rows + reach
        if (stop - start) % 4:
            start, stop = -HALO, rows + HALO

        def emit(row, value, layer=layer, target=target):
            if layer < layers - 1:
                held[here_of(row, ch), :] = value
                space.put(target, here_of(row, ch), value, row)
            else:
                fout[pl.ds(row * ch, ch), :] = value

        conv_layer(ch, conv[layer], source, held, start, stop, emit)
        source, target = target, source


def first_kernel(ch, steps, *refs):
    xq, along, cross, join, join_both, conv, codes, far_in, *refs = refs
    fout, msg_e, msg_o, far_out, act_a, act_b, held, sent, *choices = refs
    half = HALO * ch
    rows = QUAD * BS
    place = Place()
    space = Rows(ch, xq.shape[1], jnp.logical_not(place.top), jnp.logical_not(place.bottom), rows)
    send_choices(code_of_next(ch, place, 0, steps, codes, along, cross), choices)
    above, below = above_below(place, along[pl.ds(0, half), :], cross[pl.ds(0, half), :])
    clear_outside(space, ch, rows, (act_a, act_b))
    join_mat = join[...]
    for first in range(-HALO, rows + HALO, 4):
        inp = above if first < 0 else below if first >= rows else xq[pl.ds(first * ch, 4 * ch), :]
        for n, value in enumerate(join_first_rows(ch, join_mat, inp)):
            held[here_of(first + n, ch), :] = value
            space.put(act_a, here_of(first + n, ch), value, first + n)
    conv_layers(ch, conv, space, rows, act_a, act_b, held, fout)
    pack_messages(ch, fout, place.odd, join_both[...], choices, None, sent, msg_e, msg_o)


def step_kernel(ch, step, steps, *refs):
    strip = BS * ch
    half = HALO * ch
    last = step == steps - 1
    refs = list(refs)

    def take(count):
        taken = refs[:count]
        del refs[:count]
        return taken

    xq, along, cross, join, conv = take(5)
    feat_e, feat_o = take(2)
    choices = take(2 if last else 6)
    before, out_a, out_b = take(3)
    (local,) = take(1)
    if last:
        (x_inner,) = take(1)
    else:
        next_edges, fout, msg_e, msg_o = take(4)
    own_out, part_out = take(2) if last else (None, None)
    out_f, out_g = take(2)
    tmp, act_a, act_b, held, sems, aligned, recv = take(7)
    if last:
        (fout,) = take(1)
    else:
        (sent,) = take(1)
    width = xq.shape[-1]
    place = Place()
    par = place.odd
    core = place.core
    rows = 2 * BS if last else QUAD * BS
    left_side = place.side == 0

    copies = own_copies(strip, step - 1, steps, before, out_f, out_g, sems.at[0])
    for n, copy in copies:
        pl.when(core == n)(copy.start)

    def choose(which, one, two):
        return jnp.where(which, one.astype(F32), two.astype(F32)).astype(BF)

    fold = fold_rows(ch)
    zero = jnp.zeros((half, width), BF)
    one, two = feat_e[pl.ds(fold, half), :], feat_o[pl.ds(fold, half), :]
    over_sent, under_sent = choose(par == 1, one, two), choose(par == 1, two, one)
    over, under = zero, zero
    if step == 1:
        over, under = above_below(place, along[pl.ds(half, half), :], cross[pl.ds(half, half), :])
    if last:
        inner = x_inner[...]
        over, under = choose(left_side, zero, inner), choose(left_side, inner, zero)
        over_sent, under_sent = choose(left_side, over_sent, zero), choose(left_side, zero, under_sent)
    unpack_message(ch, feat_e, recv, 1 - par)
    unpack_message(ch, feat_o, recv, par)
    for edge in (0, half + QUAD * strip):
        aligned[pl.ds(edge, half), :] = local[pl.ds(edge, half), :]
    for side in range(2):
        got = jnp.dot(recv[side], choices[side][...], preferred_element_type=F32)
        for m in range(2):
            here = pl.ds(half + (2 * side + m) * strip, strip)
            both = got[:, m * width : (m + 1) * width] + local[here, :].astype(F32)
            aligned[here, :] = both.astype(BF)

    space = Rows(ch, width, jnp.logical_not(place.top), jnp.logical_not(place.bottom), rows)
    if last:
        space.top_ok = space.top_ok | (place.side == 1)
        space.bottom_ok = space.bottom_ok | left_side
    clear_outside(space, ch, rows, (act_a, act_b))
    join_mat = join[...]
    for first in range(-HALO, rows + HALO, 4):
        inp, extra = xq, None
        if first < 0:
            inp, extra = over, over_sent
        elif first >= rows:
            inp, extra = under, under_sent
        else:
            inp = xq[pl.ds(first * ch, 4 * ch), :]
        at = (first + HALO) * ch
        if last:
            at = pl.multiple_of(place.side * (2 * strip) + at, half)
        al = aligned[pl.ds(at, half), :]
        for n, value in enumerate(join_rows(ch, join_mat, al, inp, extra)):
            held[here_of(first + n, ch), :] = value
            space.put(act_a, here_of(first + n, ch), value, first + n)

    conv_layers(ch, conv, space, rows, act_a, act_b, held, fout)
    if not last:
        pack_messages(ch, fout, par, join_mat, choices[2:], next_edges, sent, msg_e, msg_o)
    else:
        channels_first(fout, pl.multiple_of(core * strip, strip), own_out, tmp, ch)
        channels_first(fout, pl.multiple_of((core ^ 1) * strip, strip), part_out, tmp, ch)
    for n, copy in copies:
        pl.when(core == n)(copy.wait)


def parts_kernel(*refs):
    out = refs[-1]
    strip = refs[0].shape[0]
    for n in range(out.shape[0] // strip):
        out[pl.ds(n * strip, strip), :] = refs[n][...]


def own_copies(strip, step, steps, own, out_f, out_g, sem):
    return [
        (0, pltpu.make_async_copy(own, out_f.at[pl.ds(step * strip, strip)], sem)),
        (1, pltpu.make_async_copy(own, out_g.at[pl.ds((steps - 1 - step) * strip, strip)], sem)),
    ]


def back_copies(strip, step, steps, back, out_f, out_g, sem):
    return [
        (0, pltpu.make_async_copy(back, out_g.at[pl.ds((steps - 1 - step) * strip, strip)], sem)),
        (1, pltpu.make_async_copy(back, out_f.at[pl.ds(step * strip, strip)], sem)),
    ]


def run_copies(copies):
    core = Place().core
    for n, copy in copies:
        pl.when(core == n)(copy.start)
    for n, copy in copies:
        pl.when(core == n)(copy.wait)


def finish_own_kernel(strip, steps, own, backs, out_a, out_b, out_f, out_g, sems):
    copies = own_copies(strip, steps - 1, steps, own, out_f, out_g, sems.at[0])
    for step in range(steps - 1):
        before = backs.at[pl.ds(step * strip, strip)]
        copies += back_copies(strip, step, steps, before, out_f, out_g, sems.at[1 + step])
    run_copies(copies)


def finish_kernel(strip, steps, back, out_a, out_b, out_f, out_g, sem):
    run_copies(back_copies(strip, steps - 1, steps, back, out_f, out_g, sem))


def weights_kernel(conv, join, wide, join_both, join_first):
    core = Place().core
    layers, ch = conv.shape[1], conv.shape[3]
    zero = jnp.zeros((ch, ch), BF)
    for layer in range(layers):
        for dx in range(3):
            taps = [conv[core, layer, 3 * dy + dx] for dy in range(3)]
            for q in range(2):
                line = [zero] * q + taps + [zero] * (1 - q)
                wide[layer, pl.ds(q * ch, ch), pl.ds(dx * 4 * ch, 4 * ch)] = jnp.concatenate(line, axis=1)
    both = join[core]
    none = jnp.zeros_like(both)
    join_both[pl.ds(0, ch), :] = jnp.concatenate([both, none], axis=1)
    join_both[pl.ds(ch, ch), :] = jnp.concatenate([none, both], axis=1)
    enter = both[:, ch:]
    join_first[pl.ds(0, ch), :] = jnp.concatenate([enter, zero], axis=1)
    join_first[pl.ds(ch, ch), :] = jnp.concatenate([zero, enter], axis=1)


VMEM = pl.BlockSpec(memory_space=pltpu.VMEM)
ANY = pl.BlockSpec(memory_space=pl.ANY)
HBM = pl.BlockSpec(memory_space=pltpu.HBM)


def call(kernel, name, args, outs, scratch=(), flops=0, in_any=(), out_any=(), aliases=None, in_hbm=(), free=False):
    args = [pltpu.with_memory_space_constraint(a, pltpu.HBM) if n in in_hbm else a for n, a in enumerate(args)]
    return pl.pallas_call(
        kernel,
        out_shape=[jax.ShapeDtypeStruct(o, BF) for o in outs],
        in_specs=[HBM if n in in_hbm else ANY if n in in_any else VMEM for n in range(len(args))],
        out_specs=[ANY if n in out_any else VMEM for n in range(len(outs))],
        scratch_shapes=list(scratch),
        input_output_aliases=aliases or {},
        compiler_params=pltpu.CompilerParams(vmem_limit_bytes=32 << 20),
        cost_estimate=pl.CostEstimate(
            flops=flops,
            bytes_accessed=0 if free else sum(a.size * a.dtype.itemsize for a in args),
            transcendentals=0,
        ),
        name=name,
    )(*args)


def sooner(value, *after):
    return pl.pallas_call(
        lambda *refs: None,
        out_shape=jax.ShapeDtypeStruct(value.shape, value.dtype),
        in_specs=[ANY] * (1 + len(after)),
        out_specs=ANY,
        input_output_aliases={0: 0},
        compiler_params=pltpu.CompilerParams(vmem_limit_bytes=1 << 20),
        cost_estimate=pl.CostEstimate(flops=0, bytes_accessed=2 << 20, transcendentals=0),
        name="sooner",
    )(value, *after)


def pairings(count, idle):
    groups = count // QUAD
    out = []
    for parity in range(2):
        pairs = []
        for i in range(count):
            g = i // QUAD
            other = g + 1 if g % 2 == parity else g - 1
            pairs.append((i, i % QUAD + other * QUAD if 0 <= other < groups else i ^ idle))
        out.append(pairs)
    return out


def edge_pairings(count):
    groups = count // QUAD
    along, cross = [], []
    for i in range(count):
        g, side, core = i // QUAD, i % QUAD // 2, i % 2
        if side == 0:
            along += [(i, i - QUAD)] if g > 0 else []
            cross.append((i, i - QUAD + 2 if g > 0 else i ^ 1))
        else:
            along += [(i, i + QUAD)] if g < groups - 1 else []
            cross.append((i, i + QUAD - 2 if g < groups - 1 else i ^ 1))
    return along, cross


def on_device(frames, motion_forward, motion_backward, join_weight, conv_weight):
    steps, ch, strip_rows, width = frames.shape
    strip = strip_rows * ch
    half = HALO * ch
    crow = 16
    count = lax.axis_size("tiles")
    even, odd = pairings(count, 1)
    along_pairs, cross_pairs = edge_pairings(count)

    def near(k):
        return [(i, i ^ k) for i in range(count)]

    def send(value, pairs):
        return lax.ppermute(value, "tiles", pairs)

    tmp = pltpu.VMEM((strip, width), F32)
    piece = (strip, width)
    rows = QUAD * BS
    message = (fold_rows(ch) + half, width)
    feature = (rows * ch, width)
    whole = (steps * strip, width)
    flat = frames.reshape(steps, strip, width)
    later = ((steps - 1) * strip, width)
    first = (strip + crow, width)
    mine, mine_edge, other, rest = call(
        functools.partial(pack_first_kernel, ch, crow),
        "pack_first",
        (flat, motion_forward, motion_backward),
        [first, (half, width), (strip + crow + half, width), later],
        [
            pltpu.VMEM((2, *piece), BF),
            pltpu.VMEM((2, *motion_forward.shape), jnp.int32),
            tmp,
            pltpu.SemaphoreType.DMA((5 + steps,)),
        ],
        in_hbm=(0, 1, 2),
        out_any=(3,),
    )
    pair, edge, rest = call(
        functools.partial(pair_first_kernel, ch, crow),
        "pair_first",
        (mine, mine_edge, send(other, near(1)), rest),
        [(2 * (strip + crow), width), (2 * (half + crow), width), later],
        [tmp],
        in_any=(3,),
        out_any=(2,),
        aliases={3: 2},
    )
    received = send(pair, near(2))
    swapped = send(rest, near(1))
    along, cross = sooner(send(edge, along_pairs)), send(edge, cross_pairs)
    far_pairs = 2 * (steps - 3) * strip
    pair_near, pair_far, pair_last = call(
        functools.partial(pair_kernel, ch),
        "pair_rest",
        (flat, swapped),
        [(2 * strip + half, width), (far_pairs + (steps - 2) * half, width), (2 * strip, width)],
        [tmp, pltpu.SemaphoreType.DMA((2 * steps,))],
        in_hbm=(0,),
        in_any=(1,),
    )
    layers = conv_weight.shape[1]
    conv, join_both, join_first = call(
        weights_kernel,
        "weights",
        (conv_weight, join_weight),
        [(layers, 2 * ch, 12 * ch), (2 * ch, 4 * ch), (2 * ch, 2 * ch)],
        free=True,
    )
    xq, codes, pair_near = call(
        functools.partial(gather_first_kernel, ch, crow),
        "gather_first",
        (pair, received, conv, pair_near),
        [feature, (QUAD * crow, width), pair_near.shape],
        [tmp],
        in_any=(2, 3),
        out_any=(2,),
        aliases={3: 2},
        free=True,
    )
    received_near = send(pair_near, near(2))

    wide_act = pltpu.VMEM((3, (rows + 16) * ch, width), BF)
    flops = 2 * (rows + 2 * HALO) * width * ch * ch * 9 * layers
    part_shapes, sent_shapes = choice_shapes(width)
    acts = [wide_act, wide_act, pltpu.VMEM(((rows + 16) * ch, width), BF)]
    feat, msg_e, msg_o, pair_far = call(
        functools.partial(first_kernel, ch, steps),
        "refine_first",
        (xq, along, cross, join_first, join_both, conv, codes, pair_far),
        [feature, message, message, pair_far.shape],
        [*acts, pltpu.VMEM((2, *message), BF)] + [pltpu.VMEM(shape, BF) for shape in sent_shapes],
        flops,
        in_any=(7,),
        out_any=(3,),
        aliases={7: 3},
    )
    feat_e, feat_o = send(msg_e, even), send(msg_o, odd)
    parts = []
    received_far = send(pair_far, near(2))
    outputs = call(lambda after, a, b: None, "results", (feat,), [whole, whole], in_any=(0,), out_any=(0, 1), free=True)

    def choices_of(step):
        return call(
            functools.partial(choices_kernel, ch, step, steps),
            "choices",
            (codes, along, cross, feat),
            [((rows + 2 * HALO) * ch, width), piece, piece] + part_shapes + (sent_shapes if step + 1 < steps else []),
            [tmp],
        )

    def frame_of(step):
        if step == steps - 1:
            kernel = functools.partial(gather_last_kernel, ch, far_pairs + (steps - 3) * half)
            args, outs = (pair_last, received_far, feat), [(2 * strip, width), (half, width)]
        elif step == 1:
            kernel = functools.partial(gather_kernel, ch, 0, 2 * strip)
            args, outs = (pair_near, received_near, feat), [feature, (2, half, width)]
        else:
            kernel = functools.partial(gather_kernel, ch, 2 * (step - 2) * strip, far_pairs + (step - 2) * half)
            args, outs = (pair_far, received_far, feat), [feature, (2, half, width)]
        return call(kernel, "gather", args, outs, [tmp], in_any=(2,))

    for step in range(1, steps):
        last = step == steps - 1
        local, own, part, *choices = choices_of(step)
        x_now, beside = frame_of(step)
        feat_e = sooner(feat_e, x_now) if step > 1 else sooner(feat_e)
        parts = parts + [part]
        args = [x_now, along, cross, join_both, conv, feat_e, feat_o, *choices, own, *outputs]
        many = len(args)
        outs = [] if last else [feature, message, message]
        outs += [piece, piece, whole, whole] if last else [whole, whole]
        in_any = [many - 3, many - 2, many - 1]
        out_any = [len(outs) - 2, len(outs) - 1]
        aliases = {many - 2: len(outs) - 2, many - 1: len(outs) - 1}
        args += [local, beside]
        scratch = [tmp, *acts, pltpu.SemaphoreType.DMA((1,))]
        scratch += [pltpu.VMEM(((rows + 2 * HALO) * ch, width), BF), pltpu.VMEM((2, strip, width), BF)]
        scratch += [pltpu.VMEM((2 * strip, width) if last else (2, *message), BF)]
        if last:
            (before,) = call(
                parts_kernel,
                "parts",
                (*parts, feat_e, feat_o),
                [(len(parts) * strip, width)],
                in_any=(len(parts), len(parts) + 1),
            )
            backs = send(before, near(1))
        results = call(
            functools.partial(step_kernel, ch, step, steps),
            "refine",
            args,
            outs,
            scratch,
            flops,
            in_any=in_any,
            out_any=out_any,
            aliases=aliases,
        )
        if not last:
            feat, msg_e, msg_o, *results = results
            feat_e, feat_o = send(msg_e, even), send(msg_o, odd)
        if last:
            own, part, *results = results
        outputs = results
    back = send(part, near(1))

    outputs = call(
        functools.partial(finish_own_kernel, strip, steps),
        "finish_own",
        [own, backs, *outputs],
        [whole] * 2,
        [pltpu.SemaphoreType.DMA((steps,))],
        in_any=(0, 1, 2, 3),
        out_any=(0, 1),
        aliases={2: 0, 3: 1},
    )
    outputs = call(
        functools.partial(finish_kernel, strip, steps),
        "finish",
        [back, *outputs],
        [whole] * 2,
        [pltpu.SemaphoreType.DMA],
        in_any=(0, 1, 2),
        out_any=(0, 1),
        aliases={1: 0, 2: 1},
    )
    return tuple(o.reshape(frames.shape) for o in outputs)


def solution(mesh):
    return jax.shard_map(
        on_device,
        mesh=mesh,
        in_specs=(
            P(None, None, ("clips", "tiles"), None),
            P(None, ("clips", "tiles")),
            P(None, ("clips", "tiles")),
            P(),
            P(),
        ),
        out_specs=(
            P(None, None, ("clips", "tiles"), None),
            P(None, None, ("clips", "tiles"), None),
        ),
        check_vma=False,
    )
```

```python
import functools

import jax
import jax.numpy as jnp
from jax import lax
from jax.experimental import pallas as pl
from jax.experimental.pallas import tpu as pltpu
from jax.sharding import PartitionSpec as P

BS = 8
REACH = 2
QUAD = 4
HALO = 4
CAPACITY = 4
BF = jnp.bfloat16
F32 = jnp.float32


class Place:
    def __init__(self):
        me = lax.axis_index("tiles")
        self.me = me
        self.strip = me % QUAD
        self.core = me % 2
        self.side = self.strip // 2
        self.group = me // QUAD
        self.odd = self.group % 2
        self.top = self.group == 0
        self.bottom = self.group == lax.axis_size("tiles") // QUAD - 1


def leaky(value):
    widened = value.astype(F32)
    return jnp.maximum(widened, 0.1 * widened).astype(BF)


def rows_first(src, src_start, dst, dst_start, tmp, ch):
    tmp[...] = src[pl.ds(src_start, BS * ch), :].astype(F32)
    for r in range(BS):
        row = tmp[pl.ds(r, ch, stride=BS), :]
        dst[pl.ds(dst_start + r * ch, ch), :] = row.astype(BF)


def channels_first(src, src_start, dst, tmp, ch):
    for r in range(BS):
        tmp[pl.ds(r, ch, stride=BS), :] = src[pl.ds(src_start + r * ch, ch), :].astype(F32)
    dst[...] = tmp[...].astype(BF)


def pack_first_kernel(ch, crow, frames, motion_f, motion_b, mine, mine_edge, other, following, motion_buf, tmp, sems):
    place = Place()
    steps, strip = frames.shape[:2]
    half = HALO * ch
    core = place.core
    outs = (mine, other)
    lists = [
        pltpu.make_async_copy(motion, motion_buf.at[n], sems.at[4 + n]) for n, motion in enumerate((motion_f, motion_b))
    ]
    copies = []
    for n in range(2):
        back = 1 - core if n else core
        copies.append(frame_copy(frames, 0, back, outs[n].at[pl.ds(0, strip)], sems.at[n]))
        copies.append(frame_copy(frames, 1, back, following.at[n], sems.at[2 + n]))
    for copy in lists + copies:
        copy.start()
    for copy in lists:
        copy.wait()
    blocks = motion_f.shape[1]
    width = mine.shape[1]
    column = lax.broadcasted_iota(jnp.int32, motion_f.shape, 1)
    spread = jnp.where(
        lax.broadcasted_iota(jnp.int32, (blocks, width), 1) // BS
        == lax.broadcasted_iota(jnp.int32, (blocks, width), 0),
        1.0,
        0.0,
    ).astype(BF)
    wides = []
    for n in range(2):
        taken = motion_buf[n]
        across = taken // blocks
        code = (across - place.me + REACH) * (2 * blocks) + (taken - across * blocks - column + blocks - 1)
        wide = jnp.dot(code.astype(BF), spread, preferred_element_type=F32).astype(BF)
        frames_order = range(steps - 1) if n == 0 else range(steps - 2, -1, -1)
        wides += [wide[frame : frame + 1] for frame in frames_order]
    wides.append(jnp.zeros((crow - len(wides), width), BF))
    code = jnp.concatenate(wides, axis=0)
    for out in outs:
        out[pl.ds(strip, crow), :] = code
    for copy in copies:
        copy.wait()
    for n, (out, start) in enumerate(((mine_edge, 0), (other, strip + crow))):
        edge_of(place.side == 0, ch, following[n], out, start, tmp)


def edge_of(top, ch, strip_values, out, start, tmp):
    tmp[...] = strip_values.astype(F32)
    for r in range(HALO):
        one, two = tmp[pl.ds(r, ch, stride=BS), :], tmp[pl.ds(BS - HALO + r, ch, stride=BS), :]
        out[pl.ds(start + r * ch, ch), :] = jnp.where(top, one, two).astype(BF)


def pair_first_kernel(ch, crow, mine, mine_edge, partner, rest_in, out, edge, rest_out, tmp):
    place = Place()
    strip = BS * ch
    half = HALO * ch
    own = place.core == place.side
    first = jnp.where(own, mine[pl.ds(0, strip), :].astype(F32), partner[pl.ds(0, strip), :].astype(F32))
    edge_of(place.side == 0, ch, first, edge, 0, tmp)
    second = partner[pl.ds(strip + crow, half), :].astype(F32)
    edge[pl.ds(half, half), :] = jnp.where(own, mine_edge[...].astype(F32), second).astype(BF)
    for n, piece in enumerate((mine, partner)):
        at = place.core ^ n
        out[pl.ds(pl.multiple_of(at * strip, strip), strip), :] = piece[pl.ds(0, strip), :]
        for ref, start in ((out, 2 * strip), (edge, 2 * half)):
            ref[pl.ds(pl.multiple_of(start + at * crow, crow), crow), :] = piece[pl.ds(strip, crow), :]


def above_below(place, along, cross):
    left = place.side == 0
    along, cross = along.astype(F32), cross.astype(F32)
    return jnp.where(left, cross, along).astype(BF), jnp.where(left, along, cross).astype(BF)


def pack_rest_kernel(frames, after, rest, sems):
    steps, strip = frames.shape[:2]
    core = Place().core
    copies = [
        frame_copy(frames, step, 1 - core, rest.at[pl.ds((step - 1) * strip, strip)], sems.at[step])
        for step in range(1, steps)
    ]
    for copy in copies:
        copy.start()
    for copy in copies:
        copy.wait()


def frame_copy(frames, step, back, out, sem):
    steps = frames.shape[0]
    return pltpu.make_async_copy(frames.at[step + back * (steps - 1 - 2 * step)], out, sem)


def pair_copies(frames, swapped, core, first, count, out, sems):
    strip = frames.shape[1]
    copies = []
    for n in range(count):
        step = first + n
        own = out.at[pl.ds(pl.multiple_of((2 * n + core) * strip, strip), strip)]
        his = out.at[pl.ds(pl.multiple_of((2 * n + 1 - core) * strip, strip), strip)]
        copies.append(frame_copy(frames, step, core, own, sems.at[2 * n]))
        copies.append(
            pltpu.make_async_copy(swapped.at[pl.ds((step - 1) * strip, strip)], his, sems.at[2 * n + 1])
        )
    return copies


def edge_rows(place, ch, pair, outer, out, start, tmp):
    strip = BS * ch
    one, two = pair[pl.ds(0, strip), :].astype(F32), pair[pl.ds(strip, strip), :].astype(F32)
    left = place.side == 0
    if outer:
        edge_of(left, ch, jnp.where(left, one, two), out, start, tmp)
    else:
        edge_of(jnp.logical_not(left), ch, jnp.where(left, two, one), out, start, tmp)


def pair_kernel(ch, frames, swapped, near_out, far_out, last_out, tmp, sems):
    place = Place()
    steps, strip = frames.shape[:2]
    half = HALO * ch
    between = range(2, steps - 1)
    pairs = {1: near_out.at[pl.ds(0, 2 * strip)], steps - 1: last_out}
    for n, step in enumerate(between):
        pairs[step] = far_out.at[pl.ds(2 * n * strip, 2 * strip)]
    copies = []
    for step, out in pairs.items():
        copies += pair_copies(frames, swapped, place.core, step, 1, out, sems.at[pl.ds(2 * step, 2)])
    for copy in copies:
        copy.start()
    for copy in copies:
        copy.wait()
    edge_rows(place, ch, pairs[2], True, near_out, 2 * strip, tmp)
    at = 2 * len(between) * strip
    for step in range(3, steps):
        edge_rows(place, ch, pairs[step], True, far_out, at, tmp)
        at += half
    edge_rows(place, ch, last_out, False, far_out, at, tmp)


def gather_first_kernel(ch, crow, pair, received, conv, near_in, xq, codes, near_out, tmp):
    place = Place()
    strip = BS * ch
    for n, piece in enumerate((pair, received)):
        side = place.side ^ n
        for m in range(2):
            at = side * 2 + m
            rows_first(piece, m * strip, xq, pl.multiple_of(at * strip, strip), tmp, ch)
            code_at = pl.multiple_of(at * crow, crow)
            codes[pl.ds(code_at, crow), :] = piece[pl.ds(2 * strip + m * crow, crow), :]


def gather_kernel(ch, pair_at, edge_at, pair, received, after, xq, edges, tmp):
    strip = BS * ch
    half = HALO * ch
    side = Place().side
    for n, piece in enumerate((pair, received)):
        for m in range(2):
            start = ((side + n) % 2 * 2 + m) * strip
            rows_first(piece, pair_at + m * strip, xq, pl.multiple_of(start, strip), tmp, ch)
        edges[side ^ n] = piece[pl.ds(edge_at, half), :]


def split_results(ch, feat, own_out, part_out, tmp):
    strip = BS * ch
    own = Place().strip
    channels_first(feat, pl.multiple_of(own * strip, strip), own_out, tmp, ch)
    channels_first(feat, pl.multiple_of((own ^ 1) * strip, strip), part_out, tmp, ch)


def gather_last_kernel(ch, inner_at, pair, received, after, xq, inner, tmp):
    strip = BS * ch
    for m in range(2):
        rows_first(pair, m * strip, xq, m * strip, tmp, ch)
    inner[...] = received[pl.ds(inner_at, HALO * ch), :]


class Codes:
    def __init__(self, rows):
        width = rows[0].shape[1]
        self.rows = rows
        self.blocks = width // BS
        k_id = lax.broadcasted_iota(jnp.int32, (width, width), 0)
        l_id = lax.broadcasted_iota(jnp.int32, (width, width), 1)
        base = (k_id // BS - l_id // BS + self.blocks - 1).astype(F32)
        self.base = jnp.where(k_id % BS == l_id % BS, base, -1.0e4)
        self.slot = k_id.astype(F32)
        self.before = jnp.where((k_id % BS == 0) & (k_id // BS < l_id // BS), 1.0, 0.0).astype(BF)
        self.lane = (lax.broadcasted_iota(jnp.int32, (1, width), 1) % BS).astype(F32)
        self.zero = jnp.zeros((width, width), BF)
        self.ranks = {}

    def plain(self, dest, source):
        ds = source - dest
        if abs(ds) > REACH:
            return self.zero
        shift = float((ds + REACH) * 2 * self.blocks)
        return jnp.where(self.rows[dest + 2] - shift == self.base, 1.0, 0.0).astype(BF)

    def rank_all(self, wanted):
        rows = []
        for dest, source in wanted:
            low = float((source - dest + REACH) * 2 * self.blocks)
            code = self.rows[dest + 2]
            rows.append(jnp.where((code >= low) & (code < low + 2 * self.blocks), 1.0, 0.0))
        count = len(rows)
        rows += [rows[0]] * (-count % 16)
        stacked = jnp.concatenate(rows, axis=0)
        before = jnp.dot(stacked.astype(BF), self.before, preferred_element_type=F32)
        for n, key in enumerate(wanted):
            self.ranks[key] = jnp.where(
                stacked[n : n + 1] > 0, before[n : n + 1] * BS + self.lane, -1.0e4
            )

    def packed(self, dest, source, region):
        at = self.ranks[dest, source] + float(region * CAPACITY * BS)
        return jnp.where(self.slot == at, 1.0, 0.0).astype(BF)

    def pack(self, dest, source, region):
        return lax.dot_general(
            self.plain(dest, source),
            self.packed(dest, source, region),
            (((1,), (1,)), ((), ())),
            preferred_element_type=F32,
        )


FROM_ABOVE = ((0, -1), (0, -2), (1, -1))
FROM_BELOW = ((QUAD - 1, QUAD), (QUAD - 1, QUAD + 1), (QUAD - 2, QUAD))
TO_BELOW = tuple((d + QUAD, s + QUAD) for d, s in FROM_ABOVE)
TO_ABOVE = tuple((d - QUAD, s - QUAD) for d, s in FROM_BELOW)
TAKEN = (FROM_ABOVE, FROM_BELOW)
GIVEN = (TO_ABOVE, TO_BELOW)
REGIONS = len(FROM_ABOVE)


def step_codes(ch, place, step, steps, codes, along, cross):
    crow = codes.shape[0] // QUAD
    width = codes.shape[1]
    pick = place.core * (steps - 1) + step - 1
    row_id = lax.broadcasted_iota(jnp.int32, (crow, width), 0)
    start = 2 * HALO * ch
    above, below = above_below(
        place, along[pl.ds(start, 2 * crow), :], cross[pl.ds(start, 2 * crow), :]
    )

    def row(block):
        return jnp.sum(jnp.where(row_id == pick, block.astype(F32), 0.0), axis=0, keepdims=True)

    rows = [row(above[n * crow : (n + 1) * crow]) for n in range(2)]
    rows += [row(codes[pl.ds(strip * crow, crow), :]) for strip in range(QUAD)]
    rows += [row(below[n * crow : (n + 1) * crow]) for n in range(2)]
    return Codes(rows)


def own_sources(dest):
    return [source for source in range(QUAD) if abs(source - dest) <= REACH]


def choices_kernel(ch, step, steps, codes, along, cross, feat, local, own_out, part_out, *refs):
    place = Place()
    code = step_codes(ch, place, step, steps, codes, along, cross)
    code.rank_all(FROM_ABOVE + FROM_BELOW)
    half = HALO * ch
    strip = BS * ch
    width = feat.shape[1]
    for pair in range(0, QUAD, 2):
        left = [feat[pl.ds(source * strip, strip), :] for source in range(QUAD)]
        right = [
            jnp.concatenate([code.plain(pair + m, source) for m in range(2)], axis=1) for source in range(QUAD)
        ]
        got = jnp.dot(
            jnp.concatenate(left, axis=1), jnp.concatenate(right, axis=0), preferred_element_type=F32
        ).astype(BF)
        for m in range(2):
            local[pl.ds(half + (pair + m) * strip, strip), :] = got[:, m * width : (m + 1) * width]
    for dest, shift, at in ((-1, half, 0), (QUAD, 0, half + QUAD * strip)):
        sources = own_sources(dest)
        left = [feat[pl.ds(source * strip + shift, half), :] for source in sources]
        right = [code.plain(dest, source) for source in sources]
        local[pl.ds(at, half), :] = jnp.dot(
            jnp.concatenate(left, axis=1), jnp.concatenate(right, axis=0), preferred_element_type=F32
        ).astype(BF)
    for side in range(2):
        for m in range(2):
            value = [
                code.packed(dest, source, n) for n, (dest, source) in enumerate(TAKEN[side]) if dest == 2 * side + m
            ]
            refs[side][:, pl.ds(m * width, width)] = sum(value[1:], value[0])
    if step + 1 < steps:
        send_choices(code_of_next(ch, place, step, steps, codes, along, cross), refs[2:-1])
    split_results(ch, feat, own_out, part_out, refs[-1])


def code_of_next(ch, place, step, steps, codes, along, cross):
    code = step_codes(ch, place, step + 1, steps, codes, along, cross)
    code.rank_all(TO_ABOVE + TO_BELOW)
    return code


def given_sources(side):
    return sorted({source for _, source in GIVEN[side]})


def send_choices(code, outs):
    width = code.zero.shape[0]
    for side in range(2):
        blocks, edge = outs[2 * side : 2 * side + 2]
        for n, source in enumerate(given_sources(side)):
            total = sum(code.pack(d, source, at) for at, (d, origin) in enumerate(GIVEN[side]) if origin == source)
            blocks[pl.ds(n * width, width), :] = total.astype(BF)
        dest = side * (QUAD - 1)
        for n, source in enumerate(own_sources(dest)):
            edge[pl.ds(n * width, width), :] = code.plain(dest, source)


def choice_shapes(width):
    sent = []
    for side in range(2):
        sent += [(len(given_sources(side)) * width, width), (len(own_sources(side * (QUAD - 1))) * width, width)]
    return [(width, 2 * width)] * 2, sent


def join_rows(ch, join_mat, al, inp, extra=None):
    width = al.shape[1]
    sides = []
    for h in range(2):
        a, b = 2 * h * ch, (2 * h + 1) * ch
        sides.append(jnp.concatenate([al[a : a + ch], inp[a : a + ch], al[b : b + ch], inp[b : b + ch]], axis=0))
    mixed = jnp.dot(join_mat, jnp.concatenate(sides, axis=1), preferred_element_type=F32)
    rows = [mixed[q * ch : (q + 1) * ch, h * width : (h + 1) * width] for h in range(2) for q in range(2)]
    if extra is not None:
        rows = [row + extra[n * ch : (n + 1) * ch].astype(F32) for n, row in enumerate(rows)]
    return [row.astype(BF) for row in rows]


def fold_rows(ch):
    return BS * ch * REGIONS // (REGIONS + 1)


def pack_messages(ch, fout, par, join_mat, choices, inputs, sent, msg_e, msg_o):
    half = HALO * ch
    strip = BS * ch
    width = fout.shape[1]
    fold = fold_rows(ch)
    piece = strip - fold
    group = width // (REGIONS + 1)
    lane = lax.broadcasted_iota(jnp.int32, (piece, width), 1)
    for side in range(2):
        blocks, edge = choices[2 * side : 2 * side + 2]
        left = [fout[pl.ds(source * strip, strip), :] for source in given_sources(side)]
        got = jnp.dot(jnp.concatenate(left, axis=1), blocks[...], preferred_element_type=F32).astype(BF)
        for n in range(REGIONS):
            rolled = pltpu.roll(got[fold:], (REGIONS - n) * group, 1)
            sent[side, pl.ds(n * piece, piece), :] = jnp.where(
                lane < REGIONS * group, got[n * piece : (n + 1) * piece], rolled
            )
        shift = side * half
        left = [fout[pl.ds(source * strip + shift, half), :] for source in own_sources(side * (QUAD - 1))]
        al = jnp.dot(jnp.concatenate(left, axis=1), edge[...], preferred_element_type=F32).astype(BF)
        inp = jnp.zeros((half, width), BF) if inputs is None else inputs[side]
        for n, row in enumerate(join_rows(ch, join_mat, al, inp)):
            sent[side, pl.ds(fold + n * ch, ch), :] = row
    msg_e[...] = sent[1 - par]
    msg_o[...] = sent[par]


def unpack_message(ch, message, recv, side):
    strip = BS * ch
    width = message.shape[1]
    fold = fold_rows(ch)
    piece = strip - fold
    group = width // (REGIONS + 1)
    lane = lax.broadcasted_iota(jnp.int32, (piece, width), 1)
    recv[side, pl.ds(0, fold), :] = message[pl.ds(0, fold), :]
    total = None
    for n in range(REGIONS):
        rolled = pltpu.roll(message[pl.ds(n * piece, piece), :], (n + 1) * group, 1)
        total = rolled if total is None else jnp.where(lane < n * group, total, rolled)
    recv[side, pl.ds(fold, piece), :] = total


class Rows:
    def __init__(self, ch, width, top_ok, bottom_ok, count):
        lane = lax.broadcasted_iota(jnp.int32, (ch, width), 1)
        self.not_first = lane > 0
        self.not_last = lane < width - 1
        self.zero = jnp.zeros((ch, width), BF)
        self.top_ok = top_ok
        self.bottom_ok = bottom_ok
        self.count = count

    def active(self, value, row):
        act = leaky(value)
        if row < 0:
            act = jnp.where(self.top_ok, act, self.zero)
        if row >= self.count:
            act = jnp.where(self.bottom_ok, act, self.zero)
        return (
            jnp.where(self.not_first, pltpu.roll(act, 1, 1), self.zero),
            act,
            jnp.where(self.not_last, pltpu.roll(act, act.shape[1] - 1, 1), self.zero),
        )

    def put(self, buf, here, value, row):
        for n, act in enumerate(self.active(value, row)):
            buf[n, here, :] = act


OFF = 8


def here_of(row, ch, count=1):
    return pl.ds((row + OFF) * ch, count * ch)


def conv_layer(ch, weight, source, held, start, stop, emit):
    width = held.shape[1]
    for first in range(start, stop, 4):
        sides = [
            jnp.concatenate([source[n, here_of(first + 2 * h - 1, ch, 4), :] for n in range(3)], axis=0)
            for h in range(2)
        ]
        out = jnp.dot(weight, jnp.concatenate(sides, axis=1), preferred_element_type=F32)
        for h in range(2):
            for q in range(2):
                row = first + 2 * h + q
                total = held[here_of(row, ch), :].astype(F32)
                total += out[q * ch : (q + 1) * ch, h * width : (h + 1) * width]
                emit(row, total.astype(BF))


def join_first_rows(ch, join_mat, inp):
    width = inp.shape[1]
    mixed = jnp.dot(
        join_mat, jnp.concatenate([inp[: 2 * ch], inp[2 * ch :]], axis=1), preferred_element_type=F32
    ).astype(BF)
    return [mixed[q * ch : (q + 1) * ch, h * width : (h + 1) * width] for h in range(2) for q in range(2)]


def clear_outside(space, ch, rows, bufs):
    for buf in bufs:
        for row in (-HALO - 1, rows + HALO):
            for n in range(3):
                buf[n, here_of(row, ch), :] = space.zero


def conv_layers(ch, conv, space, rows, act_a, act_b, held, fout):
    layers = conv.shape[0]
    source, target = act_a, act_b
    for layer in range(layers):
        need = layers - 1 - layer
        reach = -(-need // 2) * 2
        start, stop = -reach, rows + reach
        if (stop - start) % 4:
            start, stop = -HALO, rows + HALO

        def emit(row, value, layer=layer, target=target):
            if layer < layers - 1:
                held[here_of(row, ch), :] = value
                space.put(target, here_of(row, ch), value, row)
            else:
                fout[pl.ds(row * ch, ch), :] = value

        conv_layer(ch, conv[layer], source, held, start, stop, emit)
        source, target = target, source


def first_kernel(ch, steps, *refs):
    xq, along, cross, join, join_both, conv, codes, far_in, *refs = refs
    fout, msg_e, msg_o, far_out, act_a, act_b, held, sent, *choices = refs
    half = HALO * ch
    rows = QUAD * BS
    place = Place()
    space = Rows(ch, xq.shape[1], jnp.logical_not(place.top), jnp.logical_not(place.bottom), rows)
    send_choices(code_of_next(ch, place, 0, steps, codes, along, cross), choices)
    above, below = above_below(place, along[pl.ds(0, half), :], cross[pl.ds(0, half), :])
    clear_outside(space, ch, rows, (act_a, act_b))
    join_mat = join[...]
    for first in range(-HALO, rows + HALO, 4):
        inp = above if first < 0 else below if first >= rows else xq[pl.ds(first * ch, 4 * ch), :]
        for n, value in enumerate(join_first_rows(ch, join_mat, inp)):
            held[here_of(first + n, ch), :] = value
            space.put(act_a, here_of(first + n, ch), value, first + n)
    conv_layers(ch, conv, space, rows, act_a, act_b, held, fout)
    pack_messages(ch, fout, place.odd, join_both[...], choices, None, sent, msg_e, msg_o)


def step_kernel(ch, step, steps, *refs):
    strip = BS * ch
    half = HALO * ch
    last = step == steps - 1
    refs = list(refs)

    def take(count):
        taken = refs[:count]
        del refs[:count]
        return taken

    xq, along, cross, join, conv = take(5)
    feat_e, feat_o = take(2)
    choices = take(2 if last else 6)
    before, out_a, out_b = take(3)
    (local,) = take(1)
    if last:
        (x_inner,) = take(1)
    else:
        next_edges, fout, msg_e, msg_o = take(4)
    own_out, part_out = take(2) if last else (None, None)
    out_f, out_g = take(2)
    tmp, act_a, act_b, held, sems, aligned, recv = take(7)
    if last:
        (fout,) = take(1)
    else:
        (sent,) = take(1)
    width = xq.shape[-1]
    place = Place()
    par = place.odd
    core = place.core
    rows = 2 * BS if last else QUAD * BS
    left_side = place.side == 0

    copies = own_copies(strip, step - 1, steps, before, out_f, out_g, sems.at[0])
    for n, copy in copies:
        pl.when(core == n)(copy.start)

    def choose(which, one, two):
        return jnp.where(which, one.astype(F32), two.astype(F32)).astype(BF)

    fold = fold_rows(ch)
    zero = jnp.zeros((half, width), BF)
    one, two = feat_e[pl.ds(fold, half), :], feat_o[pl.ds(fold, half), :]
    over_sent, under_sent = choose(par == 1, one, two), choose(par == 1, two, one)
    over, under = zero, zero
    if step == 1:
        over, under = above_below(place, along[pl.ds(half, half), :], cross[pl.ds(half, half), :])
    if last:
        inner = x_inner[...]
        over, under = choose(left_side, zero, inner), choose(left_side, inner, zero)
        over_sent, under_sent = choose(left_side, over_sent, zero), choose(left_side, zero, under_sent)
    unpack_message(ch, feat_e, recv, 1 - par)
    unpack_message(ch, feat_o, recv, par)
    for edge in (0, half + QUAD * strip):
        aligned[pl.ds(edge, half), :] = local[pl.ds(edge, half), :]
    for side in range(2):
        got = jnp.dot(recv[side], choices[side][...], preferred_element_type=F32)
        for m in range(2):
            here = pl.ds(half + (2 * side + m) * strip, strip)
            both = got[:, m * width : (m + 1) * width] + local[here, :].astype(F32)
            aligned[here, :] = both.astype(BF)

    space = Rows(ch, width, jnp.logical_not(place.top), jnp.logical_not(place.bottom), rows)
    if last:
        space.top_ok = space.top_ok | (place.side == 1)
        space.bottom_ok = space.bottom_ok | left_side
    clear_outside(space, ch, rows, (act_a, act_b))
    join_mat = join[...]
    for first in range(-HALO, rows + HALO, 4):
        inp, extra = xq, None
        if first < 0:
            inp, extra = over, over_sent
        elif first >= rows:
            inp, extra = under, under_sent
        else:
            inp = xq[pl.ds(first * ch, 4 * ch), :]
        at = (first + HALO) * ch
        if last:
            at = pl.multiple_of(place.side * (2 * strip) + at, half)
        al = aligned[pl.ds(at, half), :]
        for n, value in enumerate(join_rows(ch, join_mat, al, inp, extra)):
            held[here_of(first + n, ch), :] = value
            space.put(act_a, here_of(first + n, ch), value, first + n)

    conv_layers(ch, conv, space, rows, act_a, act_b, held, fout)
    if not last:
        pack_messages(ch, fout, par, join_mat, choices[2:], next_edges, sent, msg_e, msg_o)
    else:
        channels_first(fout, pl.multiple_of(core * strip, strip), own_out, tmp, ch)
        channels_first(fout, pl.multiple_of((core ^ 1) * strip, strip), part_out, tmp, ch)
    for n, copy in copies:
        pl.when(core == n)(copy.wait)


def parts_kernel(*refs):
    out = refs[-1]
    strip = refs[0].shape[0]
    for n in range(out.shape[0] // strip):
        out[pl.ds(n * strip, strip), :] = refs[n][...]


def own_copies(strip, step, steps, own, out_f, out_g, sem):
    return [
        (0, pltpu.make_async_copy(own, out_f.at[pl.ds(step * strip, strip)], sem)),
        (1, pltpu.make_async_copy(own, out_g.at[pl.ds((steps - 1 - step) * strip, strip)], sem)),
    ]


def back_copies(strip, step, steps, back, out_f, out_g, sem):
    return [
        (0, pltpu.make_async_copy(back, out_g.at[pl.ds((steps - 1 - step) * strip, strip)], sem)),
        (1, pltpu.make_async_copy(back, out_f.at[pl.ds(step * strip, strip)], sem)),
    ]


def run_copies(copies):
    core = Place().core
    for n, copy in copies:
        pl.when(core == n)(copy.start)
    for n, copy in copies:
        pl.when(core == n)(copy.wait)


def finish_own_kernel(strip, steps, own, backs, out_a, out_b, out_f, out_g, sems):
    copies = own_copies(strip, steps - 1, steps, own, out_f, out_g, sems.at[0])
    for step in range(steps - 1):
        before = backs.at[pl.ds(step * strip, strip)]
        copies += back_copies(strip, step, steps, before, out_f, out_g, sems.at[1 + step])
    run_copies(copies)


def finish_kernel(strip, steps, back, out_a, out_b, out_f, out_g, sem):
    run_copies(back_copies(strip, steps - 1, steps, back, out_f, out_g, sem))


def weights_kernel(conv, join, wide, join_both, join_first):
    core = Place().core
    layers, ch = conv.shape[1], conv.shape[3]
    zero = jnp.zeros((ch, ch), BF)
    for layer in range(layers):
        for dx in range(3):
            taps = [conv[core, layer, 3 * dy + dx] for dy in range(3)]
            for q in range(2):
                line = [zero] * q + taps + [zero] * (1 - q)
                wide[layer, pl.ds(q * ch, ch), pl.ds(dx * 4 * ch, 4 * ch)] = jnp.concatenate(line, axis=1)
    both = join[core]
    none = jnp.zeros_like(both)
    join_both[pl.ds(0, ch), :] = jnp.concatenate([both, none], axis=1)
    join_both[pl.ds(ch, ch), :] = jnp.concatenate([none, both], axis=1)
    enter = both[:, ch:]
    join_first[pl.ds(0, ch), :] = jnp.concatenate([enter, zero], axis=1)
    join_first[pl.ds(ch, ch), :] = jnp.concatenate([zero, enter], axis=1)


VMEM = pl.BlockSpec(memory_space=pltpu.VMEM)
ANY = pl.BlockSpec(memory_space=pl.ANY)
HBM = pl.BlockSpec(memory_space=pltpu.HBM)


def call(kernel, name, args, outs, scratch=(), flops=0, in_any=(), out_any=(), aliases=None, in_hbm=(), free=False):
    args = [pltpu.with_memory_space_constraint(a, pltpu.HBM) if n in in_hbm else a for n, a in enumerate(args)]
    return pl.pallas_call(
        kernel,
        out_shape=[jax.ShapeDtypeStruct(o, BF) for o in outs],
        in_specs=[HBM if n in in_hbm else ANY if n in in_any else VMEM for n in range(len(args))],
        out_specs=[ANY if n in out_any else VMEM for n in range(len(outs))],
        scratch_shapes=list(scratch),
        input_output_aliases=aliases or {},
        compiler_params=pltpu.CompilerParams(vmem_limit_bytes=32 << 20),
        cost_estimate=pl.CostEstimate(
            flops=flops,
            bytes_accessed=0 if free else sum(a.size * a.dtype.itemsize for a in args),
            transcendentals=0,
        ),
        name=name,
    )(*args)


def sooner(value, *after):
    return pl.pallas_call(
        lambda *refs: None,
        out_shape=jax.ShapeDtypeStruct(value.shape, value.dtype),
        in_specs=[ANY] * (1 + len(after)),
        out_specs=ANY,
        input_output_aliases={0: 0},
        compiler_params=pltpu.CompilerParams(vmem_limit_bytes=1 << 20),
        cost_estimate=pl.CostEstimate(flops=0, bytes_accessed=2 << 20, transcendentals=0),
        name="sooner",
    )(value, *after)


def pairings(count, idle):
    groups = count // QUAD
    out = []
    for parity in range(2):
        pairs = []
        for i in range(count):
            g = i // QUAD
            other = g + 1 if g % 2 == parity else g - 1
            pairs.append((i, i % QUAD + other * QUAD if 0 <= other < groups else i ^ idle))
        out.append(pairs)
    return out


def edge_pairings(count):
    groups = count // QUAD
    along, cross = [], []
    for i in range(count):
        g, side, core = i // QUAD, i % QUAD // 2, i % 2
        if side == 0:
            along += [(i, i - QUAD)] if g > 0 else []
            cross.append((i, i - QUAD + 2 if g > 0 else i ^ 1))
        else:
            along += [(i, i + QUAD)] if g < groups - 1 else []
            cross.append((i, i + QUAD - 2 if g < groups - 1 else i ^ 1))
    return along, cross


def on_device(frames, motion_forward, motion_backward, join_weight, conv_weight):
    steps, ch, strip_rows, width = frames.shape
    strip = strip_rows * ch
    half = HALO * ch
    crow = 16
    count = lax.axis_size("tiles")
    even, odd = pairings(count, 1)
    along_pairs, cross_pairs = edge_pairings(count)

    def near(k):
        return [(i, i ^ k) for i in range(count)]

    def send(value, pairs):
        return lax.ppermute(value, "tiles", pairs)

    tmp = pltpu.VMEM((strip, width), F32)
    piece = (strip, width)
    rows = QUAD * BS
    message = (fold_rows(ch) + half, width)
    feature = (rows * ch, width)
    whole = (steps * strip, width)
    flat = frames.reshape(steps, strip, width)
    later = ((steps - 1) * strip, width)
    first = (strip + crow, width)
    mine, mine_edge, other = call(
        functools.partial(pack_first_kernel, ch, crow),
        "pack_first",
        (flat, motion_forward, motion_backward),
        [first, (half, width), (strip + crow + half, width)],
        [
            pltpu.VMEM((2, *piece), BF),
            pltpu.VMEM((2, *motion_forward.shape), jnp.int32),
            tmp,
            pltpu.SemaphoreType.DMA((6,)),
        ],
        in_hbm=(0, 1, 2),
    )
    (rest,) = call(
        pack_rest_kernel,
        "pack_rest",
        (flat, mine),
        [later],
        [pltpu.SemaphoreType.DMA((steps,))],
        in_hbm=(0,),
        in_any=(1,),
        out_any=(0,),
    )
    pair, edge, rest = call(
        functools.partial(pair_first_kernel, ch, crow),
        "pair_first",
        (mine, mine_edge, send(other, near(1)), rest),
        [(2 * (strip + crow), width), (2 * (half + crow), width), later],
        [tmp],
        in_any=(3,),
        out_any=(2,),
        aliases={3: 2},
    )
    received = send(pair, near(2))
    swapped = send(rest, near(1))
    along, cross = sooner(send(edge, along_pairs)), send(edge, cross_pairs)
    far_pairs = 2 * (steps - 3) * strip
    pair_near, pair_far, pair_last = call(
        functools.partial(pair_kernel, ch),
        "pair_rest",
        (flat, swapped),
        [(2 * strip + half, width), (far_pairs + (steps - 2) * half, width), (2 * strip, width)],
        [tmp, pltpu.SemaphoreType.DMA((2 * steps,))],
        in_hbm=(0,),
        in_any=(1,),
    )
    layers = conv_weight.shape[1]
    conv, join_both, join_first = call(
        weights_kernel,
        "weights",
        (conv_weight, join_weight),
        [(layers, 2 * ch, 12 * ch), (2 * ch, 4 * ch), (2 * ch, 2 * ch)],
        free=True,
    )
    xq, codes, pair_near = call(
        functools.partial(gather_first_kernel, ch, crow),
        "gather_first",
        (pair, received, conv, pair_near),
        [feature, (QUAD * crow, width), pair_near.shape],
        [tmp],
        in_any=(2, 3),
        out_any=(2,),
        aliases={3: 2},
        free=True,
    )
    received_near = send(pair_near, near(2))

    wide_act = pltpu.VMEM((3, (rows + 16) * ch, width), BF)
    flops = 2 * (rows + 2 * HALO) * width * ch * ch * 9 * layers
    part_shapes, sent_shapes = choice_shapes(width)
    acts = [wide_act, wide_act, pltpu.VMEM(((rows + 16) * ch, width), BF)]
    feat, msg_e, msg_o, pair_far = call(
        functools.partial(first_kernel, ch, steps),
        "refine_first",
        (xq, along, cross, join_first, join_both, conv, codes, pair_far),
        [feature, message, message, pair_far.shape],
        [*acts, pltpu.VMEM((2, *message), BF)] + [pltpu.VMEM(shape, BF) for shape in sent_shapes],
        flops,
        in_any=(7,),
        out_any=(3,),
        aliases={7: 3},
    )
    feat_e, feat_o = send(msg_e, even), send(msg_o, odd)
    parts = []
    received_far = send(pair_far, near(2))
    outputs = call(lambda after, a, b: None, "results", (feat,), [whole, whole], in_any=(0,), out_any=(0, 1), free=True)

    def choices_of(step):
        return call(
            functools.partial(choices_kernel, ch, step, steps),
            "choices",
            (codes, along, cross, feat),
            [((rows + 2 * HALO) * ch, width), piece, piece] + part_shapes + (sent_shapes if step + 1 < steps else []),
            [tmp],
        )

    def frame_of(step):
        if step == steps - 1:
            kernel = functools.partial(gather_last_kernel, ch, far_pairs + (steps - 3) * half)
            args, outs = (pair_last, received_far, feat), [(2 * strip, width), (half, width)]
        elif step == 1:
            kernel = functools.partial(gather_kernel, ch, 0, 2 * strip)
            args, outs = (pair_near, received_near, feat), [feature, (2, half, width)]
        else:
            kernel = functools.partial(gather_kernel, ch, 2 * (step - 2) * strip, far_pairs + (step - 2) * half)
            args, outs = (pair_far, received_far, feat), [feature, (2, half, width)]
        return call(kernel, "gather", args, outs, [tmp], in_any=(2,))

    for step in range(1, steps):
        last = step == steps - 1
        local, own, part, *choices = choices_of(step)
        x_now, beside = frame_of(step)
        feat_e = sooner(feat_e, x_now) if step > 1 else sooner(feat_e)
        parts = parts + [part]
        args = [x_now, along, cross, join_both, conv, feat_e, feat_o, *choices, own, *outputs]
        many = len(args)
        outs = [] if last else [feature, message, message]
        outs += [piece, piece, whole, whole] if last else [whole, whole]
        in_any = [many - 3, many - 2, many - 1]
        out_any = [len(outs) - 2, len(outs) - 1]
        aliases = {many - 2: len(outs) - 2, many - 1: len(outs) - 1}
        args += [local, beside]
        scratch = [tmp, *acts, pltpu.SemaphoreType.DMA((1,))]
        scratch += [pltpu.VMEM(((rows + 2 * HALO) * ch, width), BF), pltpu.VMEM((2, strip, width), BF)]
        scratch += [pltpu.VMEM((2 * strip, width) if last else (2, *message), BF)]
        if last:
            (before,) = call(
                parts_kernel,
                "parts",
                (*parts, feat_e, feat_o),
                [(len(parts) * strip, width)],
                in_any=(len(parts), len(parts) + 1),
            )
            backs = send(before, near(1))
        results = call(
            functools.partial(step_kernel, ch, step, steps),
            "refine",
            args,
            outs,
            scratch,
            flops,
            in_any=in_any,
            out_any=out_any,
            aliases=aliases,
        )
        if not last:
            feat, msg_e, msg_o, *results = results
            feat_e, feat_o = send(msg_e, even), send(msg_o, odd)
        if last:
            own, part, *results = results
        outputs = results
    back = send(part, near(1))

    outputs = call(
        functools.partial(finish_own_kernel, strip, steps),
        "finish_own",
        [own, backs, *outputs],
        [whole] * 2,
        [pltpu.SemaphoreType.DMA((steps,))],
        in_any=(0, 1, 2, 3),
        out_any=(0, 1),
        aliases={2: 0, 3: 1},
    )
    outputs = call(
        functools.partial(finish_kernel, strip, steps),
        "finish",
        [back, *outputs],
        [whole] * 2,
        [pltpu.SemaphoreType.DMA],
        in_any=(0, 1, 2),
        out_any=(0, 1),
        aliases={1: 0, 2: 1},
    )
    return tuple(o.reshape(frames.shape) for o in outputs)


def solution(mesh):
    return jax.shard_map(
        on_device,
        mesh=mesh,
        in_specs=(
            P(None, None, ("clips", "tiles"), None),
            P(None, ("clips", "tiles")),
            P(None, ("clips", "tiles")),
            P(),
            P(),
        ),
        out_specs=(
            P(None, None, ("clips", "tiles"), None),
            P(None, None, ("clips", "tiles"), None),
        ),
        check_vma=False,
    )
```

```python
import functools

import jax
import jax.numpy as jnp
from jax import lax
from jax.experimental import pallas as pl
from jax.experimental.pallas import tpu as pltpu
from jax.sharding import PartitionSpec as P

BS = 8
REACH = 2
QUAD = 4
HALO = 4
CAPACITY = 4
BF = jnp.bfloat16
F32 = jnp.float32


class Place:
    def __init__(self):
        me = lax.axis_index("tiles")
        self.me = me
        self.strip = me % QUAD
        self.core = me % 2
        self.side = self.strip // 2
        self.group = me // QUAD
        self.odd = self.group % 2
        self.top = self.group == 0
        self.bottom = self.group == lax.axis_size("tiles") // QUAD - 1


def leaky(value):
    widened = value.astype(F32)
    return jnp.maximum(widened, 0.1 * widened).astype(BF)


def rows_first(src, src_start, dst, dst_start, tmp, ch):
    tmp[...] = src[pl.ds(src_start, BS * ch), :].astype(F32)
    for r in range(BS):
        row = tmp[pl.ds(r, ch, stride=BS), :]
        dst[pl.ds(dst_start + r * ch, ch), :] = row.astype(BF)


def channels_first(src, src_start, dst, tmp, ch):
    for r in range(BS):
        tmp[pl.ds(r, ch, stride=BS), :] = src[pl.ds(src_start + r * ch, ch), :].astype(F32)
    dst[...] = tmp[...].astype(BF)


def pack_first_kernel(ch, crow, frames, motion_f, motion_b, mine, mine_edge, other, following, motion_buf, tmp, sems):
    place = Place()
    steps, strip = frames.shape[:2]
    half = HALO * ch
    core = place.core
    outs = (mine, other)
    lists = [
        pltpu.make_async_copy(motion, motion_buf.at[n], sems.at[4 + n]) for n, motion in enumerate((motion_f, motion_b))
    ]
    copies = []
    for n in range(2):
        back = 1 - core if n else core
        copies.append(frame_copy(frames, 0, back, outs[n].at[pl.ds(0, strip)], sems.at[n]))
        copies.append(frame_copy(frames, 1, back, following.at[n], sems.at[2 + n]))
    for copy in lists + copies:
        copy.start()
    for copy in lists:
        copy.wait()
    blocks = motion_f.shape[1]
    width = mine.shape[1]
    column = lax.broadcasted_iota(jnp.int32, motion_f.shape, 1)
    spread = jnp.where(
        lax.broadcasted_iota(jnp.int32, (blocks, width), 1) // BS
        == lax.broadcasted_iota(jnp.int32, (blocks, width), 0),
        1.0,
        0.0,
    ).astype(BF)
    wides = []
    for n in range(2):
        taken = motion_buf[n]
        across = taken // blocks
        code = (across - place.me + REACH) * (2 * blocks) + (taken - across * blocks - column + blocks - 1)
        wide = jnp.dot(code.astype(BF), spread, preferred_element_type=F32).astype(BF)
        frames_order = range(steps - 1) if n == 0 else range(steps - 2, -1, -1)
        wides += [wide[frame : frame + 1] for frame in frames_order]
    wides.append(jnp.zeros((crow - len(wides), width), BF))
    code = jnp.concatenate(wides, axis=0)
    for out in outs:
        out[pl.ds(strip, crow), :] = code
    for copy in copies:
        copy.wait()
    for n, (out, start) in enumerate(((mine_edge, 0), (other, strip + crow))):
        edge_of(place.side == 0, ch, following[n], out, start, tmp)


def edge_of(top, ch, strip_values, out, start, tmp):
    tmp[...] = strip_values.astype(F32)
    for r in range(HALO):
        one, two = tmp[pl.ds(r, ch, stride=BS), :], tmp[pl.ds(BS - HALO + r, ch, stride=BS), :]
        out[pl.ds(start + r * ch, ch), :] = jnp.where(top, one, two).astype(BF)


def pair_first_kernel(ch, crow, mine, mine_edge, partner, rest_in, out, edge, rest_out, tmp):
    place = Place()
    strip = BS * ch
    half = HALO * ch
    own = place.core == place.side
    first = jnp.where(own, mine[pl.ds(0, strip), :].astype(F32), partner[pl.ds(0, strip), :].astype(F32))
    edge_of(place.side == 0, ch, first, edge, 0, tmp)
    second = partner[pl.ds(strip + crow, half), :].astype(F32)
    edge[pl.ds(half, half), :] = jnp.where(own, mine_edge[...].astype(F32), second).astype(BF)
    for n, piece in enumerate((mine, partner)):
        at = place.core ^ n
        out[pl.ds(pl.multiple_of(at * strip, strip), strip), :] = piece[pl.ds(0, strip), :]
        for ref, start in ((out, 2 * strip), (edge, 2 * half)):
            ref[pl.ds(pl.multiple_of(start + at * crow, crow), crow), :] = piece[pl.ds(strip, crow), :]


def above_below(place, along, cross):
    left = place.side == 0
    along, cross = along.astype(F32), cross.astype(F32)
    return jnp.where(left, cross, along).astype(BF), jnp.where(left, along, cross).astype(BF)


def pack_rest_kernel(frames, after, rest, sems):
    steps, strip = frames.shape[:2]
    core = Place().core
    copies = [
        frame_copy(frames, step, 1 - core, rest.at[pl.ds((step - 1) * strip, strip)], sems.at[step])
        for step in range(1, steps)
    ]
    for copy in copies:
        copy.start()
    for copy in copies:
        copy.wait()


def frame_copy(frames, step, back, out, sem):
    steps = frames.shape[0]
    return pltpu.make_async_copy(frames.at[step + back * (steps - 1 - 2 * step)], out, sem)


def pair_copies(frames, swapped, core, first, count, out, sems):
    strip = frames.shape[1]
    copies = []
    for n in range(count):
        step = first + n
        own = out.at[pl.ds(pl.multiple_of((2 * n + core) * strip, strip), strip)]
        his = out.at[pl.ds(pl.multiple_of((2 * n + 1 - core) * strip, strip), strip)]
        copies.append(frame_copy(frames, step, core, own, sems.at[2 * n]))
        copies.append(
            pltpu.make_async_copy(swapped.at[pl.ds((step - 1) * strip, strip)], his, sems.at[2 * n + 1])
        )
    return copies


def edge_rows(place, ch, pair, outer, out, start, tmp):
    strip = BS * ch
    one, two = pair[pl.ds(0, strip), :].astype(F32), pair[pl.ds(strip, strip), :].astype(F32)
    left = place.side == 0
    if outer:
        edge_of(left, ch, jnp.where(left, one, two), out, start, tmp)
    else:
        edge_of(jnp.logical_not(left), ch, jnp.where(left, two, one), out, start, tmp)


def pair_kernel(ch, frames, swapped, near_out, far_out, last_out, tmp, sems):
    place = Place()
    steps, strip = frames.shape[:2]
    half = HALO * ch
    between = range(2, steps - 1)
    pairs = {1: near_out.at[pl.ds(0, 2 * strip)], steps - 1: last_out}
    for n, step in enumerate(between):
        pairs[step] = far_out.at[pl.ds(2 * n * strip, 2 * strip)]
    copies = []
    for step, out in pairs.items():
        copies += pair_copies(frames, swapped, place.core, step, 1, out, sems.at[pl.ds(2 * step, 2)])
    for copy in copies:
        copy.start()
    for copy in copies:
        copy.wait()
    edge_rows(place, ch, pairs[2], True, near_out, 2 * strip, tmp)
    at = 2 * len(between) * strip
    for step in range(3, steps):
        edge_rows(place, ch, pairs[step], True, far_out, at, tmp)
        at += half
    edge_rows(place, ch, last_out, False, far_out, at, tmp)


def gather_first_kernel(ch, crow, pair, received, conv, near_in, xq, codes, near_out, tmp):
    place = Place()
    strip = BS * ch
    for n, piece in enumerate((pair, received)):
        side = place.side ^ n
        for m in range(2):
            at = side * 2 + m
            rows_first(piece, m * strip, xq, pl.multiple_of(at * strip, strip), tmp, ch)
            code_at = pl.multiple_of(at * crow, crow)
            codes[pl.ds(code_at, crow), :] = piece[pl.ds(2 * strip + m * crow, crow), :]


def gather_kernel(ch, pair_at, edge_at, pair, received, after, xq, edges, tmp):
    strip = BS * ch
    half = HALO * ch
    side = Place().side
    for n, piece in enumerate((pair, received)):
        for m in range(2):
            start = ((side + n) % 2 * 2 + m) * strip
            rows_first(piece, pair_at + m * strip, xq, pl.multiple_of(start, strip), tmp, ch)
        edges[side ^ n] = piece[pl.ds(edge_at, half), :]


def split_results(ch, feat, own_out, part_out, tmp):
    strip = BS * ch
    own = Place().strip
    channels_first(feat, pl.multiple_of(own * strip, strip), own_out, tmp, ch)
    channels_first(feat, pl.multiple_of((own ^ 1) * strip, strip), part_out, tmp, ch)


def gather_last_kernel(ch, inner_at, pair, received, after, xq, inner, tmp):
    strip = BS * ch
    for m in range(2):
        rows_first(pair, m * strip, xq, m * strip, tmp, ch)
    inner[...] = received[pl.ds(inner_at, HALO * ch), :]


class Codes:
    def __init__(self, rows):
        width = rows[0].shape[1]
        self.rows = rows
        self.blocks = width // BS
        k_id = lax.broadcasted_iota(jnp.int32, (width, width), 0)
        l_id = lax.broadcasted_iota(jnp.int32, (width, width), 1)
        base = (k_id // BS - l_id // BS + self.blocks - 1).astype(F32)
        self.base = jnp.where(k_id % BS == l_id % BS, base, -1.0e4)
        self.slot = k_id.astype(F32)
        self.before = jnp.where((k_id % BS == 0) & (k_id // BS < l_id // BS), 1.0, 0.0).astype(BF)
        self.lane = (lax.broadcasted_iota(jnp.int32, (1, width), 1) % BS).astype(F32)
        self.zero = jnp.zeros((width, width), BF)
        self.ranks = {}

    def plain(self, dest, source):
        ds = source - dest
        if abs(ds) > REACH:
            return self.zero
        shift = float((ds + REACH) * 2 * self.blocks)
        return jnp.where(self.rows[dest + 2] - shift == self.base, 1.0, 0.0).astype(BF)

    def rank_all(self, wanted):
        rows = []
        for dest, source in wanted:
            low = float((source - dest + REACH) * 2 * self.blocks)
            code = self.rows[dest + 2]
            rows.append(jnp.where((code >= low) & (code < low + 2 * self.blocks), 1.0, 0.0))
        count = len(rows)
        rows += [rows[0]] * (-count % 16)
        stacked = jnp.concatenate(rows, axis=0)
        before = jnp.dot(stacked.astype(BF), self.before, preferred_element_type=F32)
        for n, key in enumerate(wanted):
            self.ranks[key] = jnp.where(
                stacked[n : n + 1] > 0, before[n : n + 1] * BS + self.lane, -1.0e4
            )

    def packed(self, dest, source, region):
        at = self.ranks[dest, source] + float(region * CAPACITY * BS)
        return jnp.where(self.slot == at, 1.0, 0.0).astype(BF)

    def pack(self, dest, source, region):
        return lax.dot_general(
            self.plain(dest, source),
            self.packed(dest, source, region),
            (((1,), (1,)), ((), ())),
            preferred_element_type=F32,
        )


FROM_ABOVE = ((0, -1), (0, -2), (1, -1))
FROM_BELOW = ((QUAD - 1, QUAD), (QUAD - 1, QUAD + 1), (QUAD - 2, QUAD))
TO_BELOW = tuple((d + QUAD, s + QUAD) for d, s in FROM_ABOVE)
TO_ABOVE = tuple((d - QUAD, s - QUAD) for d, s in FROM_BELOW)
TAKEN = (FROM_ABOVE, FROM_BELOW)
GIVEN = (TO_ABOVE, TO_BELOW)
REGIONS = len(FROM_ABOVE)


def step_codes(ch, place, step, steps, codes, along, cross):
    crow = codes.shape[0] // QUAD
    width = codes.shape[1]
    pick = place.core * (steps - 1) + step - 1
    row_id = lax.broadcasted_iota(jnp.int32, (crow, width), 0)
    start = 2 * HALO * ch
    above, below = above_below(
        place, along[pl.ds(start, 2 * crow), :], cross[pl.ds(start, 2 * crow), :]
    )

    def row(block):
        return jnp.sum(jnp.where(row_id == pick, block.astype(F32), 0.0), axis=0, keepdims=True)

    rows = [row(above[n * crow : (n + 1) * crow]) for n in range(2)]
    rows += [row(codes[pl.ds(strip * crow, crow), :]) for strip in range(QUAD)]
    rows += [row(below[n * crow : (n + 1) * crow]) for n in range(2)]
    return Codes(rows)


def own_sources(dest):
    return [source for source in range(QUAD) if abs(source - dest) <= REACH]


def choices_kernel(ch, step, steps, codes, along, cross, feat, local, own_out, part_out, *refs):
    place = Place()
    code = step_codes(ch, place, step, steps, codes, along, cross)
    code.rank_all(FROM_ABOVE + FROM_BELOW)
    half = HALO * ch
    strip = BS * ch
    width = feat.shape[1]
    for pair in range(0, QUAD, 2):
        left = [feat[pl.ds(source * strip, strip), :] for source in range(QUAD)]
        right = [
            jnp.concatenate([code.plain(pair + m, source) for m in range(2)], axis=1) for source in range(QUAD)
        ]
        got = jnp.dot(
            jnp.concatenate(left, axis=1), jnp.concatenate(right, axis=0), preferred_element_type=F32
        ).astype(BF)
        for m in range(2):
            local[pl.ds(half + (pair + m) * strip, strip), :] = got[:, m * width : (m + 1) * width]
    for dest, shift, at in ((-1, half, 0), (QUAD, 0, half + QUAD * strip)):
        sources = own_sources(dest)
        left = [feat[pl.ds(source * strip + shift, half), :] for source in sources]
        right = [code.plain(dest, source) for source in sources]
        local[pl.ds(at, half), :] = jnp.dot(
            jnp.concatenate(left, axis=1), jnp.concatenate(right, axis=0), preferred_element_type=F32
        ).astype(BF)
    for side in range(2):
        for m in range(2):
            value = [
                code.packed(dest, source, n) for n, (dest, source) in enumerate(TAKEN[side]) if dest == 2 * side + m
            ]
            refs[side][:, pl.ds(m * width, width)] = sum(value[1:], value[0])
    if step + 1 < steps:
        send_choices(code_of_next(ch, place, step, steps, codes, along, cross), refs[2:-1])
    split_results(ch, feat, own_out, part_out, refs[-1])


def code_of_next(ch, place, step, steps, codes, along, cross):
    code = step_codes(ch, place, step + 1, steps, codes, along, cross)
    code.rank_all(TO_ABOVE + TO_BELOW)
    return code


def given_sources(side):
    return sorted({source for _, source in GIVEN[side]})


def send_choices(code, outs):
    width = code.zero.shape[0]
    for side in range(2):
        blocks, edge = outs[2 * side : 2 * side + 2]
        for n, source in enumerate(given_sources(side)):
            total = sum(code.pack(d, source, at) for at, (d, origin) in enumerate(GIVEN[side]) if origin == source)
            blocks[pl.ds(n * width, width), :] = total.astype(BF)
        dest = side * (QUAD - 1)
        for n, source in enumerate(own_sources(dest)):
            edge[pl.ds(n * width, width), :] = code.plain(dest, source)


def choice_shapes(width):
    sent = []
    for side in range(2):
        sent += [(len(given_sources(side)) * width, width), (len(own_sources(side * (QUAD - 1))) * width, width)]
    return [(width, 2 * width)] * 2, sent


def join_rows(ch, join_mat, al, inp, extra=None):
    width = al.shape[1]
    sides = []
    for h in range(2):
        a, b = 2 * h * ch, (2 * h + 1) * ch
        sides.append(jnp.concatenate([al[a : a + ch], inp[a : a + ch], al[b : b + ch], inp[b : b + ch]], axis=0))
    mixed = jnp.dot(join_mat, jnp.concatenate(sides, axis=1), preferred_element_type=F32)
    rows = [mixed[q * ch : (q + 1) * ch, h * width : (h + 1) * width] for h in range(2) for q in range(2)]
    if extra is not None:
        rows = [row + extra[n * ch : (n + 1) * ch].astype(F32) for n, row in enumerate(rows)]
    return [row.astype(BF) for row in rows]


def fold_rows(ch):
    return BS * ch * REGIONS // (REGIONS + 1)


def pack_messages(ch, fout, par, join_mat, choices, inputs, sent, msg_e, msg_o):
    half = HALO * ch
    strip = BS * ch
    width = fout.shape[1]
    fold = fold_rows(ch)
    piece = strip - fold
    group = width // (REGIONS + 1)
    lane = lax.broadcasted_iota(jnp.int32, (piece, width), 1)
    for side in range(2):
        blocks, edge = choices[2 * side : 2 * side + 2]
        left = [fout[pl.ds(source * strip, strip), :] for source in given_sources(side)]
        got = jnp.dot(jnp.concatenate(left, axis=1), blocks[...], preferred_element_type=F32).astype(BF)
        for n in range(REGIONS):
            rolled = pltpu.roll(got[fold:], (REGIONS - n) * group, 1)
            sent[side, pl.ds(n * piece, piece), :] = jnp.where(
                lane < REGIONS * group, got[n * piece : (n + 1) * piece], rolled
            )
        shift = side * half
        left = [fout[pl.ds(source * strip + shift, half), :] for source in own_sources(side * (QUAD - 1))]
        al = jnp.dot(jnp.concatenate(left, axis=1), edge[...], preferred_element_type=F32).astype(BF)
        inp = jnp.zeros((half, width), BF) if inputs is None else inputs[side]
        for n, row in enumerate(join_rows(ch, join_mat, al, inp)):
            sent[side, pl.ds(fold + n * ch, ch), :] = row
    msg_e[...] = sent[1 - par]
    msg_o[...] = sent[par]


def unpack_message(ch, message, recv, side):
    strip = BS * ch
    width = message.shape[1]
    fold = fold_rows(ch)
    piece = strip - fold
    group = width // (REGIONS + 1)
    lane = lax.broadcasted_iota(jnp.int32, (piece, width), 1)
    recv[side, pl.ds(0, fold), :] = message[pl.ds(0, fold), :]
    total = None
    for n in range(REGIONS):
        rolled = pltpu.roll(message[pl.ds(n * piece, piece), :], (n + 1) * group, 1)
        total = rolled if total is None else jnp.where(lane < n * group, total, rolled)
    recv[side, pl.ds(fold, piece), :] = total


class Rows:
    def __init__(self, ch, width, top_ok, bottom_ok, count):
        lane = lax.broadcasted_iota(jnp.int32, (ch, width), 1)
        self.not_first = lane > 0
        self.not_last = lane < width - 1
        self.zero = jnp.zeros((ch, width), BF)
        self.top_ok = top_ok
        self.bottom_ok = bottom_ok
        self.count = count

    def active(self, value, row):
        act = leaky(value)
        if row < 0:
            act = jnp.where(self.top_ok, act, self.zero)
        if row >= self.count:
            act = jnp.where(self.bottom_ok, act, self.zero)
        return (
            jnp.where(self.not_first, pltpu.roll(act, 1, 1), self.zero),
            act,
            jnp.where(self.not_last, pltpu.roll(act, act.shape[1] - 1, 1), self.zero),
        )

    def put(self, buf, here, value, row):
        for n, act in enumerate(self.active(value, row)):
            buf[n, here, :] = act


OFF = 8


def here_of(row, ch, count=1):
    return pl.ds((row + OFF) * ch, count * ch)


def conv_layer(ch, weight, source, held, start, stop, emit):
    width = held.shape[1]
    for first in range(start, stop, 4):
        sides = [
            jnp.concatenate([source[n, here_of(first + 2 * h - 1, ch, 4), :] for n in range(3)], axis=0)
            for h in range(2)
        ]
        out = jnp.dot(weight, jnp.concatenate(sides, axis=1), preferred_element_type=F32)
        for h in range(2):
            for q in range(2):
                row = first + 2 * h + q
                total = held[here_of(row, ch), :].astype(F32)
                total += out[q * ch : (q + 1) * ch, h * width : (h + 1) * width]
                emit(row, total.astype(BF))


def join_first_rows(ch, join_mat, inp):
    width = inp.shape[1]
    mixed = jnp.dot(
        join_mat, jnp.concatenate([inp[: 2 * ch], inp[2 * ch :]], axis=1), preferred_element_type=F32
    ).astype(BF)
    return [mixed[q * ch : (q + 1) * ch, h * width : (h + 1) * width] for h in range(2) for q in range(2)]


def clear_outside(space, ch, rows, bufs):
    for buf in bufs:
        for row in (-HALO - 1, rows + HALO):
            for n in range(3):
                buf[n, here_of(row, ch), :] = space.zero


def conv_layers(ch, conv, space, rows, act_a, act_b, held, fout):
    layers = conv.shape[0]
    source, target = act_a, act_b
    for layer in range(layers):
        need = layers - 1 - layer
        reach = -(-need // 2) * 2
        start, stop = -reach, rows + reach
        if (stop - start) % 4:
            start, stop = -HALO, rows + HALO

        def emit(row, value, layer=layer, target=target):
            if layer < layers - 1:
                held[here_of(row, ch), :] = value
                space.put(target, here_of(row, ch), value, row)
            else:
                fout[pl.ds(row * ch, ch), :] = value

        conv_layer(ch, conv[layer], source, held, start, stop, emit)
        source, target = target, source


def first_kernel(ch, steps, *refs):
    xq, along, cross, join, join_both, conv, codes, far_in, *refs = refs
    fout, msg_e, msg_o, far_out, act_a, act_b, held, sent, *choices = refs
    half = HALO * ch
    rows = QUAD * BS
    place = Place()
    space = Rows(ch, xq.shape[1], jnp.logical_not(place.top), jnp.logical_not(place.bottom), rows)
    above, below = above_below(place, along[pl.ds(0, half), :], cross[pl.ds(0, half), :])
    clear_outside(space, ch, rows, (act_a, act_b))
    join_mat = join[...]
    for first in range(-HALO, rows + HALO, 4):
        inp = above if first < 0 else below if first >= rows else xq[pl.ds(first * ch, 4 * ch), :]
        for n, value in enumerate(join_first_rows(ch, join_mat, inp)):
            held[here_of(first + n, ch), :] = value
            space.put(act_a, here_of(first + n, ch), value, first + n)
    send_choices(code_of_next(ch, place, 0, steps, codes, along, cross), choices)
    conv_layers(ch, conv, space, rows, act_a, act_b, held, fout)
    pack_messages(ch, fout, place.odd, join_both[...], choices, None, sent, msg_e, msg_o)


def step_kernel(ch, step, steps, *refs):
    strip = BS * ch
    half = HALO * ch
    last = step == steps - 1
    refs = list(refs)

    def take(count):
        taken = refs[:count]
        del refs[:count]
        return taken

    xq, along, cross, join, conv = take(5)
    feat_e, feat_o = take(2)
    choices = take(2 if last else 6)
    before, out_a, out_b = take(3)
    (local,) = take(1)
    if last:
        (x_inner,) = take(1)
    else:
        next_edges, fout, msg_e, msg_o = take(4)
    own_out, part_out = take(2) if last else (None, None)
    out_f, out_g = take(2)
    tmp, act_a, act_b, held, sems, aligned, recv = take(7)
    if last:
        (fout,) = take(1)
    else:
        (sent,) = take(1)
    width = xq.shape[-1]
    place = Place()
    par = place.odd
    core = place.core
    rows = 2 * BS if last else QUAD * BS
    left_side = place.side == 0

    copies = own_copies(strip, step - 1, steps, before, out_f, out_g, sems.at[0])
    for n, copy in copies:
        pl.when(core == n)(copy.start)

    def choose(which, one, two):
        return jnp.where(which, one.astype(F32), two.astype(F32)).astype(BF)

    fold = fold_rows(ch)
    zero = jnp.zeros((half, width), BF)
    one, two = feat_e[pl.ds(fold, half), :], feat_o[pl.ds(fold, half), :]
    over_sent, under_sent = choose(par == 1, one, two), choose(par == 1, two, one)
    over, under = zero, zero
    if step == 1:
        over, under = above_below(place, along[pl.ds(half, half), :], cross[pl.ds(half, half), :])
    if last:
        inner = x_inner[...]
        over, under = choose(left_side, zero, inner), choose(left_side, inner, zero)
        over_sent, under_sent = choose(left_side, over_sent, zero), choose(left_side, zero, under_sent)
    unpack_message(ch, feat_e, recv, 1 - par)
    unpack_message(ch, feat_o, recv, par)
    for edge in (0, half + QUAD * strip):
        aligned[pl.ds(edge, half), :] = local[pl.ds(edge, half), :]
    for side in range(2):
        got = jnp.dot(recv[side], choices[side][...], preferred_element_type=F32)
        for m in range(2):
            here = pl.ds(half + (2 * side + m) * strip, strip)
            both = got[:, m * width : (m + 1) * width] + local[here, :].astype(F32)
            aligned[here, :] = both.astype(BF)

    space = Rows(ch, width, jnp.logical_not(place.top), jnp.logical_not(place.bottom), rows)
    if last:
        space.top_ok = space.top_ok | (place.side == 1)
        space.bottom_ok = space.bottom_ok | left_side
    clear_outside(space, ch, rows, (act_a, act_b))
    join_mat = join[...]
    for first in range(-HALO, rows + HALO, 4):
        inp, extra = xq, None
        if first < 0:
            inp, extra = over, over_sent
        elif first >= rows:
            inp, extra = under, under_sent
        else:
            inp = xq[pl.ds(first * ch, 4 * ch), :]
        at = (first + HALO) * ch
        if last:
            at = pl.multiple_of(place.side * (2 * strip) + at, half)
        al = aligned[pl.ds(at, half), :]
        for n, value in enumerate(join_rows(ch, join_mat, al, inp, extra)):
            held[here_of(first + n, ch), :] = value
            space.put(act_a, here_of(first + n, ch), value, first + n)

    conv_layers(ch, conv, space, rows, act_a, act_b, held, fout)
    if not last:
        pack_messages(ch, fout, par, join_mat, choices[2:], next_edges, sent, msg_e, msg_o)
    else:
        channels_first(fout, pl.multiple_of(core * strip, strip), own_out, tmp, ch)
        channels_first(fout, pl.multiple_of((core ^ 1) * strip, strip), part_out, tmp, ch)
    for n, copy in copies:
        pl.when(core == n)(copy.wait)


def parts_kernel(*refs):
    out = refs[-1]
    strip = refs[0].shape[0]
    for n in range(out.shape[0] // strip):
        out[pl.ds(n * strip, strip), :] = refs[n][...]


def own_copies(strip, step, steps, own, out_f, out_g, sem):
    return [
        (0, pltpu.make_async_copy(own, out_f.at[pl.ds(step * strip, strip)], sem)),
        (1, pltpu.make_async_copy(own, out_g.at[pl.ds((steps - 1 - step) * strip, strip)], sem)),
    ]


def back_copies(strip, step, steps, back, out_f, out_g, sem):
    return [
        (0, pltpu.make_async_copy(back, out_g.at[pl.ds((steps - 1 - step) * strip, strip)], sem)),
        (1, pltpu.make_async_copy(back, out_f.at[pl.ds(step * strip, strip)], sem)),
    ]


def run_copies(copies):
    core = Place().core
    for n, copy in copies:
        pl.when(core == n)(copy.start)
    for n, copy in copies:
        pl.when(core == n)(copy.wait)


def finish_own_kernel(strip, steps, own, backs, out_a, out_b, out_f, out_g, sems):
    copies = own_copies(strip, steps - 1, steps, own, out_f, out_g, sems.at[0])
    for step in range(steps - 1):
        before = backs.at[pl.ds(step * strip, strip)]
        copies += back_copies(strip, step, steps, before, out_f, out_g, sems.at[1 + step])
    run_copies(copies)


def finish_kernel(strip, steps, back, out_a, out_b, out_f, out_g, sem):
    run_copies(back_copies(strip, steps - 1, steps, back, out_f, out_g, sem))


def weights_kernel(conv, join, wide, join_both, join_first):
    core = Place().core
    layers, ch = conv.shape[1], conv.shape[3]
    zero = jnp.zeros((ch, ch), BF)
    for layer in range(layers):
        for dx in range(3):
            taps = [conv[core, layer, 3 * dy + dx] for dy in range(3)]
            for q in range(2):
                line = [zero] * q + taps + [zero] * (1 - q)
                wide[layer, pl.ds(q * ch, ch), pl.ds(dx * 4 * ch, 4 * ch)] = jnp.concatenate(line, axis=1)
    both = join[core]
    none = jnp.zeros_like(both)
    join_both[pl.ds(0, ch), :] = jnp.concatenate([both, none], axis=1)
    join_both[pl.ds(ch, ch), :] = jnp.concatenate([none, both], axis=1)
    enter = both[:, ch:]
    join_first[pl.ds(0, ch), :] = jnp.concatenate([enter, zero], axis=1)
    join_first[pl.ds(ch, ch), :] = jnp.concatenate([zero, enter], axis=1)


VMEM = pl.BlockSpec(memory_space=pltpu.VMEM)
ANY = pl.BlockSpec(memory_space=pl.ANY)
HBM = pl.BlockSpec(memory_space=pltpu.HBM)


def call(kernel, name, args, outs, scratch=(), flops=0, in_any=(), out_any=(), aliases=None, in_hbm=(), free=False):
    args = [pltpu.with_memory_space_constraint(a, pltpu.HBM) if n in in_hbm else a for n, a in enumerate(args)]
    return pl.pallas_call(
        kernel,
        out_shape=[jax.ShapeDtypeStruct(o, BF) for o in outs],
        in_specs=[HBM if n in in_hbm else ANY if n in in_any else VMEM for n in range(len(args))],
        out_specs=[ANY if n in out_any else VMEM for n in range(len(outs))],
        scratch_shapes=list(scratch),
        input_output_aliases=aliases or {},
        compiler_params=pltpu.CompilerParams(vmem_limit_bytes=32 << 20),
        cost_estimate=pl.CostEstimate(
            flops=flops,
            bytes_accessed=0 if free else sum(a.size * a.dtype.itemsize for a in args),
            transcendentals=0,
        ),
        name=name,
    )(*args)


def sooner(value, *after):
    return pl.pallas_call(
        lambda *refs: None,
        out_shape=jax.ShapeDtypeStruct(value.shape, value.dtype),
        in_specs=[ANY] * (1 + len(after)),
        out_specs=ANY,
        input_output_aliases={0: 0},
        compiler_params=pltpu.CompilerParams(vmem_limit_bytes=1 << 20),
        cost_estimate=pl.CostEstimate(flops=0, bytes_accessed=2 << 20, transcendentals=0),
        name="sooner",
    )(value, *after)


def pairings(count, idle):
    groups = count // QUAD
    out = []
    for parity in range(2):
        pairs = []
        for i in range(count):
            g = i // QUAD
            other = g + 1 if g % 2 == parity else g - 1
            pairs.append((i, i % QUAD + other * QUAD if 0 <= other < groups else i ^ idle))
        out.append(pairs)
    return out


def edge_pairings(count):
    groups = count // QUAD
    along, cross = [], []
    for i in range(count):
        g, side, core = i // QUAD, i % QUAD // 2, i % 2
        if side == 0:
            along += [(i, i - QUAD)] if g > 0 else []
            cross.append((i, i - QUAD + 2 if g > 0 else i ^ 1))
        else:
            along += [(i, i + QUAD)] if g < groups - 1 else []
            cross.append((i, i + QUAD - 2 if g < groups - 1 else i ^ 1))
    return along, cross


def on_device(frames, motion_forward, motion_backward, join_weight, conv_weight):
    steps, ch, strip_rows, width = frames.shape
    strip = strip_rows * ch
    half = HALO * ch
    crow = 16
    count = lax.axis_size("tiles")
    even, odd = pairings(count, 1)
    along_pairs, cross_pairs = edge_pairings(count)

    def near(k):
        return [(i, i ^ k) for i in range(count)]

    def send(value, pairs):
        return lax.ppermute(value, "tiles", pairs)

    tmp = pltpu.VMEM((strip, width), F32)
    piece = (strip, width)
    rows = QUAD * BS
    message = (fold_rows(ch) + half, width)
    feature = (rows * ch, width)
    whole = (steps * strip, width)
    flat = frames.reshape(steps, strip, width)
    later = ((steps - 1) * strip, width)
    first = (strip + crow, width)
    mine, mine_edge, other = call(
        functools.partial(pack_first_kernel, ch, crow),
        "pack_first",
        (flat, motion_forward, motion_backward),
        [first, (half, width), (strip + crow + half, width)],
        [
            pltpu.VMEM((2, *piece), BF),
            pltpu.VMEM((2, *motion_forward.shape), jnp.int32),
            tmp,
            pltpu.SemaphoreType.DMA((6,)),
        ],
        in_hbm=(0, 1, 2),
    )
    (rest,) = call(
        pack_rest_kernel,
        "pack_rest",
        (flat, mine),
        [later],
        [pltpu.SemaphoreType.DMA((steps,))],
        in_hbm=(0,),
        in_any=(1,),
        out_any=(0,),
    )
    pair, edge, rest = call(
        functools.partial(pair_first_kernel, ch, crow),
        "pair_first",
        (mine, mine_edge, send(other, near(1)), rest),
        [(2 * (strip + crow), width), (2 * (half + crow), width), later],
        [tmp],
        in_any=(3,),
        out_any=(2,),
        aliases={3: 2},
    )
    received = send(pair, near(2))
    swapped = send(rest, near(1))
    along, cross = sooner(send(edge, along_pairs)), send(edge, cross_pairs)
    far_pairs = 2 * (steps - 3) * strip
    pair_near, pair_far, pair_last = call(
        functools.partial(pair_kernel, ch),
        "pair_rest",
        (flat, swapped),
        [(2 * strip + half, width), (far_pairs + (steps - 2) * half, width), (2 * strip, width)],
        [tmp, pltpu.SemaphoreType.DMA((2 * steps,))],
        in_hbm=(0,),
        in_any=(1,),
    )
    layers = conv_weight.shape[1]
    conv, join_both, join_first = call(
        weights_kernel,
        "weights",
        (conv_weight, join_weight),
        [(layers, 2 * ch, 12 * ch), (2 * ch, 4 * ch), (2 * ch, 2 * ch)],
        free=True,
    )
    xq, codes, pair_near = call(
        functools.partial(gather_first_kernel, ch, crow),
        "gather_first",
        (pair, received, conv, pair_near),
        [feature, (QUAD * crow, width), pair_near.shape],
        [tmp],
        in_any=(2, 3),
        out_any=(2,),
        aliases={3: 2},
        free=True,
    )
    received_near = send(pair_near, near(2))

    wide_act = pltpu.VMEM((3, (rows + 16) * ch, width), BF)
    flops = 2 * (rows + 2 * HALO) * width * ch * ch * 9 * layers
    part_shapes, sent_shapes = choice_shapes(width)
    acts = [wide_act, wide_act, pltpu.VMEM(((rows + 16) * ch, width), BF)]
    feat, msg_e, msg_o, pair_far = call(
        functools.partial(first_kernel, ch, steps),
        "refine_first",
        (xq, along, cross, join_first, join_both, conv, codes, pair_far),
        [feature, message, message, pair_far.shape],
        [*acts, pltpu.VMEM((2, *message), BF)] + [pltpu.VMEM(shape, BF) for shape in sent_shapes],
        flops,
        in_any=(7,),
        out_any=(3,),
        aliases={7: 3},
    )
    feat_e, feat_o = send(msg_e, even), send(msg_o, odd)
    parts = []
    received_far = send(pair_far, near(2))
    outputs = call(lambda after, a, b: None, "results", (feat,), [whole, whole], in_any=(0,), out_any=(0, 1), free=True)

    def choices_of(step):
        return call(
            functools.partial(choices_kernel, ch, step, steps),
            "choices",
            (codes, along, cross, feat),
            [((rows + 2 * HALO) * ch, width), piece, piece] + part_shapes + (sent_shapes if step + 1 < steps else []),
            [tmp],
        )

    def frame_of(step):
        if step == steps - 1:
            kernel = functools.partial(gather_last_kernel, ch, far_pairs + (steps - 3) * half)
            args, outs = (pair_last, received_far, feat), [(2 * strip, width), (half, width)]
        elif step == 1:
            kernel = functools.partial(gather_kernel, ch, 0, 2 * strip)
            args, outs = (pair_near, received_near, feat), [feature, (2, half, width)]
        else:
            kernel = functools.partial(gather_kernel, ch, 2 * (step - 2) * strip, far_pairs + (step - 2) * half)
            args, outs = (pair_far, received_far, feat), [feature, (2, half, width)]
        return call(kernel, "gather", args, outs, [tmp], in_any=(2,))

    for step in range(1, steps):
        last = step == steps - 1
        local, own, part, *choices = choices_of(step)
        x_now, beside = frame_of(step)
        feat_e = sooner(feat_e, x_now) if step > 1 else sooner(feat_e)
        parts = parts + [part]
        args = [x_now, along, cross, join_both, conv, feat_e, feat_o, *choices, own, *outputs]
        many = len(args)
        outs = [] if last else [feature, message, message]
        outs += [piece, piece, whole, whole] if last else [whole, whole]
        in_any = [many - 3, many - 2, many - 1]
        out_any = [len(outs) - 2, len(outs) - 1]
        aliases = {many - 2: len(outs) - 2, many - 1: len(outs) - 1}
        args += [local, beside]
        scratch = [tmp, *acts, pltpu.SemaphoreType.DMA((1,))]
        scratch += [pltpu.VMEM(((rows + 2 * HALO) * ch, width), BF), pltpu.VMEM((2, strip, width), BF)]
        scratch += [pltpu.VMEM((2 * strip, width) if last else (2, *message), BF)]
        if last:
            (before,) = call(
                parts_kernel,
                "parts",
                (*parts, feat_e, feat_o),
                [(len(parts) * strip, width)],
                in_any=(len(parts), len(parts) + 1),
            )
            backs = send(before, near(1))
        results = call(
            functools.partial(step_kernel, ch, step, steps),
            "refine",
            args,
            outs,
            scratch,
            flops,
            in_any=in_any,
            out_any=out_any,
            aliases=aliases,
        )
        if not last:
            feat, msg_e, msg_o, *results = results
            feat_e, feat_o = send(msg_e, even), send(msg_o, odd)
        if last:
            own, part, *results = results
        outputs = results
    back = send(part, near(1))

    outputs = call(
        functools.partial(finish_own_kernel, strip, steps),
        "finish_own",
        [own, backs, *outputs],
        [whole] * 2,
        [pltpu.SemaphoreType.DMA((steps,))],
        in_any=(0, 1, 2, 3),
        out_any=(0, 1),
        aliases={2: 0, 3: 1},
    )
    outputs = call(
        functools.partial(finish_kernel, strip, steps),
        "finish",
        [back, *outputs],
        [whole] * 2,
        [pltpu.SemaphoreType.DMA],
        in_any=(0, 1, 2),
        out_any=(0, 1),
        aliases={1: 0, 2: 1},
    )
    return tuple(o.reshape(frames.shape) for o in outputs)


def solution(mesh):
    return jax.shard_map(
        on_device,
        mesh=mesh,
        in_specs=(
            P(None, None, ("clips", "tiles"), None),
            P(None, ("clips", "tiles")),
            P(None, ("clips", "tiles")),
            P(),
            P(),
        ),
        out_specs=(
            P(None, None, ("clips", "tiles"), None),
            P(None, None, ("clips", "tiles"), None),
        ),
        check_vma=False,
    )
```
